32 devices in a mesh: down: 16 (over z, y, core), cross: 2 (over x).
Axes of the slice: x: 2, y: 2, z: 4, core: 2. Of those that a mesh axis runs over, the one named last changes fastest.
Arguments:
- particles: float32 [4096, 12, 128], P(('down', 'cross')), may hold values from -4 to 14.5, as said below
- anchor_down: int32 [2, 4096], P(None, ('down', 'cross')), may hold values from -4 to 12
- anchor_cross: int32 [2, 4096], P(None, ('down', 'cross')), may hold values from -4 to 244
- move_count: int32 [2, 4, 16, 2], P(None, None, 'down', 'cross'), may hold values from 0 to 13, as said below
- move_slots: int32 [2, 4, 13, 16, 2], P(None, None, None, 'down', 'cross'), may hold values from 0 to 127, as said below
Outputs:
- moved_particles: float32 [4096, 12, 128], P(('down', 'cross'))
The draws below stay inside these ranges and needn't reach their ends.
Inputs may be any that keep to these rules, and one draw needn't show every extreme that they name: `move_count`: entry 0 of tile (i, j) equals entry 1 of tile (i + 1, j), and entry 2 of (i, j) equals entry 3 of (i, j + 1); entries toward the outside of the grid are 0; in every step some link carries 13. `move_slots`: for each step and tile the 52 slot numbers are different. `particles`: field 0 lies in [0.5, 8 - 1.5] and field 1 in [0.5, 16 - 1.5]; fields 7 to 10 are positive.
All inputs are finite; a program needn't handle non-finite values.
Results may differ from the reference program's by a relative error of at most 0.0003.
Values sent between devices are 32-bit elements; how exact they have to be, the bound alone decides.
No kernel may reach another device: no remote copies, remote signals or barrier semaphores. Data moves between devices by JAX's collectives and lax.ppermute only.
A program may use at most 64 MiB of HBM per device.

```python
import math
import jax
import jax.numpy as jnp
from jax import lax

BLOCK_SIZE = 128
WIN_DOWN = 8
WIN_CROSS = 16
GHOST = 4
STEPS = 2
MOVE_CAP = 13
TILE_DOWN = 16
TILE_CROSS = 256
BLOCKS_DEV = 128
BLOCKS_ALL = 4096
NODES_DOWN = 256
NODES_CROSS = 512
N_DOWN = 16
N_CROSS = 2


def draw_particles(key, part):
    key_list = jax.random.split(key, 11)
    grid_shape = (BLOCKS_ALL, BLOCK_SIZE)
    offset_down = jax.random.uniform(key_list[0], grid_shape, jnp.float32, 0.5, WIN_DOWN - 1.5)
    offset_cross = jax.random.uniform(key_list[1], grid_shape, jnp.float32, 0.5, WIN_CROSS - 1.5)
    speed_down = jnp.clip(jax.random.normal(key_list[2], grid_shape, jnp.float32), -4.0, 4.0)
    speed_cross = jnp.clip(jax.random.normal(key_list[3], grid_shape, jnp.float32), -4.0, 4.0)
    stress_all = jnp.clip(jax.random.normal(key_list[5], (BLOCKS_ALL, 3, BLOCK_SIZE), jnp.float32), -4.0, 4.0)
    mass_value = jnp.exp(jax.random.uniform(key_list[6], grid_shape, jnp.float32, math.log(0.5), math.log(2.0)))
    volume_value = jnp.exp(jax.random.uniform(key_list[7], grid_shape, jnp.float32, math.log(0.5), math.log(2.0)))
    shear_value = jnp.exp(jax.random.uniform(key_list[8], grid_shape, jnp.float32, 0.0, math.log(10.0)))
    lame_value = jnp.exp(jax.random.uniform(key_list[9], grid_shape, jnp.float32, 0.0, math.log(10.0)))
    strain_value = jax.random.uniform(key_list[10], grid_shape, jnp.float32, 0.0, 1.0)
    return jnp.stack([offset_down, offset_cross, speed_down, speed_cross, stress_all[:, 0], stress_all[:, 1], stress_all[:, 2], mass_value, volume_value, shear_value, lame_value, strain_value], axis=1)


def draw_move_count(key, part):
    key_list = jax.random.split(key, 4)
    links_down = jax.random.randint(key_list[0], (STEPS, N_DOWN - 1, N_CROSS), 0, MOVE_CAP + 1)
    links_cross = jax.random.randint(key_list[1], (STEPS, N_DOWN, N_CROSS - 1), 0, MOVE_CAP + 1)
    chosen_row = jax.random.randint(key_list[2], (STEPS, 1, 1), 0, N_DOWN - 1)
    chosen_col = jax.random.randint(key_list[3], (STEPS, 1, 1), 0, N_CROSS)
    row_index = jnp.arange(N_DOWN - 1)[None, :, None]
    col_index = jnp.arange(N_CROSS)[None, None, :]
    links_down = jnp.where((row_index == chosen_row) & (col_index == chosen_col), MOVE_CAP, links_down)
    forward_down = jnp.pad(links_down, ((0, 0), (0, 1), (0, 0)))
    backward_down = jnp.pad(links_down, ((0, 0), (1, 0), (0, 0)))
    forward_cross = jnp.pad(links_cross, ((0, 0), (0, 0), (0, 1)))
    backward_cross = jnp.pad(links_cross, ((0, 0), (0, 0), (1, 0)))
    return jnp.stack([forward_down, backward_down, forward_cross, backward_cross], axis=1).astype(jnp.int32)


def pick_slots(single_key):
    return jax.random.permutation(single_key, BLOCKS_DEV)[:4 * MOVE_CAP]


def draw_move_slots(key, part):
    key_list = jax.random.split(key, STEPS * N_DOWN * N_CROSS)
    picked = jax.vmap(pick_slots)(key_list)
    picked = picked.reshape(STEPS, N_DOWN, N_CROSS, 4, MOVE_CAP)
    return jnp.transpose(picked, (0, 3, 4, 1, 2)).astype(jnp.int32)


def with_ends(drawn, rng, smallest, high):
    spot = [jax.random.randint(jax.random.fold_in(rng, axis), (), 0, length) for axis, length in enumerate(drawn.shape)]
    longest = drawn.shape.index(max(drawn.shape))
    neighbour = spot[:longest] + [(spot[longest] + 1) % drawn.shape[longest]] + spot[longest + 1:]
    return drawn.at[tuple(spot)].set(smallest).at[tuple(neighbour)].set(high)


def setup_inputs(seed: int = 0) -> dict:
    streams_of = jax.random.split(jax.random.key(seed), 6)
    return {
        "particles": draw_particles(jax.random.fold_in(streams_of[5], 71), 0),
        "anchor_down": with_ends(jax.random.randint(streams_of[1], (STEPS, BLOCKS_ALL), -GHOST, TILE_DOWN + GHOST - WIN_DOWN + 1), jax.random.fold_in(streams_of[1], 1), -GHOST, TILE_DOWN + GHOST - WIN_DOWN).astype(jnp.int32),
        "anchor_cross": with_ends(jax.random.randint(streams_of[2], (STEPS, BLOCKS_ALL), -GHOST, TILE_CROSS + GHOST - WIN_CROSS + 1), jax.random.fold_in(streams_of[2], 1), -GHOST, TILE_CROSS + GHOST - WIN_CROSS).astype(jnp.int32),
        "move_count": draw_move_count(jax.random.fold_in(streams_of[5], 71), 0),
        "move_slots": draw_move_slots(jax.random.fold_in(streams_of[5], 71), 0),
    }


TIME_STEP = 0.1
GRAVITY = 5.6
MASS_FLOOR = 0.5
HIGHEST = lax.Precision.HIGHEST
group_limit = 256


def spline_pair(distance):
    magnitude = jnp.abs(distance)
    inside = 0.75 - distance * distance
    remote = 0.5 * (1.5 - magnitude) * (1.5 - magnitude)
    spline_value = jnp.where(magnitude < 0.5, inside, jnp.where(magnitude < 1.5, remote, 0.0))
    slope_far = jnp.where(distance > 0.0, distance - 1.5, distance + 1.5)
    spline_slope = jnp.where(magnitude < 0.5, -2.0 * distance, jnp.where(magnitude < 1.5, slope_far, 0.0))
    return spline_value, spline_slope


def block_weights(block_group):
    node_index = jnp.arange(WIN_DOWN * WIN_CROSS)
    node_row = (node_index // WIN_CROSS).astype(block_group.dtype)
    node_col = (node_index % WIN_CROSS).astype(block_group.dtype)
    down_value, down_slope = spline_pair(block_group[:, 0, :, None] - node_row)
    cross_value, cross_slope = spline_pair(block_group[:, 1, :, None] - node_col)
    return down_value * cross_value, down_slope * cross_value, down_value * cross_slope


def scatter_terms(block_group):
    weight, grad_down, grad_cross = block_weights(block_group)
    mass_value = block_group[:, 7]
    volume_value = block_group[:, 8]
    carried = jnp.stack([mass_value, mass_value * block_group[:, 2], mass_value * block_group[:, 3]], axis=1)
    stress_down = jnp.stack([-volume_value * block_group[:, 4], -volume_value * block_group[:, 5]], axis=1)
    stress_cross = jnp.stack([-volume_value * block_group[:, 5], -volume_value * block_group[:, 6]], axis=1)
    lumped = jnp.einsum("bcp,bpn->bcn", carried, weight, precision=HIGHEST)
    force_sum = jnp.einsum("bcp,bpn->bcn", stress_down, grad_down, precision=HIGHEST)
    force_sum = force_sum + jnp.einsum("bcp,bpn->bcn", stress_cross, grad_cross, precision=HIGHEST)
    return jnp.concatenate([lumped, force_sum], axis=1)


def advance(block_group, particle_vel, along_down, along_cross):
    rate_dd = along_down[:, 0]
    rate_cc = along_cross[:, 1]
    rate_dc = 0.5 * (along_cross[:, 0] + along_down[:, 1])
    trace_rate = rate_dd + rate_cc
    shear_value = block_group[:, 9]
    lame_value = block_group[:, 10]
    stress_dd = block_group[:, 4] + TIME_STEP * (lame_value * trace_rate + 2.0 * shear_value * rate_dd)
    stress_dc = block_group[:, 5] + TIME_STEP * (2.0 * shear_value * rate_dc)
    stress_cc = block_group[:, 6] + TIME_STEP * (lame_value * trace_rate + 2.0 * shear_value * rate_cc)
    offset_down = jnp.clip(block_group[:, 0] + TIME_STEP * particle_vel[:, 0], 0.5, WIN_DOWN - 1.5)
    offset_cross = jnp.clip(block_group[:, 1] + TIME_STEP * particle_vel[:, 1], 0.5, WIN_CROSS - 1.5)
    volume_value = block_group[:, 8] * (1.0 + TIME_STEP * trace_rate)
    strain_value = block_group[:, 11] + TIME_STEP * (rate_dd * rate_dd + rate_cc * rate_cc + 2.0 * rate_dc * rate_dc)
    return jnp.stack([offset_down, offset_cross, particle_vel[:, 0], particle_vel[:, 1], stress_dd, stress_dc, stress_cc, block_group[:, 7], volume_value, shear_value, lame_value, strain_value], axis=1)


def gather_terms(block_group, window_vel):
    weight, grad_down, grad_cross = block_weights(block_group)
    particle_vel = jnp.einsum("bcn,bpn->bcp", window_vel, weight, precision=HIGHEST)
    along_down = jnp.einsum("bcn,bpn->bcp", window_vel, grad_down, precision=HIGHEST)
    along_cross = jnp.einsum("bcn,bpn->bcp", window_vel, grad_cross, precision=HIGHEST)
    return advance(block_group, particle_vel, along_down, along_cross)


def by_groups(block_task, particle_state, *extra_args):
    block_count = particle_state.shape[0]
    group_size = math.gcd(block_count, group_limit)
    packed = tuple(member.reshape((block_count // group_size, group_size) + member.shape[1:]) for member in (particle_state,) + extra_args)

    def run_group(pieces):
        return block_task(*pieces)

    result = lax.map(run_group, packed)
    return result.reshape((block_count,) + result.shape[2:])


def node_velocity(node_sums, keep_mask):
    mass_sum = node_sums[0]
    moved_sum = jnp.stack([node_sums[1] + TIME_STEP * (node_sums[3] + GRAVITY * mass_sum), node_sums[2] + TIME_STEP * node_sums[4]])
    return jnp.where(keep_mask, moved_sum / jnp.maximum(mass_sum, MASS_FLOOR), 0.0)


def migrate(particle_state, slot_list, count_list):
    tile_down = jnp.arange(N_DOWN, dtype=jnp.int32)[:, None]
    tile_cross = jnp.arange(N_CROSS, dtype=jnp.int32)[None, :]
    shift_down = [1, -1, 0, 0]
    shift_cross = [0, 0, 1, -1]
    opposite = [1, 0, 3, 2]
    order_index = jnp.arange(BLOCKS_ALL, dtype=jnp.int32)
    for direction in range(4):
        near_down = jnp.clip(tile_down + shift_down[direction], 0, N_DOWN - 1)
        near_cross = jnp.clip(tile_cross + shift_cross[direction], 0, N_CROSS - 1)
        target_index = (tile_down * N_CROSS + tile_cross) * BLOCKS_DEV + slot_list[direction]
        source_index = (near_down * N_CROSS + near_cross) * BLOCKS_DEV + slot_list[opposite[direction]][:, near_down, near_cross]
        valid_mask = jnp.arange(MOVE_CAP, dtype=jnp.int32)[:, None, None] < count_list[direction][None]
        chosen = jnp.where(valid_mask, source_index, target_index).reshape(-1).astype(jnp.int32)
        order_index = order_index.at[target_index.reshape(-1).astype(jnp.int32)].set(chosen)
    return particle_state[order_index]


def reference(particles, anchor_down, anchor_cross, move_count, move_slots):
    particle_state = particles
    grid_width = NODES_CROSS + 2 * GHOST
    grid_height = NODES_DOWN + 2 * GHOST
    node_index = jnp.arange(WIN_DOWN * WIN_CROSS, dtype=jnp.int32)
    node_row = node_index // WIN_CROSS
    node_col = node_index % WIN_CROSS
    tile_index = jnp.arange(BLOCKS_ALL, dtype=jnp.int32) // BLOCKS_DEV
    tile_down = tile_index // N_CROSS
    tile_cross = tile_index % N_CROSS
    row_global = jnp.arange(NODES_DOWN, dtype=jnp.int32)
    col_global = jnp.arange(NODES_CROSS, dtype=jnp.int32)
    keep_rows = (row_global > 0) & (row_global < NODES_DOWN - 1)
    keep_cols = (col_global > 0) & (col_global < NODES_CROSS - 1)
    keep_mask = keep_rows[:, None] & keep_cols[None, :]
    for step_index in range(STEPS):
        first_row = tile_down * TILE_DOWN + anchor_down[step_index] + GHOST
        first_col = tile_cross * TILE_CROSS + anchor_cross[step_index] + GHOST
        flat_index = ((first_row[:, None] + node_row[None, :]) * grid_width + first_col[:, None] + node_col[None, :]).astype(jnp.int32)
        node_terms = by_groups(scatter_terms, particle_state)
        spread = jnp.transpose(node_terms, (1, 0, 2)).reshape(5, -1)
        node_sums = jnp.zeros((5, grid_height * grid_width), jnp.float32).at[:, flat_index.reshape(-1)].add(spread)
        node_sums = node_sums.reshape(5, grid_height, grid_width)[:, GHOST:GHOST + NODES_DOWN, GHOST:GHOST + NODES_CROSS]
        velocity_grid = node_velocity(node_sums, keep_mask)
        padded = jnp.pad(velocity_grid, ((0, 0), (GHOST, GHOST), (GHOST, GHOST))).reshape(2, -1)
        window_vel = jnp.transpose(padded[:, flat_index], (1, 0, 2))
        particle_state = by_groups(gather_terms, particle_state, window_vel)
        particle_state = migrate(particle_state, move_slots[step_index], move_count[step_index])
    return particle_state
```

```python
import functools

import jax
import jax.numpy as jnp
from jax import lax
from jax.experimental import pallas as pl
from jax.experimental.pallas import tpu as pltpu
from jax.sharding import PartitionSpec as P

WIN_DOWN = 8
WIN_CROSS = 16
GHOST = 4
STEPS = 2
TILE_DOWN = 16
TILE_CROSS = 256
TIME_STEP = 0.1
GRAVITY = 5.6
MASS_FLOOR = 0.5
LANES = 128
CHANNELS = 3
STRIDE = 32
BAND = 2 * GHOST
UNROLL = 4


def spline_pair(distance):
    near = jnp.clip(distance, -0.5, 0.5)
    far = jnp.clip(distance - near, -1.0, 1.0)
    twice = near + near
    slope = far - twice
    return slope * slope + (1.5 - 1.5 * twice * twice), slope


def low_part(x):
    return x - x.astype(jnp.bfloat16).astype(jnp.float32)


def node_rows(count):
    return lax.broadcasted_iota(jnp.int32, (count, LANES), 0).astype(jnp.float32)


def cross_weights(w, cols):
    value, slope = spline_pair(w - cols)
    both = jnp.concatenate([value, slope], axis=1)
    high = both.astype(jnp.bfloat16)
    low = (both - high.astype(jnp.float32)).astype(jnp.bfloat16)
    return jnp.concatenate([high, low], axis=0)


def scatter_block(state, sums, b, first_row, first_col, rows, cols, keep):
    u, w, vd, vc = (state[b, f : f + 1, :] for f in range(4))
    sdd, sdc, scc, mass, vol = (state[b, f : f + 1, :] for f in range(4, 9))
    value, slope = spline_pair(u - rows)
    quarter = 0.25 * mass
    push = (-0.5 * TIME_STEP) * vol
    push_dc = push * sdc
    zero = jnp.zeros_like(value)
    parts = (
        (quarter * value, zero),
        (quarter * (vd + TIME_STEP * GRAVITY) * value + (push * sdd) * slope, push_dc * value),
        (quarter * vc * value + push_dc * slope, (push * scc) * value),
    )
    gap = jnp.zeros((16, 2 * LANES), jnp.bfloat16)
    pieces = []
    for along, across in parts:
        both = jnp.concatenate([along, across], axis=1)
        pieces += [jnp.concatenate([both, low_part(both)], axis=0).astype(jnp.bfloat16), gap]
    loads = jnp.concatenate(pieces, axis=0)
    found = lax.dot_general(
        cross_weights(w, cols), loads, (((1,), (1,)), ((), ())), preferred_element_type=jnp.float32
    )
    found = found[:WIN_CROSS] + found[WIN_CROSS:]
    found = jnp.concatenate(
        [found, jnp.zeros((WIN_CROSS, LANES - CHANNELS * STRIDE), jnp.float32)], axis=1
    )
    found = jnp.where(keep, found + pltpu.roll(found, LANES - WIN_DOWN, 1), 0.0)
    found = pltpu.roll(found, first_row, 1)
    spot = pl.ds(first_col, WIN_CROSS)
    sums[spot, :] = sums[spot, :] + found


def scatter_all(state, sums, anchor_down, anchor_cross, step, blocks):
    sums[...] = jnp.zeros_like(sums)
    rows = node_rows(WIN_DOWN)
    cols = node_rows(WIN_CROSS)
    lane = lax.broadcasted_iota(jnp.int32, (WIN_CROSS, LANES), 1)
    keep = (lane & (STRIDE - 1)) < WIN_DOWN

    def several(q, carry):
        for k in range(UNROLL):
            b = q * UNROLL + k
            scatter_block(
                state,
                sums,
                b,
                anchor_down[step, b] + GHOST,
                anchor_cross[step, b] + GHOST,
                rows,
                cols,
                keep,
            )
        return carry

    lax.fori_loop(0, blocks // UNROLL, several, 0)


def write_grid(sums, grid, pay, height, tiles):
    for t in range(tiles):
        turned = jnp.transpose(sums[t * LANES : (t + 1) * LANES, :])
        for c in range(CHANNELS):
            grid[t, c * height : (c + 1) * height, :] = turned[c * STRIDE : c * STRIDE + height]
    odd = lax.rem(lax.axis_index("down"), 2)
    for t in range(tiles):
        for c in range(CHANNELS):
            last = grid[t, (c + 1) * height - BAND : (c + 1) * height, :]
            first = grid[t, c * height : c * height + BAND, :]
            pay[odd, t, c * BAND : (c + 1) * BAND, :] = last
            pay[1 - odd, t, c * BAND : (c + 1) * BAND, :] = first


def first_kernel(step, anchor_down, anchor_cross, state, grid, pay, sums):
    blocks = state.shape[0]
    tiles = grid.shape[0]
    scatter_all(state, sums, anchor_down, anchor_cross, step, blocks)
    write_grid(sums, grid, pay, grid.shape[1] // CHANNELS, tiles)


def settle(state, arrived, slots, counts, step, cross_links):
    cap = slots.shape[2]
    for link in range(2 + cross_links):
        side = link_side(link)
        count = counts[step, side]

        def put(m, carry, link=link, side=side):
            state[slots[step, side, m]] = arrived[link][m]
            return carry

        lax.fori_loop(0, count, put, 0)


def link_side(link):
    axis, second = divmod(link, 2)
    odd = lax.rem(lax.axis_index(("down", "cross")[axis]), 2)
    return 2 * axis + (1 - odd if second else odd)


def next_kernel(step, cross_links, anchor_down, anchor_cross, slots, counts, old, *rest):
    arrived = rest[: 2 + cross_links]
    state, grid, pay, sums = rest[2 + cross_links :]
    state[...] = old[...]
    settle(state, arrived, slots, counts, step - 1, cross_links)
    blocks = state.shape[0]
    scatter_all(state, sums, anchor_down, anchor_cross, step, blocks)
    write_grid(sums, grid, pay, grid.shape[1] // CHANNELS, grid.shape[0])


def last_kernel(step, cross_links, slots, counts, old, *rest):
    arrived = rest[: 2 + cross_links]
    state = rest[2 + cross_links]
    state[...] = old[...]
    settle(state, arrived, slots, counts, step, cross_links)


def add_bands(total, bands, height, tiles):
    odd = lax.rem(lax.axis_index("down"), 2)
    for t in range(tiles):
        for c in range(CHANNELS):
            for link in range(2):
                band = bands[link][t, c * BAND : (c + 1) * BAND, :]
                at_first = odd if link == 0 else 1 - odd
                start = c * height + (1 - at_first) * (height - BAND)
                spot = pl.ds(pl.multiple_of(start, 8), BAND)
                total[t, spot, :] = total[t, spot, :] + band


def cross_kernel(width, grid, band0, band1, total, pay):
    tiles, rows, _ = grid.shape
    height = rows // CHANNELS
    total[...] = grid[...]
    add_bands(total, (band0, band1), height, tiles)
    odd = lax.rem(lax.axis_index("cross"), 2)
    start = width - BAND
    tile, lane = divmod(start, LANES)
    last = pltpu.roll(total[tile], LANES - lane, 1) if lane else total[tile]
    pay[odd] = last
    pay[1 - odd] = total[0]


def node_velocity(total, bands, cross_links, speed, width):
    tiles, rows, _ = total.shape
    height = rows // CHANNELS
    odd = lax.rem(lax.axis_index("cross"), 2)
    col = lax.broadcasted_iota(jnp.int32, (rows, LANES), 1)
    start = width - BAND
    tile, lane = divmod(start, LANES)
    for link in range(cross_links):
        band = jnp.where(col < BAND, bands[link][...], 0.0)
        at_first = odd if link == 0 else 1 - odd
        total[0] = total[0] + jnp.where(at_first == 1, band, 0.0)
        shifted = pltpu.roll(band, lane, 1) if lane else band
        total[tile] = total[tile] + jnp.where(at_first == 0, shifted, 0.0)
    tile_down = height - 2 * GHOST
    tile_cross = width - 2 * GHOST
    row_global = (
        lax.broadcasted_iota(jnp.int32, (height, LANES), 0)
        + lax.axis_index("down") * tile_down
        - GHOST
    )
    col_first = lax.broadcasted_iota(jnp.int32, (height, LANES), 1) - GHOST
    total_rows = tile_down * lax.axis_size("down")
    total_cols = tile_cross * lax.axis_size("cross")
    keep_rows = (row_global > 0) & (row_global < total_rows - 1)
    for t in range(tiles):
        col_global = col_first + (lax.axis_index("cross") * tile_cross + t * LANES)
        kept = keep_rows & (col_global > 0) & (col_global < total_cols - 1)
        mass = jnp.maximum(total[t, :height, :], MASS_FLOOR)
        for c in range(2):
            value = total[t, (c + 1) * height : (c + 2) * height, :] / mass
            speed[t, c] = jnp.where(kept, value, 0.0)


def gather_block(state, speed, b, first_row, first_col, rows, cols, lane):
    tile = first_col // LANES
    shift = first_col - tile * LANES
    spot = pl.ds(first_row, WIN_DOWN)
    here = jnp.concatenate([speed[tile, 0, spot, :], speed[tile, 1, spot, :]], axis=0)
    after = jnp.concatenate([speed[tile + 1, 0, spot, :], speed[tile + 1, 1, spot, :]], axis=0)
    window = jnp.where(lane >= shift, here, after)
    window = jnp.where(
        lane < WIN_CROSS,
        pltpu.roll(window, (LANES - shift) & (LANES - 1), 1),
        pltpu.roll(window, (WIN_CROSS + LANES - shift) & (LANES - 1), 1),
    )
    window = jnp.concatenate([window, low_part(window)], axis=0).astype(jnp.bfloat16)
    field = [state[b, f : f + 1, :] for f in range(12)]
    found = jnp.dot(
        window[:, : 2 * WIN_CROSS],
        cross_weights(field[1], cols),
        preferred_element_type=jnp.float32,
    )
    found = found[: 2 * WIN_DOWN] + found[2 * WIN_DOWN :]
    value, slope = spline_pair(field[0] - rows)

    def summed(weight, terms, scale):
        return scale * jnp.sum(weight * terms, axis=0, keepdims=True)

    along = found[:, :LANES]
    across = found[:, LANES:]
    vel_d = summed(value, along[:WIN_DOWN], 0.25)
    vel_c = summed(value, along[WIN_DOWN:], 0.25)
    l_dd = summed(slope, along[:WIN_DOWN], 0.5)
    l_cd = summed(slope, along[WIN_DOWN:], 0.5)
    l_dc = summed(value, across[:WIN_DOWN], 0.5)
    l_cc = summed(value, across[WIN_DOWN:], 0.5)
    rate_dc = 0.5 * (l_dc + l_cd)
    trace = l_dd + l_cc
    shear, lame = field[9], field[10]
    spread = lame * trace
    return [
        jnp.clip(field[0] + TIME_STEP * vel_d, 0.5, WIN_DOWN - 1.5),
        jnp.clip(field[1] + TIME_STEP * vel_c, 0.5, WIN_CROSS - 1.5),
        vel_d,
        vel_c,
        field[4] + TIME_STEP * (spread + 2.0 * shear * l_dd),
        field[5] + TIME_STEP * (2.0 * shear * rate_dc),
        field[6] + TIME_STEP * (spread + 2.0 * shear * l_cc),
        field[7],
        field[8] * (1.0 + TIME_STEP * trace),
        shear,
        lame,
        field[11] + TIME_STEP * (l_dd * l_dd + l_cc * l_cc + 2.0 * rate_dc * rate_dc),
    ]


def gather_kernel(step, cross_links, width, anchor_down, anchor_cross, slots, *rest):
    state, total = rest[:2]
    bands = rest[2 : 2 + cross_links]
    moved = rest[2 + cross_links]
    sent = rest[3 + cross_links : 5 + 2 * cross_links]
    speed, sums = rest[5 + 2 * cross_links :]
    blocks = state.shape[0]
    sums[...] = total[...]
    node_velocity(sums, bands, cross_links, speed, width)
    rows = node_rows(WIN_DOWN)
    cols = node_rows(WIN_CROSS)
    lane = lax.broadcasted_iota(jnp.int32, (2 * WIN_DOWN, LANES), 1)

    def several(q, carry):
        for k in range(UNROLL):
            b = q * UNROLL + k
            out = gather_block(
                state,
                speed,
                b,
                anchor_down[step, b] + GHOST,
                anchor_cross[step, b] + GHOST,
                rows,
                cols,
                lane,
            )
            for f in range(12):
                moved[b, f : f + 1, :] = out[f]
        return carry

    lax.fori_loop(0, blocks // UNROLL, several, 0)
    cap = slots.shape[2]
    for link in range(2 + cross_links):
        side = link_side(link)

        def take(m, carry, link=link, side=side):
            sent[link][m] = moved[slots[step, side, m]]
            return carry

        lax.fori_loop(0, cap, take, 0)


def swap_pairs(size, first):
    pairs = []
    for i in range(first, size - 1, 2):
        pairs += [(i, i + 1), (i + 1, i)]
    return pairs


def solution(mesh):
    size_down, size_cross = mesh.shape["down"], mesh.shape["cross"]
    cross_links = 1 if size_cross <= 2 else 2
    smem = pl.BlockSpec(memory_space=pltpu.SMEM)
    vmem = pl.BlockSpec(memory_space=pltpu.VMEM)
    params = pltpu.CompilerParams(vmem_limit_bytes=40 * 1024 * 1024)
    f32 = jnp.float32

    def swap(x, link):
        axis, second = divmod(link, 2)
        name, size = (("down", size_down), ("cross", size_cross))[axis]
        return lax.ppermute(x, name, swap_pairs(size, second))

    def on_device(particles, anchor_down, anchor_cross, move_count, move_slots):
        blocks = particles.shape[0]
        cap = move_slots.shape[2]
        slots = move_slots.reshape(STEPS, 4, cap)
        counts = move_count.reshape(STEPS, 4)
        height = TILE_DOWN + 2 * GHOST
        width = TILE_CROSS + 2 * GHOST
        tiles = -(-width // LANES)
        grid_type = jax.ShapeDtypeStruct((tiles, CHANNELS * height, LANES), f32)
        band_type = jax.ShapeDtypeStruct((2, tiles, CHANNELS * BAND, LANES), f32)
        state_type = jax.ShapeDtypeStruct(particles.shape, f32)
        sent_type = jax.ShapeDtypeStruct((cap,) + particles.shape[1:], f32)
        sums_scratch = pltpu.VMEM((tiles * LANES, LANES), f32)
        state = particles
        for step in range(STEPS):
            if step == 0:
                grid, pay = pl.pallas_call(
                    functools.partial(first_kernel, step),
                    out_shape=(grid_type, band_type),
                    in_specs=[smem, smem, vmem],
                    out_specs=(vmem, vmem),
                    scratch_shapes=[sums_scratch],
                    compiler_params=params,
                    name="scatter_first",
                )(anchor_down, anchor_cross, state)
            else:
                state, grid, pay = pl.pallas_call(
                    functools.partial(next_kernel, step, cross_links),
                    out_shape=(state_type, grid_type, band_type),
                    in_specs=[smem] * 4 + [vmem] * (3 + cross_links),
                    out_specs=(vmem, vmem, vmem),
                    scratch_shapes=[sums_scratch],
                    compiler_params=params,
                    name="scatter_next",
                )(anchor_down, anchor_cross, slots, counts, state, *arrived)
            band0 = swap(pay[0], 0)
            band1 = swap(pay[1], 1)
            total, pay = pl.pallas_call(
                functools.partial(cross_kernel, width),
                out_shape=(
                    grid_type,
                    jax.ShapeDtypeStruct((2, CHANNELS * height, LANES), f32),
                ),
                in_specs=[vmem] * 3,
                out_specs=(vmem, vmem),
                compiler_params=params,
                name="add_down",
            )(grid, band0, band1)
            bands = [swap(pay[k], 2 + k) for k in range(cross_links)]
            state, *sent = pl.pallas_call(
                functools.partial(gather_kernel, step, cross_links, width),
                out_shape=(state_type,) + (sent_type,) * (2 + cross_links),
                in_specs=[smem] * 3 + [vmem] * (2 + cross_links),
                out_specs=(vmem,) * (3 + cross_links),
                scratch_shapes=[
                    pltpu.VMEM((tiles, 2, height, LANES), f32),
                    pltpu.VMEM(grid_type.shape, f32),
                ],
                compiler_params=params,
                name="gather",
            )(anchor_down, anchor_cross, slots, state, total, *bands)
            arrived = [swap(sent[k], k) for k in range(2 + cross_links)]
        return pl.pallas_call(
            functools.partial(last_kernel, STEPS - 1, cross_links),
            out_shape=state_type,
            in_specs=[smem] * 2 + [vmem] * (3 + cross_links),
            out_specs=vmem,
            compiler_params=params,
            name="settle_last",
        )(slots, counts, state, *arrived)

    return jax.shard_map(
        on_device,
        mesh=mesh,
        in_specs=(
            P(("down", "cross"), None, None),
            P(None, ("down", "cross")),
            P(None, ("down", "cross")),
            P(None, None, "down", "cross"),
            P(None, None, None, "down", "cross"),
        ),
        out_specs=P(("down", "cross"), None, None),
        check_vma=False,
    )
```

```python
import functools

import jax
import jax.numpy as jnp
from jax import lax
from jax.experimental import pallas as pl
from jax.experimental.pallas import tpu as pltpu
from jax.sharding import PartitionSpec as P

WIN_DOWN = 8
WIN_CROSS = 16
GHOST = 4
STEPS = 2
TILE_DOWN = 16
TILE_CROSS = 256
TIME_STEP = 0.1
GRAVITY = 5.6
MASS_FLOOR = 0.5
FIELDS = 12
LANES = 128
ROWS = 8
CHANNELS = 3
STRIDE = 32
BAND = 2 * GHOST
LOADS = 6
GROUP = 64


def spline_pair(distance):
    near = jnp.clip(distance, -0.5, 0.5)
    far = jnp.clip(distance - near, -1.0, 1.0)
    twice = near + near
    slope = far - twice
    return slope * slope + (1.5 - 1.5 * twice * twice), slope


def low_part(x):
    return x - x.astype(jnp.bfloat16).astype(jnp.float32)


def node_rows(count):
    return lax.broadcasted_iota(jnp.int32, (count, LANES), 0).astype(jnp.float32)


def cross_weights(w, cols):
    value, slope = spline_pair(w - cols)
    both = jnp.concatenate([value, slope], axis=1)
    high = both.astype(jnp.bfloat16)
    low = (both - high.astype(jnp.float32)).astype(jnp.bfloat16)
    return jnp.concatenate([high, low], axis=0)


def particle_loads(state, loads, blocks, keep=None):
    def several(q, carry):
        spot = pl.ds(pl.multiple_of(q * ROWS, ROWS), ROWS)
        vd, vc, sdd, sdc, scc, mass, vol = (state[f, spot, :] for f in range(2, 9))
        quarter = 0.25 * mass
        push = (-0.5 * TIME_STEP) * vol
        terms = (
            quarter,
            quarter * (vd + TIME_STEP * GRAVITY),
            quarter * vc,
            push * sdd,
            push * sdc,
            push * scc,
        )
        for k, term in enumerate(terms):
            loads[k, spot, :] = term if keep is None else term * keep[spot, :]
        return carry

    lax.fori_loop(0, blocks // ROWS, several, 0, unroll=4)


def scatter_block(u, w, load, sums, first_row, first_col, rows, cols, inside):
    value, slope = spline_pair(u - rows)
    zero = jnp.zeros_like(value)
    load_dc = load(4)
    parts = (
        (load(0) * value, zero),
        (load(1) * value + load(3) * slope, load_dc * value),
        (load(2) * value + load_dc * slope, load(5) * value),
    )
    gap = jnp.zeros((16, 2 * LANES), jnp.bfloat16)
    pieces = []
    for along, across in parts:
        both = jnp.concatenate([along, across], axis=1)
        pieces += [jnp.concatenate([both, low_part(both)], axis=0).astype(jnp.bfloat16), gap]
    found = lax.dot_general(
        cross_weights(w, cols),
        jnp.concatenate(pieces, axis=0),
        (((1,), (1,)), ((), ())),
        preferred_element_type=jnp.float32,
    )
    found = found[:WIN_CROSS] + found[WIN_CROSS:]
    found = jnp.concatenate(
        [found, jnp.zeros((WIN_CROSS, LANES - CHANNELS * STRIDE), jnp.float32)], axis=1
    )
    found = jnp.where(inside, found + pltpu.roll(found, LANES - WIN_DOWN, 1), 0.0)
    found = pltpu.roll(found, first_row, 1)
    spot = pl.ds(first_col, WIN_CROSS)
    sums[spot, :] = sums[spot, :] + found


def scatter_rows(state, loads, sums, place, blocks, group):
    rows = node_rows(WIN_DOWN)
    cols = node_rows(WIN_CROSS)
    lane = lax.broadcasted_iota(jnp.int32, (WIN_CROSS, LANES), 1)
    inside = (lane & (STRIDE - 1)) < WIN_DOWN

    def several(q, carry):
        for k in range(group):
            m = q * group + k
            row = pl.ds(m, 1)
            first_row, first_col = place(m)
            scatter_block(
                state[0, row, :],
                state[1, row, :],
                lambda f, row=row: loads[f, row, :],
                sums,
                first_row,
                first_col,
                rows,
                cols,
                inside,
            )
        return carry

    lax.fori_loop(0, blocks // group, several, 0)


def window_place(anchor_down, anchor_cross, step):
    return lambda b: (anchor_down[step, b] + GHOST, anchor_cross[step, b] + GHOST)


def write_grid(sums, grid, pay):
    tiles, rows, _ = grid.shape
    height = rows // CHANNELS
    odd = lax.rem(lax.axis_index("down"), 2)
    for t in range(tiles):
        turned = jnp.transpose(sums[t * LANES : (t + 1) * LANES, :])
        for c in range(CHANNELS):
            part = turned[c * STRIDE : c * STRIDE + height]
            grid[t, c * height : (c + 1) * height, :] = part
            spot = slice(c * BAND, (c + 1) * BAND)
            pay[odd, t, spot, :] = part[height - BAND :]
            pay[1 - odd, t, spot, :] = part[:BAND]


def first_kernel(step, anchor_down, anchor_cross, state, grid, pay, sums, loads):
    blocks = state.shape[1]
    sums[...] = jnp.zeros_like(sums)
    particle_loads(state, loads, blocks)
    scatter_rows(
        state, loads, sums, window_place(anchor_down, anchor_cross, step), blocks, GROUP
    )
    write_grid(sums, grid, pay)


def link_side(link):
    axis, second = divmod(link, 2)
    odd = lax.rem(lax.axis_index(("down", "cross")[axis]), 2)
    return 2 * axis + (1 - odd if second else odd)


def settle(state, arrived, slots, counts, step):
    for link, came in enumerate(arrived):
        side = link_side(link)

        def put(m, carry, came=came, side=side):
            slot = pl.ds(slots[step, side, m], 1)
            state[:, slot, :] = came[:, pl.ds(m, 1), :]
            return carry

        lax.fori_loop(0, counts[step, side], put, 0)


def next_kernel(step, links, anchor_down, anchor_cross, slots, counts, old, *rest):
    arrived = rest[:links]
    state, grid, pay, sums, loads = rest[links:]
    blocks = state.shape[1]
    state[...] = old[...]
    settle(state, arrived, slots, counts, step - 1)
    sums[...] = jnp.zeros_like(sums)
    particle_loads(state, loads, blocks)
    scatter_rows(
        state, loads, sums, window_place(anchor_down, anchor_cross, step), blocks, GROUP
    )
    write_grid(sums, grid, pay)


def last_kernel(step, links, slots, counts, old, *rest):
    arrived = rest[:links]
    state = rest[links]
    state[...] = old[...]
    settle(state, arrived, slots, counts, step)


def cross_kernel(width, grid, band0, band1, total, pay):
    tiles, rows, _ = grid.shape
    height = rows // CHANNELS
    odd = lax.rem(lax.axis_index("down"), 2)
    index = lax.axis_index("down")
    size = lax.axis_size("down")
    total[...] = grid[...]
    partner = index - 1 + 2 * odd
    there = (partner >= 0) & (partner < size)
    for t in range(tiles):
        for c in range(CHANNELS):
            spot = slice(c * BAND, (c + 1) * BAND)
            for link in range(2):
                if link == 0:
                    band = band0[t, spot, :]
                else:
                    band = jnp.where(there, band1[odd, t, spot, :], 0.0)
                at_first = odd if link == 0 else 1 - odd
                start = c * height + (1 - at_first) * (height - BAND)
                place = pl.ds(pl.multiple_of(start, 8), BAND)
                total[t, place, :] = total[t, place, :] + band
    odd = lax.rem(lax.axis_index("cross"), 2)
    tile, lane = divmod(width - BAND, LANES)
    last = pltpu.roll(total[tile], LANES - lane, 1) if lane else total[tile]
    pad = jnp.zeros((LANES - rows, LANES), jnp.float32)
    pay[odd] = jnp.transpose(jnp.concatenate([last, pad], axis=0))[:BAND]
    pay[1 - odd] = jnp.transpose(jnp.concatenate([total[0], pad], axis=0))[:BAND]


def node_velocity(total, bands, speed, width):
    tiles, rows, _ = total.shape
    height = rows // CHANNELS
    odd = lax.rem(lax.axis_index("cross"), 2)
    tile, lane = divmod(width - BAND, LANES)
    pad = jnp.zeros((LANES - BAND, LANES), jnp.float32)
    for link, came in enumerate(bands):
        band = jnp.transpose(jnp.concatenate([came[...], pad], axis=0))[:rows]
        at_first = odd if link == 0 else 1 - odd
        total[0] = total[0] + jnp.where(at_first == 1, band, 0.0)
        shifted = pltpu.roll(band, lane, 1) if lane else band
        total[tile] = total[tile] + jnp.where(at_first == 0, shifted, 0.0)
    tile_down = height - 2 * GHOST
    tile_cross = width - 2 * GHOST
    row_global = (
        lax.broadcasted_iota(jnp.int32, (height, LANES), 0)
        + lax.axis_index("down") * tile_down
        - GHOST
    )
    col_first = lax.broadcasted_iota(jnp.int32, (height, LANES), 1) - GHOST
    total_rows = tile_down * lax.axis_size("down")
    total_cols = tile_cross * lax.axis_size("cross")
    keep_rows = (row_global > 0) & (row_global < total_rows - 1)
    for t in range(tiles):
        col_global = col_first + (lax.axis_index("cross") * tile_cross + t * LANES)
        kept = keep_rows & (col_global > 0) & (col_global < total_cols - 1)
        mass = jnp.maximum(total[t, :height, :], MASS_FLOOR)
        for c in range(2):
            value = total[t, (c + 1) * height : (c + 2) * height, :] / mass
            speed[t, c] = jnp.where(kept, value, 0.0)


def row_sums(terms, row):
    half = row < 4
    four = [
        jnp.where(half, terms[k], terms[k + 4])
        + pltpu.roll(jnp.where(half, terms[k + 4], terms[k]), 4, 0)
        for k in range(4)
    ]
    pair = (row & 2) == 0
    two = [
        jnp.where(
            pair, four[k] + pltpu.roll(four[k], 6, 0), four[k + 2] + pltpu.roll(four[k + 2], 2, 0)
        )
        for k in range(2)
    ]
    return jnp.where(
        (row & 1) == 0, two[0] + pltpu.roll(two[0], 7, 0), two[1] + pltpu.roll(two[1], 1, 0)
    )


def gather_terms(u, w, speed, first_row, first_col, rows, cols, lane):
    tile = first_col // LANES
    shift = first_col - tile * LANES
    spot = pl.ds(first_row, WIN_DOWN)
    here = jnp.concatenate([speed[tile, 0, spot, :], speed[tile, 1, spot, :]], axis=0)
    after = jnp.concatenate([speed[tile + 1, 0, spot, :], speed[tile + 1, 1, spot, :]], axis=0)
    window = jnp.where(lane >= shift, here, after)
    window = jnp.where(
        lane < WIN_CROSS,
        pltpu.roll(window, (LANES - shift) & (LANES - 1), 1),
        pltpu.roll(window, (WIN_CROSS + LANES - shift) & (LANES - 1), 1),
    )
    window = jnp.concatenate([window, low_part(window)], axis=0).astype(jnp.bfloat16)
    found = jnp.dot(
        window[:, : 2 * WIN_CROSS], cross_weights(w, cols), preferred_element_type=jnp.float32
    )
    found = found[: 2 * WIN_DOWN] + found[2 * WIN_DOWN :]
    value, slope = spline_pair(u - rows)
    along_d, along_c = found[:WIN_DOWN, :LANES], found[WIN_DOWN:, :LANES]
    across_d, across_c = found[:WIN_DOWN, LANES:], found[WIN_DOWN:, LANES:]
    return (
        value * along_d,
        value * along_c,
        slope * along_d,
        slope * along_c,
        value * across_d,
        value * across_c,
    )


def gather_rows(state, speed, place, blocks, group, out):
    rows = node_rows(WIN_DOWN)
    cols = node_rows(WIN_CROSS)
    lane = lax.broadcasted_iota(jnp.int32, (2 * WIN_DOWN, LANES), 1)
    row = lax.broadcasted_iota(jnp.int32, (ROWS, LANES), 0)

    def several(q, carry):
        for part in range(group // ROWS):
            base = q * group + part * ROWS
            terms = []
            for k in range(ROWS):
                one = pl.ds(base + k, 1)
                first_row, first_col = place(base + k)
                terms.append(
                    gather_terms(
                        state[0, one, :],
                        state[1, one, :],
                        speed,
                        first_row,
                        first_col,
                        rows,
                        cols,
                        lane,
                    )
                )
            vel_d, vel_c, l_dd, l_cd, l_dc, l_cc = (row_sums(t, row) for t in zip(*terms))
            vel_d, vel_c = 0.25 * vel_d, 0.25 * vel_c
            l_dd, l_cc = 0.5 * l_dd, 0.5 * l_cc
            rate_dc = 0.25 * (l_dc + l_cd)
            trace = l_dd + l_cc
            spot = pl.ds(pl.multiple_of(base, ROWS), ROWS)
            field = [state[f, spot, :] for f in range(FIELDS)]
            shear = (2.0 * TIME_STEP) * field[9]
            spread = (TIME_STEP * field[10]) * trace
            stretch = TIME_STEP * trace
            result = {
                0: jnp.clip(field[0] + TIME_STEP * vel_d, 0.5, WIN_DOWN - 1.5),
                1: jnp.clip(field[1] + TIME_STEP * vel_c, 0.5, WIN_CROSS - 1.5),
                2: vel_d,
                3: vel_c,
                4: field[4] + (spread + shear * l_dd),
                5: field[5] + shear * rate_dc,
                6: field[6] + (spread + shear * l_cc),
                8: field[8] + field[8] * stretch,
                11: field[11]
                + TIME_STEP * (l_dd * l_dd + l_cc * l_cc + 2.0 * rate_dc * rate_dc),
            }
            for f in range(FIELDS):
                out[f, spot, :] = result.get(f, field[f])
        return carry

    lax.fori_loop(0, blocks // group, several, 0)


def gather_kernel(step, links, width, anchor_down, anchor_cross, slots, *rest):
    state, total = rest[:2]
    bands = rest[2:links]
    moved = rest[links]
    sent = rest[links + 1 : 2 * links + 1]
    speed, sums = rest[2 * links + 1 :]
    blocks = state.shape[1]
    sums[...] = total[...]
    node_velocity(sums, bands, speed, width)
    gather_rows(
        state, speed, window_place(anchor_down, anchor_cross, step), blocks, GROUP, moved
    )
    cap = slots.shape[2]
    for link in range(links):
        side = link_side(link)
        for m in range(cap):
            sent[link][:, m : m + 1, :] = moved[:, pl.ds(slots[step, side, m], 1), :]


def swap_pairs(size, first):
    pairs = []
    for i in range(first, size - 1, 2):
        pairs += [(i, i + 1), (i + 1, i)]
    return pairs


def odd_groups(size_down, size_cross):
    groups = []
    for i in (0, size_down - 1):
        groups += [[i * size_cross + j, i * size_cross + j + 1] for j in range(0, size_cross, 2)]
    for i in range(1, size_down - 1, 2):
        groups += [[i * size_cross + j, (i + 1) * size_cross + j] for j in range(size_cross)]
    return groups


def solution(mesh):
    size_down, size_cross = mesh.shape["down"], mesh.shape["cross"]
    links = 3 if size_cross <= 2 else 4
    smem = pl.BlockSpec(memory_space=pltpu.SMEM)
    vmem = pl.BlockSpec(memory_space=pltpu.VMEM)
    params = pltpu.CompilerParams(vmem_limit_bytes=40 * 1024 * 1024)
    f32 = jnp.float32

    def swap(x, link):
        axis, second = divmod(link, 2)
        name, size = (("down", size_down), ("cross", size_cross))[axis]
        return lax.ppermute(x, name, swap_pairs(size, second))

    def on_device(particles, anchor_down, anchor_cross, move_count, move_slots):
        blocks = particles.shape[0]
        cap = move_slots.shape[2]
        slots = move_slots.reshape(STEPS, 4, cap)
        counts = move_count.reshape(STEPS, 4)
        height = TILE_DOWN + 2 * GHOST
        width = TILE_CROSS + 2 * GHOST
        tiles = -(-width // LANES)
        grid_type = jax.ShapeDtypeStruct((tiles, CHANNELS * height, LANES), f32)
        band_type = jax.ShapeDtypeStruct((2, tiles, CHANNELS * BAND, LANES), f32)
        state_type = jax.ShapeDtypeStruct((FIELDS, blocks, LANES), f32)
        sent_type = jax.ShapeDtypeStruct((FIELDS, cap, LANES), f32)
        sums_scratch = pltpu.VMEM((tiles * LANES, LANES), f32)
        loads_scratch = pltpu.VMEM((LOADS, blocks, LANES), f32)
        state = jnp.transpose(particles, (1, 0, 2))
        arrived = []
        for step in range(STEPS):
            if step == 0:
                grid, pay = pl.pallas_call(
                    functools.partial(first_kernel, step),
                    out_shape=(grid_type, band_type),
                    in_specs=[smem, smem, vmem],
                    out_specs=(vmem, vmem),
                    scratch_shapes=[sums_scratch, loads_scratch],
                    compiler_params=params,
                    name="scatter_first",
                )(anchor_down, anchor_cross, state)
            else:
                state, grid, pay = pl.pallas_call(
                    functools.partial(next_kernel, step, links),
                    out_shape=(state_type, grid_type, band_type),
                    in_specs=[smem] * 4 + [vmem] * (1 + links),
                    out_specs=(vmem, vmem, vmem),
                    scratch_shapes=[sums_scratch, loads_scratch],
                    compiler_params=params,
                    name="scatter_next",
                )(anchor_down, anchor_cross, slots, counts, state, *arrived)
            band0 = swap(pay[0], 0)
            band1 = lax.all_gather(
                pay[1], ("down", "cross"), axis_index_groups=odd_groups(size_down, size_cross)
            )
            total, pay = pl.pallas_call(
                functools.partial(cross_kernel, width),
                out_shape=(grid_type, jax.ShapeDtypeStruct((2, BAND, LANES), f32)),
                in_specs=[vmem] * 3,
                out_specs=(vmem, vmem),
                compiler_params=params,
                name="add_down",
            )(grid, band0, band1)
            bands = [swap(pay[k], 2 + k) for k in range(links - 2)]
            state, *sent = pl.pallas_call(
                functools.partial(gather_kernel, step, links, width),
                out_shape=(state_type,) + (sent_type,) * links,
                in_specs=[smem] * 3 + [vmem] * links,
                out_specs=(vmem,) * (1 + links),
                scratch_shapes=[
                    pltpu.VMEM((tiles, 2, height, LANES), f32),
                    pltpu.VMEM(grid_type.shape, f32),
                ],
                compiler_params=params,
                name="gather",
            )(anchor_down, anchor_cross, slots, state, total, *bands)
            arrived = [swap(sent[k], k) for k in range(links)]
        state = pl.pallas_call(
            functools.partial(last_kernel, STEPS - 1, links),
            out_shape=state_type,
            in_specs=[smem] * 2 + [vmem] * (1 + links),
            out_specs=vmem,
            compiler_params=params,
            name="settle_last",
        )(slots, counts, state, *arrived)
        return jnp.transpose(state, (1, 0, 2))

    return jax.shard_map(
        on_device,
        mesh=mesh,
        in_specs=(
            P(("down", "cross"), None, None),
            P(None, ("down", "cross")),
            P(None, ("down", "cross")),
            P(None, None, "down", "cross"),
            P(None, None, None, "down", "cross"),
        ),
        out_specs=P(("down", "cross"), None, None),
        check_vma=False,
    )
```

```python
import functools

import jax
import jax.numpy as jnp
from jax import lax
from jax.experimental import pallas as pl
from jax.experimental.pallas import tpu as pltpu
from jax.sharding import PartitionSpec as P

WIN_DOWN = 8
WIN_CROSS = 16
GHOST = 4
STEPS = 2
TILE_DOWN = 16
TILE_CROSS = 256
TIME_STEP = 0.1
GRAVITY = 5.6
MASS_FLOOR = 0.5
FIELDS = 12
LANES = 128
ROWS = 8
CHANNELS = 3
STRIDE = 32
BAND = 2 * GHOST
LOADS = 6
GROUP = 64
VMEM_BYTES = 32 * 1024 * 1024


def spline_pair(distance):
    near = jnp.clip(distance, -0.5, 0.5)
    far = jnp.clip(distance - near, -1.0, 1.0)
    twice = near + near
    slope = far - twice
    return slope * slope + (1.5 - 1.5 * twice * twice), slope


def low_part(x):
    return x - x.astype(jnp.bfloat16).astype(jnp.float32)


def node_rows(count):
    return lax.broadcasted_iota(jnp.int32, (count, LANES), 0).astype(jnp.float32)


def cross_weights(w, cols):
    value, slope = spline_pair(w - cols)
    both = jnp.concatenate([value, slope], axis=1)
    high = both.astype(jnp.bfloat16)
    low = (both - high.astype(jnp.float32)).astype(jnp.bfloat16)
    return jnp.concatenate([high, low], axis=0)


def particle_loads(state, loads, blocks, keep=None):
    for base in range(0, blocks, ROWS):
        spot = pl.ds(base, ROWS)
        vd, vc, sdd, sdc, scc, mass, vol = (state[f, spot, :] for f in range(2, 9))
        quarter = 0.25 * mass
        push = (-0.5 * TIME_STEP) * vol
        terms = (
            quarter,
            quarter * (vd + TIME_STEP * GRAVITY),
            quarter * vc,
            push * sdd,
            push * sdc,
            push * scc,
        )
        for k, term in enumerate(terms):
            loads[k, spot, :] = term if keep is None else term * keep[spot, :]


def scatter_block(u, w, load, sums, weights, slot, first_row, first_col, rows, cols, inside):
    value, slope = spline_pair(u - rows)
    across_weights = cross_weights(w, cols)
    if weights is not None:
        weights[0][slot] = across_weights
        weights[1][slot, :WIN_DOWN, :] = value
        weights[1][slot, WIN_DOWN:, :] = slope
    load_dc = load(4)
    parts = (
        (load(0) * value,),
        (load(1) * value + load(3) * slope, load_dc * value),
        (load(2) * value + load_dc * slope, load(5) * value),
    )
    gap = jnp.zeros((16, 2 * LANES), jnp.bfloat16)
    none = jnp.zeros((16, LANES), jnp.bfloat16)
    pieces = []
    for part in parts:
        halves = [jnp.concatenate([x, low_part(x)], axis=0).astype(jnp.bfloat16) for x in part]
        pieces += [jnp.concatenate((halves + [none])[:2], axis=1), gap]
    found = lax.dot_general(
        across_weights,
        jnp.concatenate(pieces, axis=0),
        (((1,), (1,)), ((), ())),
        preferred_element_type=jnp.float32,
    )
    found = found[:WIN_CROSS] + found[WIN_CROSS:]
    found = jnp.concatenate(
        [found, jnp.zeros((WIN_CROSS, LANES - CHANNELS * STRIDE), jnp.float32)], axis=1
    )
    found = jnp.where(inside, found + pltpu.roll(found, LANES - WIN_DOWN, 1), 0.0)
    found = pltpu.roll(found, first_row, 1)
    spot = pl.ds(first_col, WIN_CROSS)
    sums[spot, :] = sums[spot, :] + found


def scatter_rows(state, loads, sums, weights, slot_of, place, first, count, group):
    rows = node_rows(WIN_DOWN)
    cols = node_rows(WIN_CROSS)
    lane = lax.broadcasted_iota(jnp.int32, (WIN_CROSS, LANES), 1)
    inside = (lane & (STRIDE - 1)) < WIN_DOWN

    def several(q, carry):
        for k in range(group):
            m = first + q * group + k
            row = pl.ds(m, 1)
            slot = slot_of(m)
            first_row, first_col = place(slot)
            scatter_block(
                state[0, row, :],
                state[1, row, :],
                lambda f, row=row: loads[f, row, :],
                sums,
                weights,
                slot,
                first_row,
                first_col,
                rows,
                cols,
                inside,
            )
        return carry

    steps = count // group
    if steps == 1:
        several(0, 0)
    else:
        lax.fori_loop(0, steps, several, 0)


def window_place(anchor_down, anchor_cross, step):
    return lambda b: (anchor_down[step, b] + GHOST, anchor_cross[step, b] + GHOST)


def write_grid(sums, grid, pay):
    tiles, rows, _ = grid.shape
    height = rows // CHANNELS
    odd = lax.rem(lax.axis_index("down"), 2)
    for t in range(tiles):
        turned = jnp.transpose(sums[t * LANES : (t + 1) * LANES, :])
        for c in range(CHANNELS):
            part = turned[c * STRIDE : c * STRIDE + height]
            grid[t, c * height : (c + 1) * height, :] = part
            spot = slice(c * BAND, (c + 1) * BAND)
            pay[odd, t, spot, :] = part[height - BAND :]
            pay[1 - odd, t, spot, :] = part[:BAND]


def first_kernel(
    step,
    parts,
    down_in,
    cross_in,
    slots_in,
    counts_in,
    particles,
    state,
    grid,
    pay,
    wide,
    tall,
    anchor_down,
    anchor_cross,
    slots,
    counts,
    sums,
    loads,
    down_scalar,
    cross_scalar,
    sems,
):
    blocks = particles.shape[1]
    size = blocks // parts
    scalars = [
        pltpu.make_async_copy(src, dst, sems.at[k])
        for k, (src, dst) in enumerate(((down_in, down_scalar), (cross_in, cross_scalar)))
    ]
    whole = [
        pltpu.make_async_copy(
            particles.at[:, pl.ds(k * size, size), :],
            state.at[:, pl.ds(k * size, size), :],
            sems.at[2 + k],
        )
        for k in range(parts)
    ]
    others = [
        pltpu.make_async_copy(src, dst, sems.at[2 + parts + k])
        for k, (src, dst) in enumerate(
            (
                (down_in, anchor_down),
                (cross_in, anchor_cross),
                (slots_in, slots),
                (counts_in, counts),
            )
        )
    ]
    for copy in scalars + whole + others:
        copy.start()
    sums[...] = jnp.zeros_like(sums)
    for copy in scalars:
        copy.wait()
    place = window_place(down_scalar, cross_scalar, step)
    for k in range(parts):
        whole[k].wait()
        particle_loads(state.at[:, pl.ds(k * size, size), :], loads.at[:, pl.ds(k * size, size), :], size)
        scatter_rows(
            state, loads, sums, (wide, tall), lambda m: m, place, k * size, size, min(GROUP, size)
        )
    for copy in others:
        copy.wait()
    write_grid(sums, grid, pay)


def link_side(link):
    axis, second = divmod(link, 2)
    odd = lax.rem(lax.axis_index(("down", "cross")[axis]), 2)
    return 2 * axis + (1 - odd if second else odd)


def settle(state, field, arrived, slots, counts, step, blocks):
    cap = slots.shape[2]
    for link, came in enumerate(arrived):
        side = link_side(link)
        for m in range(cap):
            slot = jnp.where(m < counts[step, side], slots[step, side, m], blocks)
            state[field, pl.ds(slot, 1), :] = came[field * cap + m : field * cap + m + 1, :]


def pick_arrived(refs):
    odd = lax.rem(lax.axis_index("down"), 2)
    return [ref.at[odd] if link == 1 else ref for link, ref in enumerate(refs)]


def next_kernel(step, links, anchor_down, anchor_cross, slots, counts, old, *rest):
    arrived = pick_arrived(rest[:links])
    state, grid, pay, wide, tall, sums, loads = rest[links:]
    blocks = loads.shape[1]
    state[:, :blocks, :] = old[:, :blocks, :]
    for f in range(FIELDS):
        settle(state, f, arrived, slots, counts, step - 1, blocks)
    sums[...] = jnp.zeros_like(sums)
    particle_loads(state, loads, blocks)
    scatter_rows(
        state,
        loads,
        sums,
        (wide, tall),
        lambda m: m,
        window_place(anchor_down, anchor_cross, step),
        0,
        blocks,
        min(GROUP, blocks),
    )
    write_grid(sums, grid, pay)


def gather_kernel(step, links, width, anchor_down, anchor_cross, slots, state, total, *rest):
    bands = rest[: links - 2]
    wide, tall, after = rest[links - 2 : links + 1]
    sent = rest[links + 1 : 2 * links + 1]
    speed, sums = rest[2 * links + 1 :]
    blocks = wide.shape[0]
    sums[...] = total[...]
    node_velocity(sums, bands, speed, width)
    gather_rows(
        state,
        speed,
        (wide, tall),
        lambda m: m,
        window_place(anchor_down, anchor_cross, step),
        blocks,
        min(GROUP, blocks),
        after,
    )
    cap = slots.shape[2]
    for link in range(links):
        side = link_side(link)
        for m in range(cap):
            slot = pl.ds(slots[step, side, m], 1)
            for f in range(FIELDS):
                sent[link][f * cap + m : f * cap + m + 1, :] = after[f, slot, :]


def last_kernel(step, links, slots, counts, old, *rest):
    arrived = pick_arrived(rest[:links])
    out, state, sems = rest[links:]
    blocks = out.shape[1]
    copies = []
    for f in range(FIELDS):
        state[f, :blocks, :] = old[f, :blocks, :]
        settle(state, f, arrived, slots, counts, step, blocks)
        copies.append(pltpu.make_async_copy(state.at[f, pl.ds(0, blocks), :], out.at[f], sems.at[f]))
        copies[-1].start()
    for copy in copies:
        copy.wait()


def cross_kernel(width, grid, band0, band1, total, pay):
    tiles, rows, _ = grid.shape
    height = rows // CHANNELS
    odd = lax.rem(lax.axis_index("down"), 2)
    index = lax.axis_index("down")
    size = lax.axis_size("down")
    total[...] = grid[...]
    partner = index - 1 + 2 * odd
    there = (partner >= 0) & (partner < size)
    for t in range(tiles):
        for c in range(CHANNELS):
            spot = slice(c * BAND, (c + 1) * BAND)
            for link in range(2):
                if link == 0:
                    band = band0[t, spot, :]
                else:
                    band = jnp.where(there, band1[odd, t, spot, :], 0.0)
                at_first = odd if link == 0 else 1 - odd
                start = c * height + (1 - at_first) * (height - BAND)
                place = pl.ds(pl.multiple_of(start, 8), BAND)
                total[t, place, :] = total[t, place, :] + band
    odd = lax.rem(lax.axis_index("cross"), 2)
    tile, lane = divmod(width - BAND, LANES)
    last = pltpu.roll(total[tile], LANES - lane, 1) if lane else total[tile]
    pad = jnp.zeros((LANES - rows, LANES), jnp.float32)
    pay[odd] = jnp.transpose(jnp.concatenate([last, pad], axis=0))[:BAND]
    pay[1 - odd] = jnp.transpose(jnp.concatenate([total[0], pad], axis=0))[:BAND]


def node_velocity(total, bands, speed, width):
    tiles, rows, _ = total.shape
    height = rows // CHANNELS
    odd = lax.rem(lax.axis_index("cross"), 2)
    tile, lane = divmod(width - BAND, LANES)
    pad = jnp.zeros((LANES - BAND, LANES), jnp.float32)
    for link, came in enumerate(bands):
        band = jnp.transpose(jnp.concatenate([came[...], pad], axis=0))[:rows]
        at_first = odd if link == 0 else 1 - odd
        total[0] = total[0] + jnp.where(at_first == 1, band, 0.0)
        shifted = pltpu.roll(band, lane, 1) if lane else band
        total[tile] = total[tile] + jnp.where(at_first == 0, shifted, 0.0)
    tile_down = height - 2 * GHOST
    tile_cross = width - 2 * GHOST
    row_global = (
        lax.broadcasted_iota(jnp.int32, (height, LANES), 0)
        + lax.axis_index("down") * tile_down
        - GHOST
    )
    col_first = lax.broadcasted_iota(jnp.int32, (height, LANES), 1) - GHOST
    total_rows = tile_down * lax.axis_size("down")
    total_cols = tile_cross * lax.axis_size("cross")
    keep_rows = (row_global > 0) & (row_global < total_rows - 1)
    for t in range(tiles):
        col_global = col_first + (lax.axis_index("cross") * tile_cross + t * LANES)
        kept = keep_rows & (col_global > 0) & (col_global < total_cols - 1)
        mass = jnp.maximum(total[t, :height, :], MASS_FLOOR)
        for c in range(2):
            value = total[t, (c + 1) * height : (c + 2) * height, :] / mass
            speed[t, c] = jnp.where(kept, value, 0.0)


def row_sums(terms, row):
    half = row < 4
    four = [
        jnp.where(half, terms[k], terms[k + 4])
        + pltpu.roll(jnp.where(half, terms[k + 4], terms[k]), 4, 0)
        for k in range(4)
    ]
    pair = (row & 2) == 0
    two = [
        jnp.where(
            pair, four[k] + pltpu.roll(four[k], 6, 0), four[k + 2] + pltpu.roll(four[k + 2], 2, 0)
        )
        for k in range(2)
    ]
    return jnp.where(
        (row & 1) == 0, two[0] + pltpu.roll(two[0], 7, 0), two[1] + pltpu.roll(two[1], 1, 0)
    )


def gather_terms(weights, speed, slot, first_row, first_col, lane):
    tile = first_col // LANES
    shift = first_col - tile * LANES
    spot = pl.ds(first_row, WIN_DOWN)
    here = jnp.concatenate([speed[tile, 0, spot, :], speed[tile, 1, spot, :]], axis=0)
    after = jnp.concatenate([speed[tile + 1, 0, spot, :], speed[tile + 1, 1, spot, :]], axis=0)
    window = jnp.where(lane >= shift, here, after)
    window = jnp.where(
        lane < WIN_CROSS,
        pltpu.roll(window, (LANES - shift) & (LANES - 1), 1),
        pltpu.roll(window, (WIN_CROSS + LANES - shift) & (LANES - 1), 1),
    )
    window = jnp.concatenate([window, low_part(window)], axis=0).astype(jnp.bfloat16)
    found = jnp.dot(
        window[:, : 2 * WIN_CROSS], weights[0][slot], preferred_element_type=jnp.float32
    )
    found = found[: 2 * WIN_DOWN] + found[2 * WIN_DOWN :]
    value, slope = weights[1][slot, :WIN_DOWN, :], weights[1][slot, WIN_DOWN:, :]
    along_d, along_c = found[:WIN_DOWN, :LANES], found[WIN_DOWN:, :LANES]
    across_d, across_c = found[:WIN_DOWN, LANES:], found[WIN_DOWN:, LANES:]
    return (
        value * along_d,
        value * along_c,
        slope * along_d,
        slope * along_c,
        value * across_d,
        value * across_c,
    )


def gather_rows(state, speed, weights, slot_of, place, blocks, group, out):
    lane = lax.broadcasted_iota(jnp.int32, (2 * WIN_DOWN, LANES), 1)
    row = lax.broadcasted_iota(jnp.int32, (ROWS, LANES), 0)

    def several(q, carry):
        for part in range(group // ROWS):
            base = q * group + part * ROWS
            terms = []
            for k in range(ROWS):
                slot = slot_of(base + k)
                first_row, first_col = place(slot)
                terms.append(gather_terms(weights, speed, slot, first_row, first_col, lane))
            vel_d, vel_c, l_dd, l_cd, l_dc, l_cc = (row_sums(t, row) for t in zip(*terms))
            vel_d, vel_c = 0.25 * vel_d, 0.25 * vel_c
            l_dd, l_cc = 0.5 * l_dd, 0.5 * l_cc
            rate_dc = 0.25 * (l_dc + l_cd)
            trace = l_dd + l_cc
            spot = pl.ds(base if isinstance(base, int) else pl.multiple_of(base, ROWS), ROWS)
            field = [state[f, spot, :] for f in range(FIELDS)]
            shear = (2.0 * TIME_STEP) * field[9]
            spread = (TIME_STEP * field[10]) * trace
            stretch = TIME_STEP * trace
            result = {
                0: jnp.clip(field[0] + TIME_STEP * vel_d, 0.5, WIN_DOWN - 1.5),
                1: jnp.clip(field[1] + TIME_STEP * vel_c, 0.5, WIN_CROSS - 1.5),
                2: vel_d,
                3: vel_c,
                4: field[4] + (spread + shear * l_dd),
                5: field[5] + shear * rate_dc,
                6: field[6] + (spread + shear * l_cc),
                8: field[8] + field[8] * stretch,
                11: field[11]
                + TIME_STEP * (l_dd * l_dd + l_cc * l_cc + 2.0 * rate_dc * rate_dc),
            }
            for f in range(FIELDS):
                out[f, spot, :] = result.get(f, field[f])
        return carry

    steps = blocks // group
    if steps == 1:
        several(0, 0)
    else:
        lax.fori_loop(0, steps, several, 0)


def swap_pairs(size, first):
    pairs = []
    for i in range(first, size - 1, 2):
        pairs += [(i, i + 1), (i + 1, i)]
    return pairs


def odd_groups(size_down, size_cross):
    groups = []
    for i in (0, size_down - 1):
        groups += [[i * size_cross + j, i * size_cross + j + 1] for j in range(0, size_cross, 2)]
    for i in range(1, size_down - 1, 2):
        groups += [[i * size_cross + j, (i + 1) * size_cross + j] for j in range(size_cross)]
    return groups


def solution(mesh):
    size_down, size_cross = mesh.shape["down"], mesh.shape["cross"]
    links = 3 if size_cross <= 2 else 4
    smem = pl.BlockSpec(memory_space=pltpu.SMEM)
    vmem = pl.BlockSpec(memory_space=pltpu.VMEM)
    hbm = pl.BlockSpec(memory_space=pltpu.HBM)
    f32 = jnp.float32

    def swap(x, link):
        axis, second = divmod(link, 2)
        name, size = (("down", size_down), ("cross", size_cross))[axis]
        return lax.ppermute(x, name, swap_pairs(size, second))

    def gather_pairs(x):
        return lax.all_gather(
            x, ("down", "cross"), axis_index_groups=odd_groups(size_down, size_cross)
        )

    def call(name, kernel, outs, in_specs, scratch=()):
        return pl.pallas_call(
            kernel,
            out_shape=outs,
            in_specs=in_specs,
            out_specs=tuple(hbm if isinstance(x, pl.MemoryRef) else vmem for x in outs),
            scratch_shapes=scratch,
            compiler_params=pltpu.CompilerParams(vmem_limit_bytes=VMEM_BYTES),
            name=name,
        )

    def on_device(particles, anchor_down, anchor_cross, move_count, move_slots):
        blocks = particles.shape[0]
        cap = move_slots.shape[2]
        height = TILE_DOWN + 2 * GHOST
        width = TILE_CROSS + 2 * GHOST
        tiles = -(-width // LANES)

        def array(*shape, dtype=f32):
            return jax.ShapeDtypeStruct(shape, dtype)

        grid_type = array(tiles, CHANNELS * height, LANES)
        band_type = array(2, tiles, CHANNELS * BAND, LANES)
        state_type = array(FIELDS, blocks + ROWS, LANES)
        sent_type = array(-(-FIELDS * cap // 8) * 8, LANES)
        weight_types = (
            array(blocks, 2 * WIN_CROSS, 2 * LANES, dtype=jnp.bfloat16),
            array(blocks, 2 * WIN_DOWN, LANES),
        )
        scatter_scratch = [
            pltpu.VMEM((tiles * LANES, LANES), f32),
            pltpu.VMEM((LOADS, blocks, LANES), f32),
        ]
        ints = (
            anchor_down,
            anchor_cross,
            move_slots.reshape(STEPS, 4, cap),
            move_count.reshape(STEPS, 4),
        )
        given = ints + (jnp.transpose(particles, (1, 0, 2)),)
        parts = 2
        state, grid, pay, *rest = call(
            "scatter_first",
            functools.partial(first_kernel, 0, parts),
            (state_type, grid_type, band_type)
            + weight_types
            + tuple(array(*x.shape, dtype=x.dtype) for x in ints),
            [hbm] * 5,
            scatter_scratch
            + [
                pltpu.SMEM(anchor_down.shape, jnp.int32),
                pltpu.SMEM(anchor_cross.shape, jnp.int32),
                pltpu.SemaphoreType.DMA((6 + parts,)),
            ],
        )(*(pltpu.with_memory_space_constraint(x, pltpu.HBM) for x in given))
        weights, ints = rest[:2], rest[2:]
        for step in range(STEPS):
            if step:
                state, grid, pay, *weights = call(
                    "scatter_next",
                    functools.partial(next_kernel, step, links),
                    (state_type, grid_type, band_type) + weight_types,
                    [smem] * 4 + [vmem] * (links + 1),
                    scatter_scratch,
                )(*ints, state, *arrived)
            band0 = swap(pay[0], 0)
            band1 = gather_pairs(pay[1])
            total, pay = call(
                "add_down",
                functools.partial(cross_kernel, width),
                (grid_type, array(2, BAND, LANES)),
                [vmem] * 3,
            )(grid, band0, band1)
            bands = [swap(pay[k], 2 + k) for k in range(links - 2)]
            state, *sent = call(
                "gather",
                functools.partial(gather_kernel, step, links, width),
                (state_type,) + (sent_type,) * links,
                [smem] * 3 + [vmem] * (2 + links),
                [
                    pltpu.VMEM((tiles, 2, height, LANES), f32),
                    pltpu.VMEM(grid_type.shape, f32),
                ],
            )(*ints[:3], state, total, *bands, *weights)
            arrived = [
                gather_pairs(x) if link == 1 else swap(x, link) for link, x in enumerate(sent)
            ]
        (state,) = call(
            "settle_last",
            functools.partial(last_kernel, STEPS - 1, links),
            (pltpu.HBM((FIELDS, blocks, LANES), f32),),
            [smem] * 2 + [vmem] * (links + 1),
            [pltpu.VMEM(state_type.shape, f32), pltpu.SemaphoreType.DMA((FIELDS,))],
        )(*ints[2:], state, *arrived)
        return jnp.transpose(state, (1, 0, 2))

    return jax.shard_map(
        on_device,
        mesh=mesh,
        in_specs=(
            P(("down", "cross"), None, None),
            P(None, ("down", "cross")),
            P(None, ("down", "cross")),
            P(None, None, "down", "cross"),
            P(None, None, None, "down", "cross"),
        ),
        out_specs=P(("down", "cross"), None, None),
        check_vma=False,
    )
```

```python
import functools

import jax
import jax.numpy as jnp
from jax import lax
from jax.experimental import pallas as pl
from jax.experimental.pallas import tpu as pltpu
from jax.sharding import PartitionSpec as P

WIN_DOWN = 8
WIN_CROSS = 16
GHOST = 4
STEPS = 2
TILE_DOWN = 16
TILE_CROSS = 256
TIME_STEP = 0.1
GRAVITY = 5.6
MASS_FLOOR = 0.5
FIELDS = 12
LANES = 128
HALF_BITS = 6
HALF = 1 << HALF_BITS
ROWS = 8
CHANNELS = 3
STRIDE = 32
BAND = 2 * GHOST
LOADS = 6
GROUP = 128
VMEM_BYTES = 32 * 1024 * 1024


def spline_pair(distance):
    reach = jnp.clip(distance, -1.5, 1.5)
    near = jnp.clip(3.0 * distance, -1.5, 1.5)
    slope = reach - near
    return (slope * slope + 1.5) - (2.0 / 3.0) * (near * near), slope


def low_part(x):
    return x - x.astype(jnp.bfloat16).astype(jnp.float32)


def node_rows(count):
    return lax.broadcasted_iota(jnp.int32, (count, LANES), 0).astype(jnp.float32)


def cross_weights(w, cols):
    value, slope = spline_pair(w - cols)
    both = jnp.concatenate([value, slope], axis=1)
    high = both.astype(jnp.bfloat16)
    low = (both - high.astype(jnp.float32)).astype(jnp.bfloat16)
    return jnp.concatenate([high, low], axis=0)


def particle_loads(state, loads, blocks, keep=None):
    for base in range(0, blocks, ROWS):
        spot = pl.ds(base, ROWS)
        vd, vc, sdd, sdc, scc, mass, vol = (state[f, spot, :] for f in range(2, 9))
        quarter = 0.25 * mass
        push = (-0.5 * TIME_STEP) * vol
        terms = (
            quarter,
            quarter * (vd + TIME_STEP * GRAVITY),
            quarter * vc,
            push * sdd,
            push * sdc,
            push * scc,
        )
        for k, term in enumerate(terms):
            loads[k, spot, :] = term if keep is None else term * keep[spot, :]


def scatter_block(u, w, load, sums, weights, slot, first_row, first_col, rows, cols, inside):
    value, slope = spline_pair(u - rows)
    across_weights = cross_weights(w, cols)
    if weights is not None:
        weights[0][slot] = across_weights
        weights[1][slot, :WIN_DOWN, :] = value
        weights[1][slot, WIN_DOWN:, :] = slope
    load_dc = load(4)
    parts = (
        (load(0) * value,),
        (load(1) * value + load(3) * slope, load_dc * value),
        (load(2) * value + load_dc * slope, load(5) * value),
    )
    gap = jnp.zeros((16, 2 * LANES), jnp.bfloat16)
    none = jnp.zeros((16, LANES), jnp.bfloat16)
    pieces = []
    for part in parts:
        halves = [jnp.concatenate([x, low_part(x)], axis=0).astype(jnp.bfloat16) for x in part]
        pieces += [jnp.concatenate((halves + [none])[:2], axis=1), gap]
    found = lax.dot_general(
        across_weights,
        jnp.concatenate(pieces, axis=0),
        (((1,), (1,)), ((), ())),
        preferred_element_type=jnp.float32,
    )
    found = found[:WIN_CROSS] + found[WIN_CROSS:]
    found = jnp.concatenate(
        [found, jnp.zeros((WIN_CROSS, LANES - CHANNELS * STRIDE), jnp.float32)], axis=1
    )
    found = jnp.where(inside, found + pltpu.roll(found, LANES - WIN_DOWN, 1), 0.0)
    found = pltpu.roll(found, first_row, 1)
    spot = pl.ds(first_col, WIN_CROSS)
    sums[spot, :] = sums[spot, :] + found


def scatter_rows(state, loads, sums, weights, slot_of, place, first, count, group):
    rows = node_rows(WIN_DOWN)
    cols = node_rows(WIN_CROSS)
    lane = lax.broadcasted_iota(jnp.int32, (WIN_CROSS, LANES), 1)
    inside = (lane & (STRIDE - 1)) < WIN_DOWN

    def several(q, carry):
        for k in range(group):
            m = first + q * group + k
            row = pl.ds(m, 1)
            slot = slot_of(m)
            first_row, first_col = place(slot)
            scatter_block(
                state[0, row, :],
                state[1, row, :],
                lambda f, row=row: loads[f, row, :],
                sums,
                weights,
                slot,
                first_row,
                first_col,
                rows,
                cols,
                inside,
            )
        return carry

    steps = count // group
    if steps == 1:
        several(0, 0)
    else:
        lax.fori_loop(0, steps, several, 0)


def window_place(first, second, step, add=0):
    return lambda b: (first[step, b] + add, second[step, b] + add)


def write_grid(sums, grid, pay):
    tiles, rows, _ = grid.shape
    height = rows // CHANNELS
    odd = lax.rem(lax.axis_index("down"), 2)
    for t in range(tiles):
        turned = jnp.transpose(sums[t * LANES : (t + 1) * LANES, :])
        for c in range(CHANNELS):
            part = turned[c * STRIDE : c * STRIDE + height]
            grid[t, c * height : (c + 1) * height, :] = part
            spot = slice(c * BAND, (c + 1) * BAND)
            pay[odd, t, spot, :] = part[height - BAND :]
            pay[1 - odd, t, spot, :] = part[:BAND]


def first_kernel(
    step,
    parts,
    down_in,
    cross_in,
    slots_in,
    counts_in,
    particles,
    state,
    grid,
    pay,
    wide,
    tall,
    first_row,
    first_col,
    window_row,
    window_turn,
    slots,
    counts,
    sums,
    loads,
    table,
    down_scalar,
    cross_scalar,
    sems,
):
    blocks = particles.shape[1]
    size = blocks // parts
    scalars = [
        pltpu.make_async_copy(src, dst, sems.at[k])
        for k, (src, dst) in enumerate(((down_in, down_scalar), (cross_in, cross_scalar)))
    ]
    whole = [
        pltpu.make_async_copy(
            particles.at[:, pl.ds(k * size, size), :],
            state.at[:, pl.ds(k * size, size), :],
            sems.at[2 + k],
        )
        for k in range(parts)
    ]
    anchors = [
        pltpu.make_async_copy(src, table.at[k], sems.at[2 + parts + k])
        for k, src in enumerate((down_in, cross_in))
    ]
    moves = [
        pltpu.make_async_copy(src, dst, sems.at[4 + parts + k])
        for k, (src, dst) in enumerate(((slots_in, slots), (counts_in, counts)))
    ]
    for copy in scalars + whole[:1] + anchors + whole[1:] + moves:
        copy.start()
    sums[...] = jnp.zeros_like(sums)
    for copy in anchors:
        copy.wait()
    row = table[0] + GHOST
    col = table[1] + GHOST
    table[0] = row
    table[1] = col
    table[2] = (col >> HALF_BITS) * (2 * (TILE_DOWN + 2 * GHOST)) + row
    table[3] = (LANES - (col & (HALF - 1))) & (LANES - 1)
    tables = [
        pltpu.make_async_copy(table.at[k], dst, sems.at[6 + parts + k])
        for k, dst in enumerate((first_row, first_col, window_row, window_turn))
    ]
    for copy in tables:
        copy.start()
    for copy in scalars:
        copy.wait()
    place = window_place(down_scalar, cross_scalar, step, GHOST)
    for k in range(parts):
        whole[k].wait()
        particle_loads(state.at[:, pl.ds(k * size, size), :], loads.at[:, pl.ds(k * size, size), :], size)
        scatter_rows(
            state, loads, sums, (wide, tall), lambda m: m, place, k * size, size, min(GROUP, size)
        )
    write_grid(sums, grid, pay)
    for copy in tables + moves:
        copy.wait()


def link_side(link):
    axis, second = divmod(link, 2)
    odd = lax.rem(lax.axis_index(("down", "cross")[axis]), 2)
    return 2 * axis + (1 - odd if second else odd)


def settle(state, arrived, slots, counts, step, blocks):
    cap = slots.shape[2]
    for link, came in enumerate(arrived):
        side = link_side(link)
        count = counts[step, side]
        for m in range(cap):
            slot = pl.ds(jnp.where(m < count, slots[step, side, m], blocks), 1)
            for f in range(FIELDS):
                state[f, slot, :] = came[f * cap + m : f * cap + m + 1, :]


def pick_arrived(refs):
    odd = lax.rem(lax.axis_index("down"), 2)
    return [ref.at[odd] if link == 1 else ref for link, ref in enumerate(refs)]


def next_kernel(step, links, first_row, first_col, slots, counts, old, *rest):
    arrived = pick_arrived(rest[:links])
    state, grid, pay, wide, tall, sums, loads = rest[links:]
    blocks = loads.shape[1]
    state[:, :blocks, :] = old[:, :blocks, :]
    settle(state, arrived, slots, counts, step - 1, blocks)
    sums[...] = jnp.zeros_like(sums)
    particle_loads(state, loads, blocks)
    scatter_rows(
        state,
        loads,
        sums,
        (wide, tall),
        lambda m: m,
        window_place(first_row, first_col, step),
        0,
        blocks,
        min(GROUP, blocks),
    )
    write_grid(sums, grid, pay)


def gather_kernel(step, links, width, window_row, window_turn, slots, state, total, *rest):
    bands = rest[: links - 2]
    wide, tall, after = rest[links - 2 : links + 1]
    sent = rest[links + 1 : 2 * links + 1]
    speed, sums = rest[2 * links + 1 :]
    blocks = wide.shape[0]
    sums[...] = total[...]
    node_velocity(sums, bands, speed, width)
    gather_rows(
        state,
        speed,
        (wide, tall),
        lambda m: m,
        window_place(window_row, window_turn, step),
        blocks,
        min(GROUP, blocks),
        after,
    )
    cap = slots.shape[2]
    for link in range(links):
        side = link_side(link)
        for m in range(cap):
            slot = pl.ds(slots[step, side, m], 1)
            for f in range(FIELDS):
                sent[link][f * cap + m : f * cap + m + 1, :] = after[f, slot, :]


def last_kernel(step, links, slots, counts, old, *rest):
    arrived = pick_arrived(rest[:links])
    out, state, sems = rest[links:]
    blocks = out.shape[1]
    state[:, :blocks, :] = old[:, :blocks, :]
    settle(state, arrived, slots, counts, step, blocks)
    copy = pltpu.make_async_copy(state.at[:, pl.ds(0, blocks), :], out, sems.at[0])
    copy.start()
    copy.wait()


def cross_kernel(width, grid, band0, band1, total, pay):
    tiles, rows, _ = grid.shape
    height = rows // CHANNELS
    odd = lax.rem(lax.axis_index("down"), 2)
    index = lax.axis_index("down")
    size = lax.axis_size("down")
    total[...] = grid[...]
    partner = index - 1 + 2 * odd
    there = (partner >= 0) & (partner < size)
    for t in range(tiles):
        for c in range(CHANNELS):
            spot = slice(c * BAND, (c + 1) * BAND)
            for link in range(2):
                if link == 0:
                    band = band0[t, spot, :]
                else:
                    band = jnp.where(there, band1[odd, t, spot, :], 0.0)
                at_first = odd if link == 0 else 1 - odd
                start = c * height + (1 - at_first) * (height - BAND)
                place = pl.ds(pl.multiple_of(start, 8), BAND)
                total[t, place, :] = total[t, place, :] + band
    odd = lax.rem(lax.axis_index("cross"), 2)
    tile, lane = divmod(width - BAND, LANES)
    last = pltpu.roll(total[tile], LANES - lane, 1) if lane else total[tile]
    pad = jnp.zeros((LANES - rows, LANES), jnp.float32)
    pay[odd] = jnp.transpose(jnp.concatenate([last, pad], axis=0))[:BAND]
    pay[1 - odd] = jnp.transpose(jnp.concatenate([total[0], pad], axis=0))[:BAND]


def node_velocity(total, bands, speed, width):
    tiles, rows, _ = total.shape
    height = rows // CHANNELS
    odd = lax.rem(lax.axis_index("cross"), 2)
    tile, lane = divmod(width - BAND, LANES)
    pad = jnp.zeros((LANES - BAND, LANES), jnp.float32)
    for link, came in enumerate(bands):
        band = jnp.transpose(jnp.concatenate([came[...], pad], axis=0))[:rows]
        at_first = odd if link == 0 else 1 - odd
        total[0] = total[0] + jnp.where(at_first == 1, band, 0.0)
        shifted = pltpu.roll(band, lane, 1) if lane else band
        total[tile] = total[tile] + jnp.where(at_first == 0, shifted, 0.0)
    tile_down = height - 2 * GHOST
    tile_cross = width - 2 * GHOST
    row_global = (
        lax.broadcasted_iota(jnp.int32, (height, LANES), 0)
        + lax.axis_index("down") * tile_down
        - GHOST
    )
    col_first = lax.broadcasted_iota(jnp.int32, (height, LANES), 1) - GHOST
    total_rows = tile_down * lax.axis_size("down")
    total_cols = tile_cross * lax.axis_size("cross")
    keep_rows = (row_global > 0) & (row_global < total_rows - 1)
    halves = speed.shape[0] // (2 * height)
    lane = lax.broadcasted_iota(jnp.int32, (2 * height, LANES), 1)
    before = None
    for t in range(tiles):
        col_global = col_first + (lax.axis_index("cross") * tile_cross + t * LANES)
        kept = keep_rows & (col_global > 0) & (col_global < total_cols - 1)
        factor = jnp.where(kept, 1.0 / jnp.maximum(total[t, :height, :], MASS_FLOOR), 0.0)
        value = total[t, height:, :] * jnp.concatenate([factor, factor], axis=0)
        turned = pltpu.roll(value, HALF, 1)
        if 2 * t < halves:
            speed[4 * t * height : (4 * t + 2) * height, :] = value
        if t and 2 * t - 1 < halves:
            speed[(4 * t - 2) * height : 4 * t * height, :] = jnp.where(lane < HALF, before, turned)
        before = turned


def row_sums(terms, row):
    half = row < 4
    four = [
        jnp.where(half, terms[k], terms[k + 4])
        + pltpu.roll(jnp.where(half, terms[k + 4], terms[k]), 4, 0)
        for k in range(4)
    ]
    pair = (row & 2) == 0
    two = [
        jnp.where(
            pair, four[k] + pltpu.roll(four[k], 6, 0), four[k + 2] + pltpu.roll(four[k + 2], 2, 0)
        )
        for k in range(2)
    ]
    return jnp.where(
        (row & 1) == 0, two[0] + pltpu.roll(two[0], 7, 0), two[1] + pltpu.roll(two[1], 1, 0)
    )


def gather_terms(weights, speed, slot, window_row, window_turn, lane):
    height = TILE_DOWN + 2 * GHOST
    window = jnp.concatenate(
        [speed[pl.ds(window_row, WIN_DOWN), :], speed[pl.ds(window_row + height, WIN_DOWN), :]],
        axis=0,
    )
    window = pltpu.roll(window, window_turn, 1)
    window = jnp.where(lane < WIN_CROSS, window, pltpu.roll(window, WIN_CROSS, 1))
    window = jnp.concatenate([window, low_part(window)], axis=0).astype(jnp.bfloat16)
    found = jnp.dot(
        window[:, : 2 * WIN_CROSS], weights[0][slot], preferred_element_type=jnp.float32
    )
    found = found[: 2 * WIN_DOWN] + found[2 * WIN_DOWN :]
    value, slope = weights[1][slot, :WIN_DOWN, :], weights[1][slot, WIN_DOWN:, :]
    along_d, along_c = found[:WIN_DOWN, :LANES], found[WIN_DOWN:, :LANES]
    across_d, across_c = found[:WIN_DOWN, LANES:], found[WIN_DOWN:, LANES:]
    return (
        value * along_d,
        value * along_c,
        slope * along_d,
        slope * along_c,
        value * across_d,
        value * across_c,
    )


def gather_rows(state, speed, weights, slot_of, place, blocks, group, out):
    lane = lax.broadcasted_iota(jnp.int32, (2 * WIN_DOWN, LANES), 1)
    row = lax.broadcasted_iota(jnp.int32, (ROWS, LANES), 0)

    def several(q, carry):
        for part in range(group // ROWS):
            base = q * group + part * ROWS
            terms = []
            for k in range(ROWS):
                slot = slot_of(base + k)
                terms.append(gather_terms(weights, speed, slot, *place(slot), lane))
            vel_d, vel_c, l_dd, l_cd, l_dc, l_cc = (row_sums(t, row) for t in zip(*terms))
            vel_d, vel_c = 0.25 * vel_d, 0.25 * vel_c
            l_dd, l_cc = 0.5 * l_dd, 0.5 * l_cc
            rate_dc = 0.25 * (l_dc + l_cd)
            trace = l_dd + l_cc
            spot = pl.ds(base if isinstance(base, int) else pl.multiple_of(base, ROWS), ROWS)
            field = [state[f, spot, :] for f in range(FIELDS)]
            shear = (2.0 * TIME_STEP) * field[9]
            spread = (TIME_STEP * field[10]) * trace
            stretch = TIME_STEP * trace
            result = {
                0: jnp.clip(field[0] + TIME_STEP * vel_d, 0.5, WIN_DOWN - 1.5),
                1: jnp.clip(field[1] + TIME_STEP * vel_c, 0.5, WIN_CROSS - 1.5),
                2: vel_d,
                3: vel_c,
                4: field[4] + (spread + shear * l_dd),
                5: field[5] + shear * rate_dc,
                6: field[6] + (spread + shear * l_cc),
                8: field[8] + field[8] * stretch,
                11: field[11]
                + TIME_STEP * (l_dd * l_dd + l_cc * l_cc + 2.0 * rate_dc * rate_dc),
            }
            for f in range(FIELDS):
                out[f, spot, :] = result.get(f, field[f])
        return carry

    steps = blocks // group
    if steps == 1:
        several(0, 0)
    else:
        lax.fori_loop(0, steps, several, 0)


def swap_pairs(size, first):
    pairs = []
    for i in range(first, size - 1, 2):
        pairs += [(i, i + 1), (i + 1, i)]
    return pairs


def odd_groups(size_down, size_cross):
    groups = []
    for i in (0, size_down - 1):
        groups += [[i * size_cross + j, i * size_cross + j + 1] for j in range(0, size_cross, 2)]
    for i in range(1, size_down - 1, 2):
        groups += [[i * size_cross + j, (i + 1) * size_cross + j] for j in range(size_cross)]
    return groups


def solution(mesh):
    size_down, size_cross = mesh.shape["down"], mesh.shape["cross"]
    links = 3 if size_cross <= 2 else 4
    smem = pl.BlockSpec(memory_space=pltpu.SMEM)
    vmem = pl.BlockSpec(memory_space=pltpu.VMEM)
    hbm = pl.BlockSpec(memory_space=pltpu.HBM)
    f32 = jnp.float32

    def swap(x, link):
        axis, second = divmod(link, 2)
        name, size = (("down", size_down), ("cross", size_cross))[axis]
        return lax.ppermute(x, name, swap_pairs(size, second))

    def gather_pairs(x):
        return lax.all_gather(
            x, ("down", "cross"), axis_index_groups=odd_groups(size_down, size_cross)
        )

    def call(name, kernel, outs, in_specs, scratch=()):
        return pl.pallas_call(
            kernel,
            out_shape=outs,
            in_specs=in_specs,
            out_specs=tuple(pl.BlockSpec(memory_space=x.memory_space) if isinstance(x, pl.MemoryRef) else vmem for x in outs),
            scratch_shapes=scratch,
            compiler_params=pltpu.CompilerParams(vmem_limit_bytes=VMEM_BYTES),
            name=name,
        )

    def on_device(particles, anchor_down, anchor_cross, move_count, move_slots):
        blocks = particles.shape[0]
        cap = move_slots.shape[2]
        height = TILE_DOWN + 2 * GHOST
        width = TILE_CROSS + 2 * GHOST
        tiles = -(-width // LANES)
        halves = (width - WIN_CROSS) // HALF + 1

        def array(*shape, dtype=f32):
            return jax.ShapeDtypeStruct(shape, dtype)

        grid_type = array(tiles, CHANNELS * height, LANES)
        band_type = array(2, tiles, CHANNELS * BAND, LANES)
        state_type = array(FIELDS, blocks + ROWS, LANES)
        sent_type = array(-(-FIELDS * cap // 8) * 8, LANES)
        weight_types = (
            array(blocks, 2 * WIN_CROSS, 2 * LANES, dtype=jnp.bfloat16),
            array(blocks, 2 * WIN_DOWN, LANES),
        )
        scatter_scratch = [
            pltpu.VMEM((tiles * LANES, LANES), f32),
            pltpu.VMEM((LOADS, blocks, LANES), f32),
        ]
        ints = (
            anchor_down,
            anchor_cross,
            move_slots.reshape(STEPS, 4, cap),
            move_count.reshape(STEPS, 4),
        )
        given = ints + (jnp.transpose(particles, (1, 0, 2)),)
        parts = 1
        state, grid, pay, *rest = call(
            "scatter_first",
            functools.partial(first_kernel, 0, parts),
            (state_type, grid_type, band_type)
            + weight_types
            + tuple(pltpu.SMEM(x.shape, x.dtype) for x in ints[:2] * 2 + ints[2:]),
            [hbm] * 5,
            scatter_scratch
            + [
                pltpu.VMEM((4,) + anchor_down.shape, jnp.int32),
                pltpu.SMEM(anchor_down.shape, jnp.int32),
                pltpu.SMEM(anchor_cross.shape, jnp.int32),
                pltpu.SemaphoreType.DMA((10 + parts,)),
            ],
        )(*(pltpu.with_memory_space_constraint(x, pltpu.HBM) for x in given))
        weights = rest[:2]
        rest = [pltpu.with_memory_space_constraint(x, pltpu.SMEM) for x in rest[2:]]
        windows, moves = rest[:4], rest[4:]
        for step in range(STEPS):
            if step:
                state, grid, pay, *weights = call(
                    "scatter_next",
                    functools.partial(next_kernel, step, links),
                    (state_type, grid_type, band_type) + weight_types,
                    [smem] * 4 + [vmem] * (links + 1),
                    scatter_scratch,
                )(*windows[:2], *moves, state, *arrived)
            band0 = swap(pay[0], 0)
            band1 = gather_pairs(pay[1])
            total, pay = call(
                "add_down",
                functools.partial(cross_kernel, width),
                (grid_type, array(2, BAND, LANES)),
                [vmem] * 3,
            )(grid, band0, band1)
            bands = [swap(pay[k], 2 + k) for k in range(links - 2)]
            state, *sent = call(
                "gather",
                functools.partial(gather_kernel, step, links, width),
                (state_type,) + (sent_type,) * links,
                [smem] * 3 + [vmem] * (2 + links),
                [
                    pltpu.VMEM((halves * 2 * height, LANES), f32),
                    pltpu.VMEM(grid_type.shape, f32),
                ],
            )(*windows[2:], moves[0], state, total, *bands, *weights)
            arrived = [
                gather_pairs(x) if link == 1 else swap(x, link) for link, x in enumerate(sent)
            ]
        (state,) = call(
            "settle_last",
            functools.partial(last_kernel, STEPS - 1, links),
            (pltpu.HBM((FIELDS, blocks, LANES), f32),),
            [smem] * 2 + [vmem] * (links + 1),
            [pltpu.VMEM(state_type.shape, f32), pltpu.SemaphoreType.DMA((1,))],
        )(*moves, state, *arrived)
        return jnp.transpose(state, (1, 0, 2))

    return jax.shard_map(
        on_device,
        mesh=mesh,
        in_specs=(
            P(("down", "cross"), None, None),
            P(None, ("down", "cross")),
            P(None, ("down", "cross")),
            P(None, None, "down", "cross"),
            P(None, None, None, "down", "cross"),
        ),
        out_specs=P(("down", "cross"), None, None),
        check_vma=False,
    )
```

```python
import functools

import jax
import jax.numpy as jnp
from jax import lax
from jax.experimental import pallas as pl
from jax.experimental.pallas import tpu as pltpu
from jax.sharding import PartitionSpec as P

WIN_DOWN = 8
WIN_CROSS = 16
GHOST = 4
STEPS = 2
TILE_DOWN = 16
TILE_CROSS = 256
TIME_STEP = 0.1
GRAVITY = 5.6
MASS_FLOOR = 0.5
FIELDS = 12
LANES = 128
HALF_BITS = 6
HALF = 1 << HALF_BITS
ROWS = 8
CHANNELS = 3
STRIDE = 32
BAND = 2 * GHOST
LOADS = 6
GROUP = 128
VMEM_BYTES = 32 * 1024 * 1024


def spline_pair(distance):
    reach = jnp.clip(distance, -1.5, 1.5)
    near = jnp.clip(3.0 * distance, -1.5, 1.5)
    slope = reach - near
    return (slope * slope + 1.5) - (2.0 / 3.0) * (near * near), slope


def low_part(x):
    return x - x.astype(jnp.bfloat16).astype(jnp.float32)


def node_rows(count):
    return lax.broadcasted_iota(jnp.int32, (count, LANES), 0).astype(jnp.float32)


def cross_weights(w, cols):
    value, slope = spline_pair(w - cols)
    both = jnp.concatenate([value, slope], axis=1)
    high = both.astype(jnp.bfloat16)
    low = (both - high.astype(jnp.float32)).astype(jnp.bfloat16)
    return jnp.concatenate([high, low], axis=0)


def particle_loads(state, loads, blocks, keep=None):
    for base in range(0, blocks, ROWS):
        spot = pl.ds(base, ROWS)
        vd, vc, sdd, sdc, scc, mass, vol = (state[f, spot, :] for f in range(2, 9))
        quarter = 0.25 * mass
        push = (-0.5 * TIME_STEP) * vol
        terms = (
            quarter,
            quarter * (vd + TIME_STEP * GRAVITY),
            quarter * vc,
            push * sdd,
            push * sdc,
            push * scc,
        )
        for k, term in enumerate(terms):
            loads[k, spot, :] = term if keep is None else term * keep[spot, :]


def scatter_block(u, w, load, sums, weights, slot, first_row, first_col, rows, cols, inside):
    value, slope = spline_pair(u - rows)
    across_weights = cross_weights(w, cols)
    if weights is not None:
        weights[0][slot] = across_weights
        weights[1][slot, :WIN_DOWN, :] = value
        weights[1][slot, WIN_DOWN:, :] = slope
    load_dc = load(4)
    parts = (
        (load(0) * value,),
        (load(1) * value + load(3) * slope, load_dc * value),
        (load(2) * value + load_dc * slope, load(5) * value),
    )
    gap = jnp.zeros((16, 2 * LANES), jnp.bfloat16)
    none = jnp.zeros((16, LANES), jnp.bfloat16)
    pieces = []
    for part in parts:
        halves = [jnp.concatenate([x, low_part(x)], axis=0).astype(jnp.bfloat16) for x in part]
        pieces += [jnp.concatenate((halves + [none])[:2], axis=1), gap]
    found = lax.dot_general(
        across_weights,
        jnp.concatenate(pieces, axis=0),
        (((1,), (1,)), ((), ())),
        preferred_element_type=jnp.float32,
    )
    found = found[:WIN_CROSS] + found[WIN_CROSS:]
    found = jnp.concatenate(
        [found, jnp.zeros((WIN_CROSS, LANES - CHANNELS * STRIDE), jnp.float32)], axis=1
    )
    found = jnp.where(inside, found + pltpu.roll(found, LANES - WIN_DOWN, 1), 0.0)
    found = pltpu.roll(found, first_row, 1)
    spot = pl.ds(first_col, WIN_CROSS)
    sums[spot, :] = sums[spot, :] + found


def edge_limits(width):
    index = lax.axis_index("cross")
    low = jnp.where(index > 0, BAND, 0)
    high = jnp.where(index < lax.axis_size("cross") - 1, width - BAND - WIN_CROSS, width)
    return low, high


def scatter_rows(state, loads, sums, weights, place, blocks, group, edge, limits):
    rows = node_rows(WIN_DOWN)
    cols = node_rows(WIN_CROSS)
    lane = lax.broadcasted_iota(jnp.int32, (WIN_CROSS, LANES), 1)
    inside = (lane & (STRIDE - 1)) < WIN_DOWN

    def several(q, listed):
        for k in range(group):
            m = q * group + k
            row = pl.ds(m, 1)
            first_row, first_col = place(m)
            edge[listed] = m
            at_edge = (first_col < limits[0]) | (first_col > limits[1])
            listed = listed + at_edge.astype(jnp.int32)
            scatter_block(
                state[0, row, :],
                state[1, row, :],
                lambda f, row=row: loads[f, row, :],
                sums,
                weights,
                m,
                first_row,
                first_col,
                rows,
                cols,
                inside,
            )
        return listed

    steps = blocks // group
    edge[blocks] = several(0, 0) if steps == 1 else lax.fori_loop(0, steps, several, 0)


def window_place(first, second, step, add=0):
    return lambda b: (first[step, b] + add, second[step, b] + add)


def write_grid(sums, grid, pay):
    tiles, rows, _ = grid.shape
    height = rows // CHANNELS
    odd = lax.rem(lax.axis_index("down"), 2)
    for t in range(tiles):
        turned = jnp.transpose(sums[t * LANES : (t + 1) * LANES, :])
        for c in range(CHANNELS):
            part = turned[c * STRIDE : c * STRIDE + height]
            grid[t, c * height : (c + 1) * height, :] = part
            spot = slice(c * BAND, (c + 1) * BAND)
            pay[odd, t, spot, :] = part[height - BAND :]
            pay[1 - odd, t, spot, :] = part[:BAND]


def first_kernel(
    step,
    width,
    down_in,
    cross_in,
    slots_in,
    counts_in,
    particles,
    state,
    grid,
    pay,
    wide,
    tall,
    first_row,
    first_col,
    window_row,
    window_turn,
    slots,
    counts,
    edge,
    sums,
    loads,
    table,
    down_scalar,
    cross_scalar,
    sems,
):
    blocks = particles.shape[1]
    scalars = [
        pltpu.make_async_copy(src, dst, sems.at[k])
        for k, (src, dst) in enumerate(((down_in, down_scalar), (cross_in, cross_scalar)))
    ]
    whole = pltpu.make_async_copy(particles, state.at[:, pl.ds(0, blocks), :], sems.at[2])
    anchors = [
        pltpu.make_async_copy(src, table.at[k], sems.at[3 + k])
        for k, src in enumerate((down_in, cross_in))
    ]
    moves = [
        pltpu.make_async_copy(src, dst, sems.at[5 + k])
        for k, (src, dst) in enumerate(((slots_in, slots), (counts_in, counts)))
    ]
    for copy in scalars + [whole] + anchors + moves:
        copy.start()
    sums[...] = jnp.zeros_like(sums)
    for copy in anchors:
        copy.wait()
    row = table[0] + GHOST
    col = table[1] + GHOST
    table[0] = row
    table[1] = col
    table[2] = (col >> HALF_BITS) * (2 * (TILE_DOWN + 2 * GHOST)) + row
    table[3] = (LANES - (col & (HALF - 1))) & (LANES - 1)
    tables = [
        pltpu.make_async_copy(table.at[k], dst, sems.at[7 + k])
        for k, dst in enumerate((first_row, first_col, window_row, window_turn))
    ]
    for copy in tables:
        copy.start()
    for copy in scalars:
        copy.wait()
    place = window_place(down_scalar, cross_scalar, step, GHOST)
    whole.wait()
    particle_loads(state, loads, blocks)
    scatter_rows(
        state, loads, sums, (wide, tall), place, blocks, GROUP, edge, edge_limits(width)
    )
    write_grid(sums, grid, pay)
    for copy in tables + moves:
        copy.wait()


def link_side(link):
    axis, second = divmod(link, 2)
    odd = lax.rem(lax.axis_index(("down", "cross")[axis]), 2)
    return 2 * axis + (1 - odd if second else odd)


def settle(state, arrived, slots, counts, step, blocks):
    cap = slots.shape[2]
    for link, came in enumerate(arrived):
        side = link_side(link)
        count = counts[step, side]
        for m in range(cap):
            slot = pl.ds(jnp.where(m < count, slots[step, side, m], blocks), 1)
            for f in range(FIELDS):
                state[f, slot, :] = came[f * cap + m : f * cap + m + 1, :]


def pick_arrived(refs):
    odd = lax.rem(lax.axis_index("down"), 2)
    return [ref.at[odd] if link == 1 else ref for link, ref in enumerate(refs)]


def next_kernel(step, links, width, first_row, first_col, slots, counts, old, *rest):
    arrived = pick_arrived(rest[:links])
    state, grid, pay, wide, tall, edge, sums, loads = rest[links:]
    blocks = loads.shape[1]
    state[:, :blocks, :] = old[:, :blocks, :]
    settle(state, arrived, slots, counts, step - 1, blocks)
    sums[...] = jnp.zeros_like(sums)
    particle_loads(state, loads, blocks)
    scatter_rows(
        state,
        loads,
        sums,
        (wide, tall),
        window_place(first_row, first_col, step),
        blocks,
        GROUP,
        edge,
        edge_limits(width),
    )
    write_grid(sums, grid, pay)


def gather_kernel(step, links, width, window_row, window_turn, slots, state, total, *rest):
    bands = rest[: links - 2]
    wide, tall, after = rest[links - 2 : links + 1]
    sent = rest[links + 1 : 2 * links + 1]
    speed, sums = rest[2 * links + 1 :]
    blocks = wide.shape[0]
    sums[...] = total[...]
    node_velocity(sums, bands, speed, width)
    gather_rows(
        state,
        speed,
        (wide, tall),
        lambda m: m,
        window_place(window_row, window_turn, step),
        blocks,
        min(GROUP, blocks),
        after,
    )
    cap = slots.shape[2]
    for link in range(links):
        side = link_side(link)
        for m in range(cap):
            slot = pl.ds(slots[step, side, m], 1)
            for f in range(FIELDS):
                sent[link][f * cap + m : f * cap + m + 1, :] = after[f, slot, :]


def last_kernel(step, links, slots, counts, old, *rest):
    arrived = pick_arrived(rest[:links])
    out, state, sems = rest[links:]
    blocks = out.shape[1]
    state[:, :blocks, :] = old[:, :blocks, :]
    settle(state, arrived, slots, counts, step, blocks)
    copy = pltpu.make_async_copy(state.at[:, pl.ds(0, blocks), :], out, sems.at[0])
    copy.start()
    copy.wait()


def cross_kernel(width, grid, band0, band1, total, pay):
    tiles, rows, _ = grid.shape
    height = rows // CHANNELS
    odd = lax.rem(lax.axis_index("down"), 2)
    index = lax.axis_index("down")
    size = lax.axis_size("down")
    total[...] = grid[...]
    partner = index - 1 + 2 * odd
    there = (partner >= 0) & (partner < size)
    for t in range(tiles):
        for c in range(CHANNELS):
            spot = slice(c * BAND, (c + 1) * BAND)
            for link in range(2):
                if link == 0:
                    band = band0[t, spot, :]
                else:
                    band = jnp.where(there, band1[odd, t, spot, :], 0.0)
                at_first = odd if link == 0 else 1 - odd
                start = c * height + (1 - at_first) * (height - BAND)
                place = pl.ds(pl.multiple_of(start, 8), BAND)
                total[t, place, :] = total[t, place, :] + band
    odd = lax.rem(lax.axis_index("cross"), 2)
    tile, lane = divmod(width - BAND, LANES)
    last = pltpu.roll(total[tile], LANES - lane, 1) if lane else total[tile]
    pad = jnp.zeros((LANES - rows, LANES), jnp.float32)
    pay[odd] = jnp.transpose(jnp.concatenate([last, pad], axis=0))[:BAND]
    pay[1 - odd] = jnp.transpose(jnp.concatenate([total[0], pad], axis=0))[:BAND]


def add_across(total, bands, sums, width):
    tiles, rows, _ = total.shape
    sums[...] = total[...]
    odd = lax.rem(lax.axis_index("cross"), 2)
    tile, lane = divmod(width - BAND, LANES)
    pad = jnp.zeros((LANES - BAND, LANES), jnp.float32)
    for link, came in enumerate(bands):
        band = jnp.transpose(jnp.concatenate([came[...], pad], axis=0))[:rows]
        at_first = odd if link == 0 else 1 - odd
        sums[0] = sums[0] + jnp.where(at_first == 1, band, 0.0)
        shifted = pltpu.roll(band, lane, 1) if lane else band
        sums[tile] = sums[tile] + jnp.where(at_first == 0, shifted, 0.0)


def node_velocity(total, speed, width):
    tiles, rows, _ = total.shape
    height = rows // CHANNELS
    tile_down = height - 2 * GHOST
    tile_cross = width - 2 * GHOST
    row_global = (
        lax.broadcasted_iota(jnp.int32, (height, LANES), 0)
        + lax.axis_index("down") * tile_down
        - GHOST
    )
    col_first = lax.broadcasted_iota(jnp.int32, (height, LANES), 1) - GHOST
    total_rows = tile_down * lax.axis_size("down")
    total_cols = tile_cross * lax.axis_size("cross")
    keep_rows = (row_global > 0) & (row_global < total_rows - 1)
    halves = speed.shape[0] // (2 * height)
    lane = lax.broadcasted_iota(jnp.int32, (2 * height, LANES), 1)
    before = None
    for t in range(tiles):
        col_global = col_first + (lax.axis_index("cross") * tile_cross + t * LANES)
        kept = keep_rows & (col_global > 0) & (col_global < total_cols - 1)
        factor = jnp.where(kept, 1.0 / jnp.maximum(total[t, :height, :], MASS_FLOOR), 0.0)
        value = total[t, height:, :] * jnp.concatenate([factor, factor], axis=0)
        turned = pltpu.roll(value, HALF, 1)
        if 2 * t < halves:
            speed[4 * t * height : (4 * t + 2) * height, :] = value
        if t and 2 * t - 1 < halves:
            speed[(4 * t - 2) * height : 4 * t * height, :] = jnp.where(lane < HALF, before, turned)
        before = turned


def row_sums(terms, row):
    half = row < 4
    four = [
        jnp.where(half, terms[k], terms[k + 4])
        + pltpu.roll(jnp.where(half, terms[k + 4], terms[k]), 4, 0)
        for k in range(4)
    ]
    pair = (row & 2) == 0
    two = [
        jnp.where(
            pair, four[k] + pltpu.roll(four[k], 6, 0), four[k + 2] + pltpu.roll(four[k + 2], 2, 0)
        )
        for k in range(2)
    ]
    return jnp.where(
        (row & 1) == 0, two[0] + pltpu.roll(two[0], 7, 0), two[1] + pltpu.roll(two[1], 1, 0)
    )


def gather_terms(weights, speed, slot, window_row, window_turn, lane):
    height = TILE_DOWN + 2 * GHOST
    window = jnp.concatenate(
        [speed[pl.ds(window_row, WIN_DOWN), :], speed[pl.ds(window_row + height, WIN_DOWN), :]],
        axis=0,
    )
    window = pltpu.roll(window, window_turn, 1)
    window = jnp.where(lane < WIN_CROSS, window, pltpu.roll(window, WIN_CROSS, 1))
    window = jnp.concatenate([window, low_part(window)], axis=0).astype(jnp.bfloat16)
    found = jnp.dot(
        window[:, : 2 * WIN_CROSS], weights[0][slot], preferred_element_type=jnp.float32
    )
    found = found[: 2 * WIN_DOWN] + found[2 * WIN_DOWN :]
    value, slope = weights[1][slot, :WIN_DOWN, :], weights[1][slot, WIN_DOWN:, :]
    along_d, along_c = found[:WIN_DOWN, :LANES], found[WIN_DOWN:, :LANES]
    across_d, across_c = found[:WIN_DOWN, LANES:], found[WIN_DOWN:, LANES:]
    return (
        value * along_d,
        value * along_c,
        slope * along_d,
        slope * along_c,
        value * across_d,
        value * across_c,
    )


def gather_eight(weights, speed, slots, place, field, lane, row):
    terms = [gather_terms(weights, speed, slot, *place(slot), lane) for slot in slots]
    vel_d, vel_c, l_dd, l_cd, l_dc, l_cc = (row_sums(t, row) for t in zip(*terms))
    vel_d, vel_c = 0.25 * vel_d, 0.25 * vel_c
    l_dd, l_cc = 0.5 * l_dd, 0.5 * l_cc
    rate_dc = 0.25 * (l_dc + l_cd)
    trace = l_dd + l_cc
    shear = (2.0 * TIME_STEP) * field[9]
    spread = (TIME_STEP * field[10]) * trace
    stretch = TIME_STEP * trace
    return {
        0: jnp.clip(field[0] + TIME_STEP * vel_d, 0.5, WIN_DOWN - 1.5),
        1: jnp.clip(field[1] + TIME_STEP * vel_c, 0.5, WIN_CROSS - 1.5),
        2: vel_d,
        3: vel_c,
        4: field[4] + (spread + shear * l_dd),
        5: field[5] + shear * rate_dc,
        6: field[6] + (spread + shear * l_cc),
        8: field[8] + field[8] * stretch,
        11: field[11] + TIME_STEP * (l_dd * l_dd + l_cc * l_cc + 2.0 * rate_dc * rate_dc),
    }


def gather_lanes():
    lane = lax.broadcasted_iota(jnp.int32, (2 * WIN_DOWN, LANES), 1)
    row = lax.broadcasted_iota(jnp.int32, (ROWS, LANES), 0)
    return lane, row


def inner_kernel(step, width, window_row, window_turn, state, total, wide, tall, after, speed):
    blocks = wide.shape[0]
    node_velocity(total, speed, width)
    place = window_place(window_row, window_turn, step)
    lane, row = gather_lanes()

    def several(q, carry):
        for base in range(0, GROUP, ROWS):
            slots = [q * GROUP + base + k for k in range(ROWS)]
            start = base if isinstance(q, int) else pl.multiple_of(slots[0], ROWS)
            spot = pl.ds(start, ROWS)
            field = [state[f, spot, :] for f in range(FIELDS)]
            result = gather_eight((wide, tall), speed, slots, place, field, lane, row)
            for f in range(FIELDS):
                after[f, spot, :] = result.get(f, field[f])
        return carry

    steps = blocks // GROUP
    if steps == 1:
        several(0, 0)
    else:
        lax.fori_loop(0, steps, several, 0)


def edge_kernel(step, links, width, window_row, window_turn, slots, edge, state, total, *rest):
    bands = rest[: links - 2]
    wide, tall, before, after = rest[links - 2 : links + 2]
    sent = rest[links + 2 : 2 * links + 2]
    speed, sums, rows = rest[2 * links + 2 :]
    blocks = wide.shape[0]
    after[:, :blocks, :] = before[:, :blocks, :]
    add_across(total, bands, sums, width)
    node_velocity(sums, speed, width)
    place = window_place(window_row, window_turn, step)
    lane, row = gather_lanes()
    count = edge[blocks]

    def eight(q, carry):
        picked = [edge[jnp.minimum(q * ROWS + k, count - 1)] for k in range(ROWS)]
        for k, slot in enumerate(picked):
            for f in range(FIELDS):
                rows[f, k : k + 1, :] = state[f, pl.ds(slot, 1), :]
        field = [rows[f] for f in range(FIELDS)]
        result = gather_eight((wide, tall), speed, picked, place, field, lane, row)
        for f, value in result.items():
            rows[f] = value
        for k, slot in enumerate(picked):
            for f in result:
                after[f, pl.ds(slot, 1), :] = rows[f, k : k + 1, :]
        return carry

    lax.fori_loop(0, (count + ROWS - 1) // ROWS, eight, 0)
    cap = slots.shape[2]
    for link in range(links):
        side = link_side(link)
        for m in range(cap):
            slot = pl.ds(slots[step, side, m], 1)
            for f in range(FIELDS):
                sent[link][f * cap + m : f * cap + m + 1, :] = after[f, slot, :]


def swap_pairs(size, first):
    pairs = []
    for i in range(first, size - 1, 2):
        pairs += [(i, i + 1), (i + 1, i)]
    return pairs


def odd_groups(size_down, size_cross):
    groups = []
    for i in (0, size_down - 1):
        groups += [[i * size_cross + j, i * size_cross + j + 1] for j in range(0, size_cross, 2)]
    for i in range(1, size_down - 1, 2):
        groups += [[i * size_cross + j, (i + 1) * size_cross + j] for j in range(size_cross)]
    return groups


def solution(mesh):
    size_down, size_cross = mesh.shape["down"], mesh.shape["cross"]
    links = 3 if size_cross <= 2 else 4
    smem = pl.BlockSpec(memory_space=pltpu.SMEM)
    vmem = pl.BlockSpec(memory_space=pltpu.VMEM)
    hbm = pl.BlockSpec(memory_space=pltpu.HBM)
    f32 = jnp.float32

    def swap(x, link):
        axis, second = divmod(link, 2)
        name, size = (("down", size_down), ("cross", size_cross))[axis]
        return lax.ppermute(x, name, swap_pairs(size, second))

    def gather_pairs(x):
        return lax.all_gather(
            x, ("down", "cross"), axis_index_groups=odd_groups(size_down, size_cross)
        )

    def call(name, kernel, outs, in_specs, scratch=(), flops=0):
        return pl.pallas_call(
            kernel,
            out_shape=outs,
            in_specs=in_specs,
            out_specs=tuple(pl.BlockSpec(memory_space=x.memory_space) if isinstance(x, pl.MemoryRef) else vmem for x in outs),
            scratch_shapes=scratch,
            compiler_params=pltpu.CompilerParams(vmem_limit_bytes=VMEM_BYTES),
            cost_estimate=pl.CostEstimate(flops=flops, bytes_accessed=1 << 20, transcendentals=0),
            name=name,
        )

    def on_device(particles, anchor_down, anchor_cross, move_count, move_slots):
        blocks = particles.shape[0]
        cap = move_slots.shape[2]
        height = TILE_DOWN + 2 * GHOST
        width = TILE_CROSS + 2 * GHOST
        tiles = -(-width // LANES)
        halves = (width - WIN_CROSS) // HALF + 1

        def array(*shape, dtype=f32):
            return jax.ShapeDtypeStruct(shape, dtype)

        grid_type = array(tiles, CHANNELS * height, LANES)
        band_type = array(2, tiles, CHANNELS * BAND, LANES)
        state_type = array(FIELDS, blocks + ROWS, LANES)
        sent_type = array(-(-FIELDS * cap // 8) * 8, LANES)
        weight_types = (
            array(blocks, 2 * WIN_CROSS, 2 * LANES, dtype=jnp.bfloat16),
            array(blocks, 2 * WIN_DOWN, LANES),
        )
        scatter_scratch = [
            pltpu.VMEM((tiles * LANES, LANES), f32),
            pltpu.VMEM((LOADS, blocks, LANES), f32),
        ]
        ints = (
            anchor_down,
            anchor_cross,
            move_slots.reshape(STEPS, 4, cap),
            move_count.reshape(STEPS, 4),
        )
        given = ints + (jnp.transpose(particles, (1, 0, 2)),)
        edge_type = pltpu.SMEM((blocks + 1,), jnp.int32)
        speed_scratch = pltpu.VMEM((halves * 2 * height, LANES), f32)
        state, grid, pay, *rest = call(
            "scatter_first",
            functools.partial(first_kernel, 0, width),
            (state_type, grid_type, band_type)
            + weight_types
            + tuple(pltpu.SMEM(x.shape, x.dtype) for x in ints[:2] * 2 + ints[2:])
            + (edge_type,),
            [hbm] * 5,
            scatter_scratch
            + [
                pltpu.VMEM((4,) + anchor_down.shape, jnp.int32),
                pltpu.SMEM(anchor_down.shape, jnp.int32),
                pltpu.SMEM(anchor_cross.shape, jnp.int32),
                pltpu.SemaphoreType.DMA((11,)),
            ],
        )(*(pltpu.with_memory_space_constraint(x, pltpu.HBM) for x in given))
        weights = rest[:2]
        rest = [pltpu.with_memory_space_constraint(x, pltpu.SMEM) for x in rest[2:]]
        windows, moves, edge = rest[:4], rest[4:6], rest[6]
        for step in range(STEPS):
            if step:
                state, grid, pay, *weights, edge = call(
                    "scatter_next",
                    functools.partial(next_kernel, step, links, width),
                    (state_type, grid_type, band_type) + weight_types + (edge_type,),
                    [smem] * 4 + [vmem] * (links + 1),
                    scatter_scratch,
                )(*windows[:2], *moves, state, *arrived)
            band0 = swap(pay[0], 0)
            band1 = gather_pairs(pay[1])
            total, pay = call(
                "add_down",
                functools.partial(cross_kernel, width),
                (grid_type, array(2, BAND, LANES)),
                [vmem] * 3,
            )(grid, band0, band1)
            bands = [swap(pay[k], 2 + k) for k in range(links - 2)]
            ahead = call(
                "gather_inner",
                functools.partial(inner_kernel, step, width),
                (state_type,),
                [smem] * 2 + [vmem] * 4,
                [speed_scratch],
                1 << 32,
            )(*windows[2:], state, total, *weights)
            edge = pltpu.with_memory_space_constraint(edge, pltpu.SMEM)
            state, *sent = call(
                "gather_edge",
                functools.partial(edge_kernel, step, links, width),
                (state_type,) + (sent_type,) * links,
                [smem] * 4 + [vmem] * (3 + links),
                [
                    speed_scratch,
                    pltpu.VMEM(grid_type.shape, f32),
                    pltpu.VMEM((FIELDS, ROWS, LANES), f32),
                ],
            )(*windows[2:], moves[0], edge, state, total, *bands, *weights, *ahead)
            arrived = [
                gather_pairs(x) if link == 1 else swap(x, link) for link, x in enumerate(sent)
            ]
        (state,) = call(
            "settle_last",
            functools.partial(last_kernel, STEPS - 1, links),
            (pltpu.HBM((FIELDS, blocks, LANES), f32),),
            [smem] * 2 + [vmem] * (links + 1),
            [pltpu.VMEM(state_type.shape, f32), pltpu.SemaphoreType.DMA((1,))],
        )(*moves, state, *arrived)
        return jnp.transpose(state, (1, 0, 2))

    return jax.shard_map(
        on_device,
        mesh=mesh,
        in_specs=(
            P(("down", "cross"), None, None),
            P(None, ("down", "cross")),
            P(None, ("down", "cross")),
            P(None, None, "down", "cross"),
            P(None, None, None, "down", "cross"),
        ),
        out_specs=P(("down", "cross"), None, None),
        check_vma=False,
    )
```

```python
import functools

import jax
import jax.numpy as jnp
from jax import lax
from jax.experimental import pallas as pl
from jax.experimental.pallas import tpu as pltpu
from jax.sharding import PartitionSpec as P

WIN_DOWN = 8
WIN_CROSS = 16
GHOST = 4
STEPS = 2
TILE_DOWN = 16
TILE_CROSS = 256
TIME_STEP = 0.1
GRAVITY = 5.6
MASS_FLOOR = 0.5
FIELDS = 12
LANES = 128
HALF_BITS = 6
HALF = 1 << HALF_BITS
ROWS = 8
CHANNELS = 3
STRIDE = 32
BAND = 2 * GHOST
LOADS = 6
GROUP = 128
VMEM_BYTES = 32 * 1024 * 1024


def spline_pair(distance):
    reach = jnp.clip(distance, -1.5, 1.5)
    near = jnp.clip(3.0 * distance, -1.5, 1.5)
    slope = reach - near
    return (slope * slope + 1.5) - (2.0 / 3.0) * (near * near), slope


def low_part(x):
    return x - x.astype(jnp.bfloat16).astype(jnp.float32)


def node_rows(count):
    return lax.broadcasted_iota(jnp.int32, (count, LANES), 0).astype(jnp.float32)


def cross_weights(w, cols):
    value, slope = spline_pair(w - cols)
    both = jnp.concatenate([value, slope], axis=1)
    high = both.astype(jnp.bfloat16)
    low = (both - high.astype(jnp.float32)).astype(jnp.bfloat16)
    return jnp.concatenate([high, low], axis=0)


def particle_loads(state, loads, blocks, keep=None):
    for base in range(0, blocks, ROWS):
        spot = pl.ds(base, ROWS)
        vd, vc, sdd, sdc, scc, mass, vol = (state[f, spot, :] for f in range(2, 9))
        quarter = 0.25 * mass
        push = (-0.5 * TIME_STEP) * vol
        terms = (
            quarter,
            quarter * (vd + TIME_STEP * GRAVITY),
            quarter * vc,
            push * sdd,
            push * sdc,
            push * scc,
        )
        for k, term in enumerate(terms):
            loads[k, spot, :] = term if keep is None else term * keep[spot, :]


def scatter_block(u, w, load, sums, weights, slot, first_row, first_col, rows, cols, inside):
    value, slope = spline_pair(u - rows)
    across_weights = cross_weights(w, cols)
    if weights is not None:
        weights[0][slot] = across_weights
        weights[1][slot, :WIN_DOWN, :] = value
        weights[1][slot, WIN_DOWN:, :] = slope
    load_dc = load(4)
    parts = (
        (load(0) * value,),
        (load(1) * value + load(3) * slope, load_dc * value),
        (load(2) * value + load_dc * slope, load(5) * value),
    )
    gap = jnp.zeros((16, 2 * LANES), jnp.bfloat16)
    none = jnp.zeros((16, LANES), jnp.bfloat16)
    pieces = []
    for part in parts:
        halves = [jnp.concatenate([x, low_part(x)], axis=0).astype(jnp.bfloat16) for x in part]
        pieces += [jnp.concatenate((halves + [none])[:2], axis=1), gap]
    found = lax.dot_general(
        across_weights,
        jnp.concatenate(pieces, axis=0),
        (((1,), (1,)), ((), ())),
        preferred_element_type=jnp.float32,
    )
    found = found[:WIN_CROSS] + found[WIN_CROSS:]
    found = jnp.concatenate(
        [found, jnp.zeros((WIN_CROSS, LANES - CHANNELS * STRIDE), jnp.float32)], axis=1
    )
    found = jnp.where(inside, found + pltpu.roll(found, LANES - WIN_DOWN, 1), 0.0)
    found = pltpu.roll(found, first_row, 1)
    spot = pl.ds(first_col, WIN_CROSS)
    sums[spot, :] = sums[spot, :] + found


def edge_limits(width):
    index = lax.axis_index("cross")
    low = jnp.where(index > 0, BAND, 0)
    high = jnp.where(index < lax.axis_size("cross") - 1, width - BAND - WIN_CROSS, width)
    return low, high


def scatter_rows(state, loads, sums, weights, place, blocks, group):
    rows = node_rows(WIN_DOWN)
    cols = node_rows(WIN_CROSS)
    lane = lax.broadcasted_iota(jnp.int32, (WIN_CROSS, LANES), 1)
    inside = (lane & (STRIDE - 1)) < WIN_DOWN

    def several(q, carry):
        for k in range(group):
            m = q * group + k
            row = pl.ds(m, 1)
            first_row, first_col = place(m)
            scatter_block(
                state[0, row, :],
                state[1, row, :],
                lambda f, row=row: loads[f, row, :],
                sums,
                weights,
                m,
                first_row,
                first_col,
                rows,
                cols,
                inside,
            )
        return carry

    steps = blocks // group
    if steps == 1:
        several(0, 0)
    else:
        lax.fori_loop(0, steps, several, 0)


def grid_place(anchor_down, anchor_cross, step):
    return lambda b: (anchor_down[step, b] + GHOST, anchor_cross[step, b] + GHOST)


def speed_place(anchor_down, anchor_cross, step):
    def place(b):
        col = anchor_cross[step, b] + GHOST
        row = (col >> HALF_BITS) * (2 * (TILE_DOWN + 2 * GHOST)) + anchor_down[step, b] + GHOST
        return row, (LANES - (col & (HALF - 1))) & (LANES - 1)

    return place


def write_grid(sums, grid, pay):
    tiles, rows, _ = grid.shape
    height = rows // CHANNELS
    odd = lax.rem(lax.axis_index("down"), 2)
    for t in range(tiles):
        turned = jnp.transpose(sums[t * LANES : (t + 1) * LANES, :])
        for c in range(CHANNELS):
            part = turned[c * STRIDE : c * STRIDE + height]
            grid[t, c * height : (c + 1) * height, :] = part
            spot = slice(c * BAND, (c + 1) * BAND)
            pay[odd, t, spot, :] = part[height - BAND :]
            pay[1 - odd, t, spot, :] = part[:BAND]


def first_kernel(
    step,
    down_in,
    cross_in,
    slots_in,
    counts_in,
    particles,
    state,
    grid,
    pay,
    wide,
    tall,
    anchor_down,
    anchor_cross,
    slots,
    counts,
    sums,
    loads,
    sems,
):
    blocks = particles.shape[1]
    whole = pltpu.make_async_copy(particles, state.at[:, pl.ds(0, blocks), :], sems.at[0])
    ints = [
        pltpu.make_async_copy(src, dst, sems.at[1 + k])
        for k, (src, dst) in enumerate(
            (
                (down_in, anchor_down),
                (cross_in, anchor_cross),
                (slots_in, slots),
                (counts_in, counts),
            )
        )
    ]
    for copy in ints[:2] + [whole] + ints[2:]:
        copy.start()
    sums[...] = jnp.zeros_like(sums)
    for copy in ints[:2]:
        copy.wait()
    whole.wait()
    particle_loads(state, loads, blocks)
    place = grid_place(anchor_down, anchor_cross, step)
    scatter_rows(state, loads, sums, (wide, tall), place, blocks, GROUP)
    write_grid(sums, grid, pay)
    for copy in ints[2:]:
        copy.wait()


def link_side(link):
    axis, second = divmod(link, 2)
    odd = lax.rem(lax.axis_index(("down", "cross")[axis]), 2)
    return 2 * axis + (1 - odd if second else odd)


def settle(state, arrived, slots, counts, step, blocks):
    cap = slots.shape[2]
    for link, came in enumerate(arrived):
        side = link_side(link)
        count = counts[step, side]
        for m in range(cap):
            slot = pl.ds(jnp.where(m < count, slots[step, side, m], blocks), 1)
            for f in range(FIELDS):
                state[f, slot, :] = came[f * cap + m : f * cap + m + 1, :]


def pick_arrived(refs):
    odd = lax.rem(lax.axis_index("down"), 2)
    return [ref.at[odd] if link == 1 else ref for link, ref in enumerate(refs)]


def next_kernel(step, links, anchor_down, anchor_cross, slots, counts, old, *rest):
    arrived = pick_arrived(rest[:links])
    state, grid, pay, wide, tall, sums, loads = rest[links:]
    blocks = loads.shape[1]
    state[:, :blocks, :] = old[:, :blocks, :]
    settle(state, arrived, slots, counts, step - 1, blocks)
    sums[...] = jnp.zeros_like(sums)
    particle_loads(state, loads, blocks)
    scatter_rows(
        state,
        loads,
        sums,
        (wide, tall),
        grid_place(anchor_down, anchor_cross, step),
        blocks,
        GROUP,
    )
    write_grid(sums, grid, pay)


def gather_kernel(step, links, width, window_row, window_turn, slots, state, total, *rest):
    bands = rest[: links - 2]
    wide, tall, after = rest[links - 2 : links + 1]
    sent = rest[links + 1 : 2 * links + 1]
    speed, sums = rest[2 * links + 1 :]
    blocks = wide.shape[0]
    sums[...] = total[...]
    node_velocity(sums, bands, speed, width)
    gather_rows(
        state,
        speed,
        (wide, tall),
        lambda m: m,
        window_place(window_row, window_turn, step),
        blocks,
        min(GROUP, blocks),
        after,
    )
    cap = slots.shape[2]
    for link in range(links):
        side = link_side(link)
        for m in range(cap):
            slot = pl.ds(slots[step, side, m], 1)
            for f in range(FIELDS):
                sent[link][f * cap + m : f * cap + m + 1, :] = after[f, slot, :]


def last_kernel(step, links, slots, counts, old, *rest):
    arrived = pick_arrived(rest[:links])
    out, state, sems = rest[links:]
    blocks = out.shape[1]
    state[:, :blocks, :] = old[:, :blocks, :]
    settle(state, arrived, slots, counts, step, blocks)
    copy = pltpu.make_async_copy(state.at[:, pl.ds(0, blocks), :], out, sems.at[0])
    copy.start()
    copy.wait()


def cross_kernel(width, grid, band0, band1, total, pay):
    tiles, rows, _ = grid.shape
    height = rows // CHANNELS
    odd = lax.rem(lax.axis_index("down"), 2)
    index = lax.axis_index("down")
    size = lax.axis_size("down")
    total[...] = grid[...]
    partner = index - 1 + 2 * odd
    there = (partner >= 0) & (partner < size)
    for t in range(tiles):
        for c in range(CHANNELS):
            spot = slice(c * BAND, (c + 1) * BAND)
            for link in range(2):
                if link == 0:
                    band = band0[t, spot, :]
                else:
                    band = jnp.where(there, band1[odd, t, spot, :], 0.0)
                at_first = odd if link == 0 else 1 - odd
                start = c * height + (1 - at_first) * (height - BAND)
                place = pl.ds(pl.multiple_of(start, 8), BAND)
                total[t, place, :] = total[t, place, :] + band
    odd = lax.rem(lax.axis_index("cross"), 2)
    tile, lane = divmod(width - BAND, LANES)
    last = pltpu.roll(total[tile], LANES - lane, 1) if lane else total[tile]
    pad = jnp.zeros((LANES - rows, LANES), jnp.float32)
    pay[odd] = jnp.transpose(jnp.concatenate([last, pad], axis=0))[:BAND]
    pay[1 - odd] = jnp.transpose(jnp.concatenate([total[0], pad], axis=0))[:BAND]


def add_across(total, bands, sums, width):
    tiles, rows, _ = total.shape
    sums[...] = total[...]
    odd = lax.rem(lax.axis_index("cross"), 2)
    tile, lane = divmod(width - BAND, LANES)
    pad = jnp.zeros((LANES - BAND, LANES), jnp.float32)
    for link, came in enumerate(bands):
        band = jnp.transpose(jnp.concatenate([came[...], pad], axis=0))[:rows]
        at_first = odd if link == 0 else 1 - odd
        sums[0] = sums[0] + jnp.where(at_first == 1, band, 0.0)
        shifted = pltpu.roll(band, lane, 1) if lane else band
        sums[tile] = sums[tile] + jnp.where(at_first == 0, shifted, 0.0)


def node_velocity(total, speed, width):
    tiles, rows, _ = total.shape
    height = rows // CHANNELS
    tile_down = height - 2 * GHOST
    tile_cross = width - 2 * GHOST
    row_global = (
        lax.broadcasted_iota(jnp.int32, (height, LANES), 0)
        + lax.axis_index("down") * tile_down
        - GHOST
    )
    col_first = lax.broadcasted_iota(jnp.int32, (height, LANES), 1) - GHOST
    total_rows = tile_down * lax.axis_size("down")
    total_cols = tile_cross * lax.axis_size("cross")
    keep_rows = (row_global > 0) & (row_global < total_rows - 1)
    halves = speed.shape[0] // (2 * height)
    lane = lax.broadcasted_iota(jnp.int32, (2 * height, LANES), 1)
    before = None
    for t in range(tiles):
        col_global = col_first + (lax.axis_index("cross") * tile_cross + t * LANES)
        kept = keep_rows & (col_global > 0) & (col_global < total_cols - 1)
        factor = jnp.where(kept, 1.0 / jnp.maximum(total[t, :height, :], MASS_FLOOR), 0.0)
        value = total[t, height:, :] * jnp.concatenate([factor, factor], axis=0)
        turned = pltpu.roll(value, HALF, 1)
        if 2 * t < halves:
            speed[4 * t * height : (4 * t + 2) * height, :] = value
        if t and 2 * t - 1 < halves:
            speed[(4 * t - 2) * height : 4 * t * height, :] = jnp.where(lane < HALF, before, turned)
        before = turned


def row_sums(terms, row):
    half = row < 4
    four = [
        jnp.where(half, terms[k], terms[k + 4])
        + pltpu.roll(jnp.where(half, terms[k + 4], terms[k]), 4, 0)
        for k in range(4)
    ]
    pair = (row & 2) == 0
    two = [
        jnp.where(
            pair, four[k] + pltpu.roll(four[k], 6, 0), four[k + 2] + pltpu.roll(four[k + 2], 2, 0)
        )
        for k in range(2)
    ]
    return jnp.where(
        (row & 1) == 0, two[0] + pltpu.roll(two[0], 7, 0), two[1] + pltpu.roll(two[1], 1, 0)
    )


def gather_terms(weights, speed, slot, window_row, window_turn, lane):
    height = TILE_DOWN + 2 * GHOST
    window = jnp.concatenate(
        [speed[pl.ds(window_row, WIN_DOWN), :], speed[pl.ds(window_row + height, WIN_DOWN), :]],
        axis=0,
    )
    window = pltpu.roll(window, window_turn, 1)
    window = jnp.where(lane < WIN_CROSS, window, pltpu.roll(window, WIN_CROSS, 1))
    window = jnp.concatenate([window, low_part(window)], axis=0).astype(jnp.bfloat16)
    found = jnp.dot(
        window[:, : 2 * WIN_CROSS], weights[0][slot], preferred_element_type=jnp.float32
    )
    found = found[: 2 * WIN_DOWN] + found[2 * WIN_DOWN :]
    value, slope = weights[1][slot, :WIN_DOWN, :], weights[1][slot, WIN_DOWN:, :]
    along_d, along_c = found[:WIN_DOWN, :LANES], found[WIN_DOWN:, :LANES]
    across_d, across_c = found[:WIN_DOWN, LANES:], found[WIN_DOWN:, LANES:]
    return (
        value * along_d,
        value * along_c,
        slope * along_d,
        slope * along_c,
        value * across_d,
        value * across_c,
    )


def gather_eight(weights, speed, slots, place, field, lane, row):
    terms = [gather_terms(weights, speed, slot, *place(slot), lane) for slot in slots]
    vel_d, vel_c, l_dd, l_cd, l_dc, l_cc = (row_sums(t, row) for t in zip(*terms))
    vel_d, vel_c = 0.25 * vel_d, 0.25 * vel_c
    l_dd, l_cc = 0.5 * l_dd, 0.5 * l_cc
    rate_dc = 0.25 * (l_dc + l_cd)
    trace = l_dd + l_cc
    shear = (2.0 * TIME_STEP) * field[9]
    spread = (TIME_STEP * field[10]) * trace
    stretch = TIME_STEP * trace
    return {
        0: jnp.clip(field[0] + TIME_STEP * vel_d, 0.5, WIN_DOWN - 1.5),
        1: jnp.clip(field[1] + TIME_STEP * vel_c, 0.5, WIN_CROSS - 1.5),
        2: vel_d,
        3: vel_c,
        4: field[4] + (spread + shear * l_dd),
        5: field[5] + shear * rate_dc,
        6: field[6] + (spread + shear * l_cc),
        8: field[8] + field[8] * stretch,
        11: field[11] + TIME_STEP * (l_dd * l_dd + l_cc * l_cc + 2.0 * rate_dc * rate_dc),
    }


def gather_lanes():
    lane = lax.broadcasted_iota(jnp.int32, (2 * WIN_DOWN, LANES), 1)
    row = lax.broadcasted_iota(jnp.int32, (ROWS, LANES), 0)
    return lane, row


def inner_kernel(
    step,
    links,
    width,
    anchor_down,
    anchor_cross,
    slots,
    state,
    total,
    wide,
    tall,
    after,
    edge,
    rank,
    *rest,
):
    sent, speed = rest[:-1], rest[-1]
    blocks = wide.shape[0]
    node_velocity(total, speed, width)
    place = speed_place(anchor_down, anchor_cross, step)
    lane, row = gather_lanes()
    low, high = edge_limits(width)

    def several(q, listed):
        for base in range(0, GROUP, ROWS):
            slots = [q * GROUP + base + k for k in range(ROWS)]
            start = base if isinstance(q, int) else pl.multiple_of(slots[0], ROWS)
            spot = pl.ds(start, ROWS)
            field = [state[f, spot, :] for f in range(FIELDS)]
            result = gather_eight((wide, tall), speed, slots, place, field, lane, row)
            for f in range(FIELDS):
                after[f, spot, :] = result.get(f, field[f])
            for slot in slots:
                edge[listed] = slot
                col = anchor_cross[step, slot] + GHOST
                listed = listed + ((col < low) | (col > high)).astype(jnp.int32)
        return listed

    steps = blocks // GROUP
    edge[blocks] = several(0, 0) if steps == 1 else lax.fori_loop(0, steps, several, 0)
    cap = slots.shape[2]
    plane = sent[0].shape[0]
    for b in range(blocks):
        rank[b] = links * plane
    for link in range(links):
        side = link_side(link)
        for m in range(cap):
            slot = slots[step, side, m]
            rank[slot] = link * plane + m
            for f in range(FIELDS):
                start = f * cap + m
                sent[link][start : start + 1, :] = after[f, pl.ds(slot, 1), :]


def edge_kernel(step, links, width, cap, anchor_down, anchor_cross, edge, rank, state, total, *rest):
    bands = rest[: links - 2]
    wide, tall, before = rest[links - 2 : links + 1]
    picked_before, after = rest[links + 1 : 2 * links + 1], rest[2 * links + 1]
    sent = rest[2 * links + 2 : 3 * links + 2]
    speed, sums, rows = rest[3 * links + 2 :]
    plane = picked_before[0].shape[0]
    blocks = wide.shape[0]
    after[:, :blocks, :] = before[:, :blocks, :]
    for out, given in zip(sent, picked_before):
        out[:plane, :] = given[...]
    add_across(total, bands, sums, width)
    node_velocity(sums, speed, width)
    place = speed_place(anchor_down, anchor_cross, step)
    lane, row = gather_lanes()
    count = edge[blocks]

    def eight(q, carry):
        picked = [edge[jnp.minimum(q * ROWS + k, count - 1)] for k in range(ROWS)]
        for k, slot in enumerate(picked):
            for f in range(FIELDS):
                rows[f, k : k + 1, :] = state[f, pl.ds(slot, 1), :]
        field = [rows[f] for f in range(FIELDS)]
        result = gather_eight((wide, tall), speed, picked, place, field, lane, row)
        for f, value in result.items():
            rows[f] = value
        for k, slot in enumerate(picked):
            start = rank[slot]
            for f in result:
                after[f, pl.ds(slot, 1), :] = rows[f, k : k + 1, :]
            for link in range(links):
                leaves = (start >= link * plane) & (start < (link + 1) * plane)
                first = jnp.where(leaves, start - link * plane, plane - 1)
                between = jnp.where(leaves, cap, 0)
                for f in result:
                    sent[link][pl.ds(first + f * between, 1), :] = rows[f, k : k + 1, :]
        return carry

    lax.fori_loop(0, (count + ROWS - 1) // ROWS, eight, 0)


def swap_pairs(size, first):
    pairs = []
    for i in range(first, size - 1, 2):
        pairs += [(i, i + 1), (i + 1, i)]
    return pairs


def odd_groups(size_down, size_cross):
    groups = []
    for i in (0, size_down - 1):
        groups += [[i * size_cross + j, i * size_cross + j + 1] for j in range(0, size_cross, 2)]
    for i in range(1, size_down - 1, 2):
        groups += [[i * size_cross + j, (i + 1) * size_cross + j] for j in range(size_cross)]
    return groups


def solution(mesh):
    size_down, size_cross = mesh.shape["down"], mesh.shape["cross"]
    links = 3 if size_cross <= 2 else 4
    smem = pl.BlockSpec(memory_space=pltpu.SMEM)
    vmem = pl.BlockSpec(memory_space=pltpu.VMEM)
    hbm = pl.BlockSpec(memory_space=pltpu.HBM)
    f32 = jnp.float32

    def swap(x, link):
        axis, second = divmod(link, 2)
        name, size = (("down", size_down), ("cross", size_cross))[axis]
        return lax.ppermute(x, name, swap_pairs(size, second))

    def gather_pairs(x):
        return lax.all_gather(
            x, ("down", "cross"), axis_index_groups=odd_groups(size_down, size_cross)
        )

    def call(name, kernel, outs, in_specs, scratch=(), flops=0):
        return pl.pallas_call(
            kernel,
            out_shape=outs,
            in_specs=in_specs,
            out_specs=tuple(pl.BlockSpec(memory_space=x.memory_space) if isinstance(x, pl.MemoryRef) else vmem for x in outs),
            scratch_shapes=scratch,
            compiler_params=pltpu.CompilerParams(vmem_limit_bytes=VMEM_BYTES),
            cost_estimate=pl.CostEstimate(flops=flops, bytes_accessed=1 << 20, transcendentals=0),
            name=name,
        )

    def on_device(particles, anchor_down, anchor_cross, move_count, move_slots):
        blocks = particles.shape[0]
        cap = move_slots.shape[2]
        height = TILE_DOWN + 2 * GHOST
        width = TILE_CROSS + 2 * GHOST
        tiles = -(-width // LANES)
        halves = (width - WIN_CROSS) // HALF + 1

        def array(*shape, dtype=f32):
            return jax.ShapeDtypeStruct(shape, dtype)

        grid_type = array(tiles, CHANNELS * height, LANES)
        band_type = array(2, tiles, CHANNELS * BAND, LANES)
        state_type = array(FIELDS, blocks + ROWS, LANES)
        plane = (FIELDS * cap // 8 + 1) * 8
        sent_type = array(plane, LANES)
        weight_types = (
            array(blocks, 2 * WIN_CROSS, 2 * LANES, dtype=jnp.bfloat16),
            array(blocks, 2 * WIN_DOWN, LANES),
        )
        scatter_scratch = [
            pltpu.VMEM((tiles * LANES, LANES), f32),
            pltpu.VMEM((LOADS, blocks, LANES), f32),
        ]
        ints = (
            anchor_down,
            anchor_cross,
            move_slots.reshape(STEPS, 4, cap),
            move_count.reshape(STEPS, 4),
        )
        given = ints + (jnp.transpose(particles, (1, 0, 2)),)
        edge_type = pltpu.SMEM((blocks + 1,), jnp.int32)
        speed_scratch = pltpu.VMEM((halves * 2 * height, LANES), f32)
        state, grid, pay, *rest = call(
            "scatter_first",
            functools.partial(first_kernel, 0),
            (state_type, grid_type, band_type)
            + weight_types
            + tuple(pltpu.SMEM(x.shape, x.dtype) for x in ints),
            [hbm] * 5,
            scatter_scratch
            + [
                pltpu.SemaphoreType.DMA((5,)),
            ],
        )(*(pltpu.with_memory_space_constraint(x, pltpu.HBM) for x in given))
        weights = rest[:2]
        rest = [pltpu.with_memory_space_constraint(x, pltpu.SMEM) for x in rest[2:]]
        anchors, moves = rest[:2], rest[2:]
        for step in range(STEPS):
            if step:
                state, grid, pay, *weights = call(
                    "scatter_next",
                    functools.partial(next_kernel, step, links),
                    (state_type, grid_type, band_type) + weight_types,
                    [smem] * 4 + [vmem] * (links + 1),
                    scatter_scratch,
                )(*anchors, *moves, state, *arrived)
            band0 = swap(pay[0], 0)
            band1 = gather_pairs(pay[1])
            total, pay = call(
                "add_down",
                functools.partial(cross_kernel, width),
                (grid_type, array(2, BAND, LANES)),
                [vmem] * 3,
            )(grid, band0, band1)
            bands = [swap(pay[k], 2 + k) for k in range(links - 2)]
            ahead, edge, rank, *picked = call(
                "gather_inner",
                functools.partial(inner_kernel, step, links, width),
                (state_type, edge_type, edge_type) + (sent_type,) * links,
                [smem] * 3 + [vmem] * 4,
                [speed_scratch],
                1 << 32,
            )(*anchors, moves[0], state, total, *weights)
            edge, rank = (pltpu.with_memory_space_constraint(x, pltpu.SMEM) for x in (edge, rank))
            state, *sent = call(
                "gather_edge",
                functools.partial(edge_kernel, step, links, width, cap),
                (state_type,) + (sent_type,) * links,
                [smem] * 4 + [vmem] * (3 + 2 * links),
                [
                    speed_scratch,
                    pltpu.VMEM(grid_type.shape, f32),
                    pltpu.VMEM((FIELDS, ROWS, LANES), f32),
                ],
            )(*anchors, edge, rank, state, total, *bands, *weights, ahead, *picked)
            arrived = [
                gather_pairs(x) if link == 1 else swap(x, link) for link, x in enumerate(sent)
            ]
        (state,) = call(
            "settle_last",
            functools.partial(last_kernel, STEPS - 1, links),
            (pltpu.HBM((FIELDS, blocks, LANES), f32),),
            [smem] * 2 + [vmem] * (links + 1),
            [pltpu.VMEM(state_type.shape, f32), pltpu.SemaphoreType.DMA((1,))],
        )(*moves, state, *arrived)
        return jnp.transpose(state, (1, 0, 2))

    return jax.shard_map(
        on_device,
        mesh=mesh,
        in_specs=(
            P(("down", "cross"), None, None),
            P(None, ("down", "cross")),
            P(None, ("down", "cross")),
            P(None, None, "down", "cross"),
            P(None, None, None, "down", "cross"),
        ),
        out_specs=P(("down", "cross"), None, None),
        check_vma=False,
    )
```

```python
import functools

import jax
import jax.numpy as jnp
from jax import lax
from jax.experimental import pallas as pl
from jax.experimental.pallas import tpu as pltpu
from jax.sharding import PartitionSpec as P

WIN_DOWN = 8
WIN_CROSS = 16
GHOST = 4
STEPS = 2
TILE_DOWN = 16
TILE_CROSS = 256
TIME_STEP = 0.1
GRAVITY = 5.6
MASS_FLOOR = 0.5
FIELDS = 12
LANES = 128
HALF_BITS = 6
HALF = 1 << HALF_BITS
ROWS = 8
CHANNELS = 3
STRIDE = 32
BAND = 2 * GHOST
LOADS = 6
GROUP = 128
VMEM_BYTES = 32 * 1024 * 1024


def spline_pair(distance):
    reach = jnp.clip(distance, -1.5, 1.5)
    near = jnp.clip(3.0 * distance, -1.5, 1.5)
    slope = reach - near
    return (slope * slope + 1.5) - (2.0 / 3.0) * (near * near), slope


def low_part(x):
    return x - x.astype(jnp.bfloat16).astype(jnp.float32)


def node_rows(count):
    return lax.broadcasted_iota(jnp.int32, (count, LANES), 0).astype(jnp.float32)


def cross_weights(w, cols):
    value, slope = spline_pair(w - cols)
    both = jnp.concatenate([value, slope], axis=1)
    high = both.astype(jnp.bfloat16)
    low = (both - high.astype(jnp.float32)).astype(jnp.bfloat16)
    return jnp.concatenate([high, low], axis=0)


def particle_loads(state, loads, blocks, keep=None):
    for base in range(0, blocks, ROWS):
        spot = pl.ds(base, ROWS)
        vd, vc, sdd, sdc, scc, mass, vol = (state[f, spot, :] for f in range(2, 9))
        quarter = 0.25 * mass
        push = (-0.5 * TIME_STEP) * vol
        terms = (
            quarter,
            quarter * (vd + TIME_STEP * GRAVITY),
            quarter * vc,
            push * sdd,
            push * sdc,
            push * scc,
        )
        for k, term in enumerate(terms):
            loads[k, spot, :] = term if keep is None else term * keep[spot, :]


def scatter_block(u, w, load, sums, weights, slot, first_row, first_col, rows, cols, inside):
    value, slope = spline_pair(u - rows)
    across_weights = cross_weights(w, cols)
    if weights is not None:
        weights[0][slot] = across_weights
        weights[1][slot, :WIN_DOWN, :] = value
        weights[1][slot, WIN_DOWN:, :] = slope
    load_dc = load(4)
    parts = (
        (load(0) * value,),
        (load(1) * value + load(3) * slope, load_dc * value),
        (load(2) * value + load_dc * slope, load(5) * value),
    )
    gap = jnp.zeros((16, 2 * LANES), jnp.bfloat16)
    none = jnp.zeros((16, LANES), jnp.bfloat16)
    pieces = []
    for part in parts:
        halves = [jnp.concatenate([x, low_part(x)], axis=0).astype(jnp.bfloat16) for x in part]
        pieces += [jnp.concatenate((halves + [none])[:2], axis=1), gap]
    found = lax.dot_general(
        across_weights,
        jnp.concatenate(pieces, axis=0),
        (((1,), (1,)), ((), ())),
        preferred_element_type=jnp.float32,
    )
    found = found[:WIN_CROSS] + found[WIN_CROSS:]
    found = jnp.concatenate(
        [found, jnp.zeros((WIN_CROSS, LANES - CHANNELS * STRIDE), jnp.float32)], axis=1
    )
    found = jnp.where(inside, found + pltpu.roll(found, LANES - WIN_DOWN, 1), 0.0)
    found = pltpu.roll(found, first_row, 1)
    spot = pl.ds(first_col, WIN_CROSS)
    sums[spot, :] = sums[spot, :] + found


def edge_limits(width):
    index = lax.axis_index("cross")
    low = jnp.where(index > 0, BAND, 0)
    high = jnp.where(index < lax.axis_size("cross") - 1, width - BAND - WIN_CROSS, width)
    return low, high


def scatter_rows(state, loads, sums, weights, place, blocks, group):
    rows = node_rows(WIN_DOWN)
    cols = node_rows(WIN_CROSS)
    lane = lax.broadcasted_iota(jnp.int32, (WIN_CROSS, LANES), 1)
    inside = (lane & (STRIDE - 1)) < WIN_DOWN

    def several(q, carry):
        for k in range(group):
            m = q * group + k
            row = pl.ds(m, 1)
            first_row, first_col = place(m)
            scatter_block(
                state[0, row, :],
                state[1, row, :],
                lambda f, row=row: loads[f, row, :],
                sums,
                weights,
                m,
                first_row,
                first_col,
                rows,
                cols,
                inside,
            )
        return carry

    steps = blocks // group
    if steps == 1:
        several(0, 0)
    else:
        lax.fori_loop(0, steps, several, 0)


def grid_place(anchor_down, anchor_cross, step):
    return lambda b: (anchor_down[step, b] + GHOST, anchor_cross[step, b] + GHOST)


def speed_place(anchor_down, anchor_cross, step):
    def place(b):
        col = anchor_cross[step, b] + GHOST
        row = (col >> HALF_BITS) * (2 * (TILE_DOWN + 2 * GHOST)) + anchor_down[step, b] + GHOST
        return row, (LANES - (col & (HALF - 1))) & (LANES - 1)

    return place


def write_grid(sums, grid, pay):
    tiles, rows, _ = grid.shape
    height = rows // CHANNELS
    odd = lax.rem(lax.axis_index("down"), 2)
    for t in range(tiles):
        turned = jnp.transpose(sums[t * LANES : (t + 1) * LANES, :])
        for c in range(CHANNELS):
            part = turned[c * STRIDE : c * STRIDE + height]
            grid[t, c * height : (c + 1) * height, :] = part
            spot = slice(c * BAND, (c + 1) * BAND)
            pay[odd, t, spot, :] = part[height - BAND :]
            pay[1 - odd, t, spot, :] = part[:BAND]


def first_kernel(
    step,
    down_in,
    cross_in,
    slots_in,
    counts_in,
    particles,
    state,
    grid,
    pay,
    wide,
    tall,
    anchor_down,
    anchor_cross,
    slots,
    counts,
    sums,
    loads,
    sems,
):
    blocks = particles.shape[1]
    whole = pltpu.make_async_copy(particles, state.at[:, pl.ds(0, blocks), :], sems.at[0])
    ints = [
        pltpu.make_async_copy(src, dst, sems.at[1 + k])
        for k, (src, dst) in enumerate(
            (
                (down_in, anchor_down),
                (cross_in, anchor_cross),
                (slots_in, slots),
                (counts_in, counts),
            )
        )
    ]
    for copy in ints[:2] + [whole] + ints[2:]:
        copy.start()
    sums[...] = jnp.zeros_like(sums)
    for copy in ints[:2]:
        copy.wait()
    whole.wait()
    particle_loads(state, loads, blocks)
    place = grid_place(anchor_down, anchor_cross, step)
    scatter_rows(state, loads, sums, (wide, tall), place, blocks, GROUP)
    write_grid(sums, grid, pay)
    for copy in ints[2:]:
        copy.wait()


def link_side(link):
    axis, second = divmod(link, 2)
    odd = lax.rem(lax.axis_index(("down", "cross")[axis]), 2)
    return 2 * axis + (1 - odd if second else odd)


def settle(state, arrived, slots, counts, step, blocks):
    cap = slots.shape[2]
    for link, came in enumerate(arrived):
        side = link_side(link)
        count = counts[step, side]
        for m in range(cap):
            slot = pl.ds(jnp.where(m < count, slots[step, side, m], blocks), 1)
            for f in range(FIELDS):
                state[f, slot, :] = came[f * cap + m : f * cap + m + 1, :]


def pick_arrived(refs):
    odd = lax.rem(lax.axis_index("down"), 2)
    return [ref.at[odd] if link == 1 else ref for link, ref in enumerate(refs)]


def next_kernel(step, links, anchor_down, anchor_cross, slots, counts, old, *rest):
    arrived = pick_arrived(rest[:links])
    state, grid, pay, wide, tall, sums, loads = rest[links:]
    blocks = loads.shape[1]
    state[:, :blocks, :] = old[:, :blocks, :]
    settle(state, arrived, slots, counts, step - 1, blocks)
    sums[...] = jnp.zeros_like(sums)
    particle_loads(state, loads, blocks)
    scatter_rows(
        state,
        loads,
        sums,
        (wide, tall),
        grid_place(anchor_down, anchor_cross, step),
        blocks,
        GROUP,
    )
    write_grid(sums, grid, pay)


def gather_kernel(step, links, width, window_row, window_turn, slots, state, total, *rest):
    bands = rest[: links - 2]
    wide, tall, after = rest[links - 2 : links + 1]
    sent = rest[links + 1 : 2 * links + 1]
    speed, sums = rest[2 * links + 1 :]
    blocks = wide.shape[0]
    sums[...] = total[...]
    node_velocity(sums, bands, speed, width)
    gather_rows(
        state,
        speed,
        (wide, tall),
        lambda m: m,
        window_place(window_row, window_turn, step),
        blocks,
        min(GROUP, blocks),
        after,
    )
    cap = slots.shape[2]
    for link in range(links):
        side = link_side(link)
        for m in range(cap):
            slot = pl.ds(slots[step, side, m], 1)
            for f in range(FIELDS):
                sent[link][f * cap + m : f * cap + m + 1, :] = after[f, slot, :]


def last_kernel(step, links, slots, counts, old, *rest):
    arrived = pick_arrived(rest[:links])
    out, state, sems = rest[links:]
    blocks = out.shape[1]
    state[:, :blocks, :] = old[:, :blocks, :]
    settle(state, arrived, slots, counts, step, blocks)
    copy = pltpu.make_async_copy(state.at[:, pl.ds(0, blocks), :], out, sems.at[0])
    copy.start()
    copy.wait()


def cross_kernel(width, grid, band0, band1, total, pay):
    tiles, rows, _ = grid.shape
    height = rows // CHANNELS
    odd = lax.rem(lax.axis_index("down"), 2)
    index = lax.axis_index("down")
    size = lax.axis_size("down")
    total[...] = grid[...]
    partner = index - 1 + 2 * odd
    there = (partner >= 0) & (partner < size)
    for t in range(tiles):
        for c in range(CHANNELS):
            spot = slice(c * BAND, (c + 1) * BAND)
            for link in range(2):
                if link == 0:
                    band = band0[t, spot, :]
                else:
                    band = jnp.where(there, band1[odd, t, spot, :], 0.0)
                at_first = odd if link == 0 else 1 - odd
                start = c * height + (1 - at_first) * (height - BAND)
                place = pl.ds(pl.multiple_of(start, 8), BAND)
                total[t, place, :] = total[t, place, :] + band
    odd = lax.rem(lax.axis_index("cross"), 2)
    tile, lane = divmod(width - BAND, LANES)
    last = pltpu.roll(total[tile], LANES - lane, 1) if lane else total[tile]
    pad = jnp.zeros((LANES - rows, LANES), jnp.float32)
    pay[odd] = jnp.transpose(jnp.concatenate([last, pad], axis=0))[:BAND]
    pay[1 - odd] = jnp.transpose(jnp.concatenate([total[0], pad], axis=0))[:BAND]


def add_across(total, bands, sums, width):
    tiles, rows, _ = total.shape
    sums[...] = total[...]
    odd = lax.rem(lax.axis_index("cross"), 2)
    tile, lane = divmod(width - BAND, LANES)
    pad = jnp.zeros((LANES - BAND, LANES), jnp.float32)
    for link, came in enumerate(bands):
        band = jnp.transpose(jnp.concatenate([came[...], pad], axis=0))[:rows]
        at_first = odd if link == 0 else 1 - odd
        sums[0] = sums[0] + jnp.where(at_first == 1, band, 0.0)
        shifted = pltpu.roll(band, lane, 1) if lane else band
        sums[tile] = sums[tile] + jnp.where(at_first == 0, shifted, 0.0)


def node_velocity(total, speed, width):
    tiles, rows, _ = total.shape
    height = rows // CHANNELS
    tile_down = height - 2 * GHOST
    tile_cross = width - 2 * GHOST
    row_global = (
        lax.broadcasted_iota(jnp.int32, (height, LANES), 0)
        + lax.axis_index("down") * tile_down
        - GHOST
    )
    col_first = lax.broadcasted_iota(jnp.int32, (height, LANES), 1) - GHOST
    total_rows = tile_down * lax.axis_size("down")
    total_cols = tile_cross * lax.axis_size("cross")
    keep_rows = (row_global > 0) & (row_global < total_rows - 1)
    halves = speed.shape[0] // (2 * height)
    lane = lax.broadcasted_iota(jnp.int32, (2 * height, LANES), 1)
    before = None
    for t in range(tiles):
        col_global = col_first + (lax.axis_index("cross") * tile_cross + t * LANES)
        kept = keep_rows & (col_global > 0) & (col_global < total_cols - 1)
        factor = jnp.where(kept, 1.0 / jnp.maximum(total[t, :height, :], MASS_FLOOR), 0.0)
        value = total[t, height:, :] * jnp.concatenate([factor, factor], axis=0)
        turned = pltpu.roll(value, HALF, 1)
        if 2 * t < halves:
            speed[4 * t * height : (4 * t + 2) * height, :] = value
        if t and 2 * t - 1 < halves:
            speed[(4 * t - 2) * height : 4 * t * height, :] = jnp.where(lane < HALF, before, turned)
        before = turned


def row_sums(terms, row):
    half = row < 4
    four = [
        jnp.where(half, terms[k], terms[k + 4])
        + pltpu.roll(jnp.where(half, terms[k + 4], terms[k]), 4, 0)
        for k in range(4)
    ]
    pair = (row & 2) == 0
    two = [
        jnp.where(
            pair, four[k] + pltpu.roll(four[k], 6, 0), four[k + 2] + pltpu.roll(four[k + 2], 2, 0)
        )
        for k in range(2)
    ]
    return jnp.where(
        (row & 1) == 0, two[0] + pltpu.roll(two[0], 7, 0), two[1] + pltpu.roll(two[1], 1, 0)
    )


def gather_terms(weights, speed, slot, window_row, window_turn, lane):
    height = TILE_DOWN + 2 * GHOST
    window = jnp.concatenate(
        [speed[pl.ds(window_row, WIN_DOWN), :], speed[pl.ds(window_row + height, WIN_DOWN), :]],
        axis=0,
    )
    window = pltpu.roll(window, window_turn, 1)
    window = jnp.where(lane < WIN_CROSS, window, pltpu.roll(window, WIN_CROSS, 1))
    window = jnp.concatenate([window, low_part(window)], axis=0).astype(jnp.bfloat16)
    found = jnp.dot(
        window[:, : 2 * WIN_CROSS], weights[0][slot], preferred_element_type=jnp.float32
    )
    found = found[: 2 * WIN_DOWN] + found[2 * WIN_DOWN :]
    value, slope = weights[1][slot, :WIN_DOWN, :], weights[1][slot, WIN_DOWN:, :]
    along_d, along_c = found[:WIN_DOWN, :LANES], found[WIN_DOWN:, :LANES]
    across_d, across_c = found[:WIN_DOWN, LANES:], found[WIN_DOWN:, LANES:]
    return (
        value * along_d,
        value * along_c,
        slope * along_d,
        slope * along_c,
        value * across_d,
        value * across_c,
    )


def gather_eight(weights, speed, slots, place, field, lane, row):
    terms = [gather_terms(weights, speed, slot, *place(slot), lane) for slot in slots]
    vel_d, vel_c, l_dd, l_cd, l_dc, l_cc = (row_sums(t, row) for t in zip(*terms))
    vel_d, vel_c = 0.25 * vel_d, 0.25 * vel_c
    l_dd, l_cc = 0.5 * l_dd, 0.5 * l_cc
    rate_dc = 0.25 * (l_dc + l_cd)
    trace = l_dd + l_cc
    shear = (2.0 * TIME_STEP) * field[9]
    spread = (TIME_STEP * field[10]) * trace
    stretch = TIME_STEP * trace
    return {
        0: jnp.clip(field[0] + TIME_STEP * vel_d, 0.5, WIN_DOWN - 1.5),
        1: jnp.clip(field[1] + TIME_STEP * vel_c, 0.5, WIN_CROSS - 1.5),
        2: vel_d,
        3: vel_c,
        4: field[4] + (spread + shear * l_dd),
        5: field[5] + shear * rate_dc,
        6: field[6] + (spread + shear * l_cc),
        8: field[8] + field[8] * stretch,
        11: field[11] + TIME_STEP * (l_dd * l_dd + l_cc * l_cc + 2.0 * rate_dc * rate_dc),
    }


def gather_lanes():
    lane = lax.broadcasted_iota(jnp.int32, (2 * WIN_DOWN, LANES), 1)
    row = lax.broadcasted_iota(jnp.int32, (ROWS, LANES), 0)
    return lane, row


def inner_kernel(
    step,
    links,
    width,
    anchor_down,
    anchor_cross,
    slots,
    state,
    total,
    wide,
    tall,
    after,
    edge,
    rank,
    *rest,
):
    sent, speed = rest[:-1], rest[-1]
    blocks = wide.shape[0]
    node_velocity(total, speed, width)
    place = speed_place(anchor_down, anchor_cross, step)
    lane, row = gather_lanes()
    low, high = edge_limits(width)

    def several(q, listed):
        for base in range(0, GROUP, ROWS):
            slots = [q * GROUP + base + k for k in range(ROWS)]
            start = base if isinstance(q, int) else pl.multiple_of(slots[0], ROWS)
            spot = pl.ds(start, ROWS)
            field = [state[f, spot, :] for f in range(FIELDS)]
            result = gather_eight((wide, tall), speed, slots, place, field, lane, row)
            for f in range(FIELDS):
                after[f, spot, :] = result.get(f, field[f])
            for slot in slots:
                edge[listed] = slot
                col = anchor_cross[step, slot] + GHOST
                listed = listed + ((col < low) | (col > high)).astype(jnp.int32)
        return listed

    steps = blocks // GROUP
    edge[blocks] = several(0, 0) if steps == 1 else lax.fori_loop(0, steps, several, 0)
    cap = slots.shape[2]
    plane = sent[0].shape[0]
    for b in range(blocks):
        rank[b] = links * plane
    for link in range(links):
        side = link_side(link)
        for m in range(cap):
            slot = slots[step, side, m]
            rank[slot] = link * plane + m
            for f in range(FIELDS):
                start = f * cap + m
                sent[link][start : start + 1, :] = after[f, pl.ds(slot, 1), :]


def edge_kernel(step, links, width, cap, anchor_down, anchor_cross, edge, rank, state, total, *rest):
    bands = rest[: links - 2]
    wide, tall, before = rest[links - 2 : links + 1]
    picked_before, after = rest[links + 1 : 2 * links + 1], rest[2 * links + 1]
    sent = rest[2 * links + 2 : 3 * links + 2]
    speed, sums, rows, mail = rest[3 * links + 2 :]
    plane = picked_before[0].shape[0]
    blocks = wide.shape[0]
    after[:, :blocks, :] = before[:, :blocks, :]
    for link, given in enumerate(picked_before):
        mail[link * plane : (link + 1) * plane, :] = given[...]
    add_across(total, bands, sums, width)
    node_velocity(sums, speed, width)
    place = speed_place(anchor_down, anchor_cross, step)
    lane, row = gather_lanes()
    count = edge[blocks]
    used = [f for f in range(FIELDS) if f not in (2, 3, 7)]

    def eight(q, carry):
        picked = [edge[jnp.minimum(q * ROWS + k, count - 1)] for k in range(ROWS)]
        for k, slot in enumerate(picked):
            for f in used:
                rows[f, k : k + 1, :] = state[f, pl.ds(slot, 1), :]
        field = {f: rows[f] for f in used}
        result = gather_eight((wide, tall), speed, picked, place, field, lane, row)
        for f, value in result.items():
            rows[f] = value
        for k, slot in enumerate(picked):
            start = rank[slot]
            for f in result:
                value = rows[f, k : k + 1, :]
                after[f, pl.ds(slot, 1), :] = value
                mail[pl.ds(start + f * cap, 1), :] = value
        return carry

    lax.fori_loop(0, (count + ROWS - 1) // ROWS, eight, 0)
    for link, out in enumerate(sent):
        out[...] = mail[link * plane : (link + 1) * plane, :]


def swap_pairs(size, first):
    pairs = []
    for i in range(first, size - 1, 2):
        pairs += [(i, i + 1), (i + 1, i)]
    return pairs


def odd_groups(size_down, size_cross):
    groups = []
    for i in (0, size_down - 1):
        groups += [[i * size_cross + j, i * size_cross + j + 1] for j in range(0, size_cross, 2)]
    for i in range(1, size_down - 1, 2):
        groups += [[i * size_cross + j, (i + 1) * size_cross + j] for j in range(size_cross)]
    return groups


def solution(mesh):
    size_down, size_cross = mesh.shape["down"], mesh.shape["cross"]
    links = 3 if size_cross <= 2 else 4
    smem = pl.BlockSpec(memory_space=pltpu.SMEM)
    vmem = pl.BlockSpec(memory_space=pltpu.VMEM)
    hbm = pl.BlockSpec(memory_space=pltpu.HBM)
    f32 = jnp.float32

    def swap(x, link):
        axis, second = divmod(link, 2)
        name, size = (("down", size_down), ("cross", size_cross))[axis]
        return lax.ppermute(x, name, swap_pairs(size, second))

    def gather_pairs(x):
        return lax.all_gather(
            x, ("down", "cross"), axis_index_groups=odd_groups(size_down, size_cross)
        )

    def call(name, kernel, outs, in_specs, scratch=(), flops=0):
        return pl.pallas_call(
            kernel,
            out_shape=outs,
            in_specs=in_specs,
            out_specs=tuple(pl.BlockSpec(memory_space=x.memory_space) if isinstance(x, pl.MemoryRef) else vmem for x in outs),
            scratch_shapes=scratch,
            compiler_params=pltpu.CompilerParams(vmem_limit_bytes=VMEM_BYTES),
            cost_estimate=pl.CostEstimate(flops=flops, bytes_accessed=1 << 20, transcendentals=0),
            name=name,
        )

    def on_device(particles, anchor_down, anchor_cross, move_count, move_slots):
        blocks = particles.shape[0]
        cap = move_slots.shape[2]
        height = TILE_DOWN + 2 * GHOST
        width = TILE_CROSS + 2 * GHOST
        tiles = -(-width // LANES)
        halves = (width - WIN_CROSS) // HALF + 1

        def array(*shape, dtype=f32):
            return jax.ShapeDtypeStruct(shape, dtype)

        grid_type = array(tiles, CHANNELS * height, LANES)
        band_type = array(2, tiles, CHANNELS * BAND, LANES)
        state_type = array(FIELDS, blocks + ROWS, LANES)
        plane = -(-FIELDS * cap // 8) * 8
        sent_type = array(plane, LANES)
        weight_types = (
            array(blocks, 2 * WIN_CROSS, 2 * LANES, dtype=jnp.bfloat16),
            array(blocks, 2 * WIN_DOWN, LANES),
        )
        scatter_scratch = [
            pltpu.VMEM((tiles * LANES, LANES), f32),
            pltpu.VMEM((LOADS, blocks, LANES), f32),
        ]
        ints = (
            anchor_down,
            anchor_cross,
            move_slots.reshape(STEPS, 4, cap),
            move_count.reshape(STEPS, 4),
        )
        given = ints + (jnp.transpose(particles, (1, 0, 2)),)
        edge_type = pltpu.SMEM((blocks + 1,), jnp.int32)
        speed_scratch = pltpu.VMEM((halves * 2 * height, LANES), f32)
        state, grid, pay, *rest = call(
            "scatter_first",
            functools.partial(first_kernel, 0),
            (state_type, grid_type, band_type)
            + weight_types
            + tuple(pltpu.SMEM(x.shape, x.dtype) for x in ints),
            [hbm] * 5,
            scatter_scratch
            + [
                pltpu.SemaphoreType.DMA((5,)),
            ],
        )(*(pltpu.with_memory_space_constraint(x, pltpu.HBM) for x in given))
        weights = rest[:2]
        rest = [pltpu.with_memory_space_constraint(x, pltpu.SMEM) for x in rest[2:]]
        anchors, moves = rest[:2], rest[2:]
        for step in range(STEPS):
            if step:
                state, grid, pay, *weights = call(
                    "scatter_next",
                    functools.partial(next_kernel, step, links),
                    (state_type, grid_type, band_type) + weight_types,
                    [smem] * 4 + [vmem] * (links + 1),
                    scatter_scratch,
                )(*anchors, *moves, state, *arrived)
            band0 = swap(pay[0], 0)
            band1 = gather_pairs(pay[1])
            total, pay = call(
                "add_down",
                functools.partial(cross_kernel, width),
                (grid_type, array(2, BAND, LANES)),
                [vmem] * 3,
            )(grid, band0, band1)
            bands = [swap(pay[k], 2 + k) for k in range(links - 2)]
            ahead, edge, rank, *picked = call(
                "gather_inner",
                functools.partial(inner_kernel, step, links, width),
                (state_type, edge_type, edge_type) + (sent_type,) * links,
                [smem] * 3 + [vmem] * 4,
                [speed_scratch],
                1 << 32,
            )(*anchors, moves[0], state, total, *weights)
            edge, rank = (pltpu.with_memory_space_constraint(x, pltpu.SMEM) for x in (edge, rank))
            state, *sent = call(
                "gather_edge",
                functools.partial(edge_kernel, step, links, width, cap),
                (state_type,) + (sent_type,) * links,
                [smem] * 4 + [vmem] * (3 + 2 * links),
                [
                    speed_scratch,
                    pltpu.VMEM(grid_type.shape, f32),
                    pltpu.VMEM((FIELDS, ROWS, LANES), f32),
                    pltpu.VMEM(((links + 1) * plane, LANES), f32),
                ],
            )(*anchors, edge, rank, state, total, *bands, *weights, ahead, *picked)
            arrived = [
                gather_pairs(x) if link == 1 else swap(x, link) for link, x in enumerate(sent)
            ]
        (state,) = call(
            "settle_last",
            functools.partial(last_kernel, STEPS - 1, links),
            (pltpu.HBM((FIELDS, blocks, LANES), f32),),
            [smem] * 2 + [vmem] * (links + 1),
            [pltpu.VMEM(state_type.shape, f32), pltpu.SemaphoreType.DMA((1,))],
        )(*moves, state, *arrived)
        return jnp.transpose(state, (1, 0, 2))

    return jax.shard_map(
        on_device,
        mesh=mesh,
        in_specs=(
            P(("down", "cross"), None, None),
            P(None, ("down", "cross")),
            P(None, ("down", "cross")),
            P(None, None, "down", "cross"),
            P(None, None, None, "down", "cross"),
        ),
        out_specs=P(("down", "cross"), None, None),
        check_vma=False,
    )
```

```python
import functools

import jax
import jax.numpy as jnp
from jax import lax
from jax.experimental import pallas as pl
from jax.experimental.pallas import tpu as pltpu
from jax.sharding import PartitionSpec as P

WIN_DOWN = 8
WIN_CROSS = 16
GHOST = 4
STEPS = 2
TILE_DOWN = 16
TILE_CROSS = 256
TIME_STEP = 0.1
GRAVITY = 5.6
MASS_FLOOR = 0.5
FIELDS = 12
LANES = 128
HALF_BITS = 6
HALF = 1 << HALF_BITS
ROWS = 8
CHANNELS = 3
STRIDE = 32
BAND = 2 * GHOST
LOADS = 6
GROUP = 128
VMEM_BYTES = 32 * 1024 * 1024


def spline_pair(distance):
    reach = jnp.clip(distance, -1.5, 1.5)
    near = jnp.clip(3.0 * distance, -1.5, 1.5)
    slope = reach - near
    return (slope * slope + 1.5) - (2.0 / 3.0) * (near * near), slope


def low_part(x):
    return x - x.astype(jnp.bfloat16).astype(jnp.float32)


def node_rows(count):
    return lax.broadcasted_iota(jnp.int32, (count, LANES), 0).astype(jnp.float32)


def cross_weights(w, cols):
    value, slope = spline_pair(w - cols)
    both = jnp.concatenate([value, slope], axis=1)
    high = both.astype(jnp.bfloat16)
    low = (both - high.astype(jnp.float32)).astype(jnp.bfloat16)
    return jnp.concatenate([high, low], axis=0)


def particle_loads(state, loads, blocks, keep=None):
    for base in range(0, blocks, ROWS):
        spot = pl.ds(base, ROWS)
        vd, vc, sdd, sdc, scc, mass, vol = (state[f, spot, :] for f in range(2, 9))
        quarter = 0.25 * mass
        push = (-0.5 * TIME_STEP) * vol
        terms = (
            quarter,
            quarter * (vd + TIME_STEP * GRAVITY),
            quarter * vc,
            push * sdd,
            push * sdc,
            push * scc,
        )
        for k, term in enumerate(terms):
            loads[k, spot, :] = term if keep is None else term * keep[spot, :]


def scatter_block(u, w, load, sums, weights, slot, first_row, first_col, rows, cols, inside):
    value, slope = spline_pair(u - rows)
    across_weights = cross_weights(w, cols)
    if weights is not None:
        weights[0][slot] = across_weights
        weights[1][slot, :WIN_DOWN, :] = value
        weights[1][slot, WIN_DOWN:, :] = slope
    load_dc = load(4)
    parts = (
        (load(0) * value,),
        (load(1) * value + load(3) * slope, load_dc * value),
        (load(2) * value + load_dc * slope, load(5) * value),
    )
    gap = jnp.zeros((16, 2 * LANES), jnp.bfloat16)
    none = jnp.zeros((16, LANES), jnp.bfloat16)
    pieces = []
    for part in parts:
        halves = [jnp.concatenate([x, low_part(x)], axis=0).astype(jnp.bfloat16) for x in part]
        pieces += [jnp.concatenate((halves + [none])[:2], axis=1), gap]
    found = lax.dot_general(
        across_weights,
        jnp.concatenate(pieces, axis=0),
        (((1,), (1,)), ((), ())),
        preferred_element_type=jnp.float32,
    )
    found = found[:WIN_CROSS] + found[WIN_CROSS:]
    found = jnp.concatenate(
        [found, jnp.zeros((WIN_CROSS, LANES - CHANNELS * STRIDE), jnp.float32)], axis=1
    )
    found = jnp.where(inside, found + pltpu.roll(found, LANES - WIN_DOWN, 1), 0.0)
    found = pltpu.roll(found, first_row, 1)
    spot = pl.ds(first_col, WIN_CROSS)
    sums[spot, :] = sums[spot, :] + found


def edge_limits(width):
    index = lax.axis_index("cross")
    low = jnp.where(index > 0, BAND, 0)
    high = jnp.where(index < lax.axis_size("cross") - 1, width - BAND - WIN_CROSS, width)
    return low, high


def scatter_rows(state, loads, sums, weights, place, blocks, group):
    rows = node_rows(WIN_DOWN)
    cols = node_rows(WIN_CROSS)
    lane = lax.broadcasted_iota(jnp.int32, (WIN_CROSS, LANES), 1)
    inside = (lane & (STRIDE - 1)) < WIN_DOWN

    def several(q, carry):
        for k in range(group):
            m = q * group + k
            row = pl.ds(m, 1)
            first_row, first_col = place(m)
            scatter_block(
                state[0, row, :],
                state[1, row, :],
                lambda f, row=row: loads[f, row, :],
                sums,
                weights,
                m,
                first_row,
                first_col,
                rows,
                cols,
                inside,
            )
        return carry

    steps = blocks // group
    if steps == 1:
        several(0, 0)
    else:
        lax.fori_loop(0, steps, several, 0)


def grid_place(anchor_down, anchor_cross, step):
    return lambda b: (anchor_down[step, b] + GHOST, anchor_cross[step, b] + GHOST)


def speed_place(anchor_down, anchor_cross, step):
    def place(b):
        col = anchor_cross[step, b] + GHOST
        row = (col >> HALF_BITS) * (2 * (TILE_DOWN + 2 * GHOST)) + anchor_down[step, b] + GHOST
        return row, (LANES - (col & (HALF - 1))) & (LANES - 1)

    return place


def write_grid(sums, grid, pay):
    tiles, rows, _ = grid.shape
    height = rows // CHANNELS
    odd = lax.rem(lax.axis_index("down"), 2)
    ends = [0.0, 0.0]
    for t in range(tiles):
        turned = jnp.transpose(sums[t * LANES : (t + 1) * LANES, :])
        for c in range(CHANNELS):
            part = turned[c * STRIDE : c * STRIDE + height]
            grid[t, c * height : (c + 1) * height, :] = part
            last, first = part[height - BAND :], part[:BAND]
            if t < tiles - 1:
                spot = slice((t * CHANNELS + c) * BAND, (t * CHANNELS + c + 1) * BAND)
                pay[odd, spot, :] = last
                pay[1 - odd, spot, :] = first
            else:
                moved = [pltpu.roll(x, c * BAND, 1) if c else x for x in (last, first)]
                ends = [end + x for end, x in zip(ends, moved)]
    spot = slice((tiles - 1) * CHANNELS * BAND, pay.shape[1])
    pay[odd, spot, :] = ends[0]
    pay[1 - odd, spot, :] = ends[1]


def band_part(band, t, c, tiles):
    if t < tiles - 1:
        return band[(t * CHANNELS + c) * BAND : (t * CHANNELS + c + 1) * BAND, :]
    end = band[(tiles - 1) * CHANNELS * BAND :, :]
    lane = lax.broadcasted_iota(jnp.int32, (BAND, LANES), 1)
    return jnp.where(lane < BAND, pltpu.roll(end, LANES - c * BAND, 1) if c else end, 0.0)


def first_kernel(
    step,
    down_in,
    cross_in,
    slots_in,
    counts_in,
    particles,
    state,
    grid,
    pay,
    wide,
    tall,
    anchor_down,
    anchor_cross,
    slots,
    counts,
    sums,
    loads,
    sems,
):
    blocks = particles.shape[1]
    whole = pltpu.make_async_copy(particles, state.at[:, pl.ds(0, blocks), :], sems.at[0])
    ints = [
        pltpu.make_async_copy(src, dst, sems.at[1 + k])
        for k, (src, dst) in enumerate(
            (
                (down_in, anchor_down),
                (cross_in, anchor_cross),
                (slots_in, slots),
                (counts_in, counts),
            )
        )
    ]
    for copy in ints[:2] + [whole] + ints[2:]:
        copy.start()
    sums[...] = jnp.zeros_like(sums)
    for copy in ints[:2]:
        copy.wait()
    whole.wait()
    particle_loads(state, loads, blocks)
    place = grid_place(anchor_down, anchor_cross, step)
    scatter_rows(state, loads, sums, (wide, tall), place, blocks, GROUP)
    write_grid(sums, grid, pay)
    for copy in ints[2:]:
        copy.wait()


def link_side(link):
    axis, second = divmod(link, 2)
    odd = lax.rem(lax.axis_index(("down", "cross")[axis]), 2)
    return 2 * axis + (1 - odd if second else odd)


def settle(state, arrived, slots, counts, step, blocks):
    cap = slots.shape[2]
    for link, came in enumerate(arrived):
        side = link_side(link)
        count = counts[step, side]
        for m in range(cap):
            slot = pl.ds(jnp.where(m < count, slots[step, side, m], blocks), 1)
            for f in range(FIELDS):
                state[f, slot, :] = came[f * cap + m : f * cap + m + 1, :]


def pick_arrived(refs):
    odd = lax.rem(lax.axis_index("down"), 2)
    return [ref.at[odd] if link == 1 else ref for link, ref in enumerate(refs)]


def next_kernel(step, links, anchor_down, anchor_cross, slots, counts, old, *rest):
    arrived = pick_arrived(rest[:links])
    state, grid, pay, wide, tall, sums, loads = rest[links:]
    blocks = loads.shape[1]
    state[:, :blocks, :] = old[:, :blocks, :]
    settle(state, arrived, slots, counts, step - 1, blocks)
    sums[...] = jnp.zeros_like(sums)
    particle_loads(state, loads, blocks)
    scatter_rows(
        state,
        loads,
        sums,
        (wide, tall),
        grid_place(anchor_down, anchor_cross, step),
        blocks,
        GROUP,
    )
    write_grid(sums, grid, pay)


def gather_kernel(step, links, width, window_row, window_turn, slots, state, total, *rest):
    bands = rest[: links - 2]
    wide, tall, after = rest[links - 2 : links + 1]
    sent = rest[links + 1 : 2 * links + 1]
    speed, sums = rest[2 * links + 1 :]
    blocks = wide.shape[0]
    sums[...] = total[...]
    node_velocity(sums, bands, speed, width)
    gather_rows(
        state,
        speed,
        (wide, tall),
        lambda m: m,
        window_place(window_row, window_turn, step),
        blocks,
        min(GROUP, blocks),
        after,
    )
    cap = slots.shape[2]
    for link in range(links):
        side = link_side(link)
        for m in range(cap):
            slot = pl.ds(slots[step, side, m], 1)
            for f in range(FIELDS):
                sent[link][f * cap + m : f * cap + m + 1, :] = after[f, slot, :]


def last_kernel(step, links, slots, counts, old, *rest):
    arrived = pick_arrived(rest[:links])
    out, state, sems = rest[links:]
    blocks = out.shape[1]
    state[:, :blocks, :] = old[:, :blocks, :]
    settle(state, arrived, slots, counts, step, blocks)
    copy = pltpu.make_async_copy(state.at[:, pl.ds(0, blocks), :], out, sems.at[0])
    copy.start()
    copy.wait()


def cross_kernel(width, grid, band0, band1, total, pay):
    tiles, rows, _ = grid.shape
    height = rows // CHANNELS
    odd = lax.rem(lax.axis_index("down"), 2)
    index = lax.axis_index("down")
    size = lax.axis_size("down")
    total[...] = grid[...]
    partner = index - 1 + 2 * odd
    there = (partner >= 0) & (partner < size)
    for t in range(tiles):
        for c in range(CHANNELS):
            for link in range(2):
                if link == 0:
                    band = band_part(band0, t, c, tiles)
                else:
                    band = jnp.where(there, band_part(band1.at[odd], t, c, tiles), 0.0)
                at_first = odd if link == 0 else 1 - odd
                start = c * height + (1 - at_first) * (height - BAND)
                place = pl.ds(pl.multiple_of(start, 8), BAND)
                total[t, place, :] = total[t, place, :] + band
    odd = lax.rem(lax.axis_index("cross"), 2)
    tile, lane = divmod(width - BAND, LANES)
    last = pltpu.roll(total[tile], LANES - lane, 1) if lane else total[tile]
    pad = jnp.zeros((LANES - rows, LANES), jnp.float32)
    pay[odd] = jnp.transpose(jnp.concatenate([last, pad], axis=0))[:BAND]
    pay[1 - odd] = jnp.transpose(jnp.concatenate([total[0], pad], axis=0))[:BAND]


def add_across(total, bands, sums, width):
    tiles, rows, _ = total.shape
    sums[...] = total[...]
    odd = lax.rem(lax.axis_index("cross"), 2)
    tile, lane = divmod(width - BAND, LANES)
    pad = jnp.zeros((LANES - BAND, LANES), jnp.float32)
    for link, came in enumerate(bands):
        band = jnp.transpose(jnp.concatenate([came[...], pad], axis=0))[:rows]
        at_first = odd if link == 0 else 1 - odd
        sums[0] = sums[0] + jnp.where(at_first == 1, band, 0.0)
        shifted = pltpu.roll(band, lane, 1) if lane else band
        sums[tile] = sums[tile] + jnp.where(at_first == 0, shifted, 0.0)


def node_velocity(total, speed, width):
    tiles, rows, _ = total.shape
    height = rows // CHANNELS
    tile_down = height - 2 * GHOST
    tile_cross = width - 2 * GHOST
    row_global = (
        lax.broadcasted_iota(jnp.int32, (height, LANES), 0)
        + lax.axis_index("down") * tile_down
        - GHOST
    )
    col_first = lax.broadcasted_iota(jnp.int32, (height, LANES), 1) - GHOST
    total_rows = tile_down * lax.axis_size("down")
    total_cols = tile_cross * lax.axis_size("cross")
    keep_rows = (row_global > 0) & (row_global < total_rows - 1)
    halves = speed.shape[0] // (2 * height)
    lane = lax.broadcasted_iota(jnp.int32, (2 * height, LANES), 1)
    before = None
    for t in range(tiles):
        col_global = col_first + (lax.axis_index("cross") * tile_cross + t * LANES)
        kept = keep_rows & (col_global > 0) & (col_global < total_cols - 1)
        factor = jnp.where(kept, 1.0 / jnp.maximum(total[t, :height, :], MASS_FLOOR), 0.0)
        value = total[t, height:, :] * jnp.concatenate([factor, factor], axis=0)
        turned = pltpu.roll(value, HALF, 1)
        if 2 * t < halves:
            speed[4 * t * height : (4 * t + 2) * height, :] = value
        if t and 2 * t - 1 < halves:
            speed[(4 * t - 2) * height : 4 * t * height, :] = jnp.where(lane < HALF, before, turned)
        before = turned


def row_sums(terms, row):
    half = row < 4
    four = [
        jnp.where(half, terms[k], terms[k + 4])
        + pltpu.roll(jnp.where(half, terms[k + 4], terms[k]), 4, 0)
        for k in range(4)
    ]
    pair = (row & 2) == 0
    two = [
        jnp.where(
            pair, four[k] + pltpu.roll(four[k], 6, 0), four[k + 2] + pltpu.roll(four[k + 2], 2, 0)
        )
        for k in range(2)
    ]
    return jnp.where(
        (row & 1) == 0, two[0] + pltpu.roll(two[0], 7, 0), two[1] + pltpu.roll(two[1], 1, 0)
    )


def gather_terms(weights, speed, slot, window_row, window_turn, lane):
    height = TILE_DOWN + 2 * GHOST
    window = jnp.concatenate(
        [speed[pl.ds(window_row, WIN_DOWN), :], speed[pl.ds(window_row + height, WIN_DOWN), :]],
        axis=0,
    )
    window = pltpu.roll(window, window_turn, 1)
    window = jnp.where(lane < WIN_CROSS, window, pltpu.roll(window, WIN_CROSS, 1))
    window = jnp.concatenate([window, low_part(window)], axis=0).astype(jnp.bfloat16)
    found = jnp.dot(
        window[:, : 2 * WIN_CROSS], weights[0][slot], preferred_element_type=jnp.float32
    )
    found = found[: 2 * WIN_DOWN] + found[2 * WIN_DOWN :]
    value, slope = weights[1][slot, :WIN_DOWN, :], weights[1][slot, WIN_DOWN:, :]
    along_d, along_c = found[:WIN_DOWN, :LANES], found[WIN_DOWN:, :LANES]
    across_d, across_c = found[:WIN_DOWN, LANES:], found[WIN_DOWN:, LANES:]
    return (
        value * along_d,
        value * along_c,
        slope * along_d,
        slope * along_c,
        value * across_d,
        value * across_c,
    )


def gather_eight(weights, speed, slots, place, field, lane, row):
    terms = [gather_terms(weights, speed, slot, *place(slot), lane) for slot in slots]
    vel_d, vel_c, l_dd, l_cd, l_dc, l_cc = (row_sums(t, row) for t in zip(*terms))
    vel_d, vel_c = 0.25 * vel_d, 0.25 * vel_c
    l_dd, l_cc = 0.5 * l_dd, 0.5 * l_cc
    rate_dc = 0.25 * (l_dc + l_cd)
    trace = l_dd + l_cc
    shear = (2.0 * TIME_STEP) * field[9]
    spread = (TIME_STEP * field[10]) * trace
    stretch = TIME_STEP * trace
    return {
        0: jnp.clip(field[0] + TIME_STEP * vel_d, 0.5, WIN_DOWN - 1.5),
        1: jnp.clip(field[1] + TIME_STEP * vel_c, 0.5, WIN_CROSS - 1.5),
        2: vel_d,
        3: vel_c,
        4: field[4] + (spread + shear * l_dd),
        5: field[5] + shear * rate_dc,
        6: field[6] + (spread + shear * l_cc),
        8: field[8] + field[8] * stretch,
        11: field[11] + TIME_STEP * (l_dd * l_dd + l_cc * l_cc + 2.0 * rate_dc * rate_dc),
    }


def gather_lanes():
    lane = lax.broadcasted_iota(jnp.int32, (2 * WIN_DOWN, LANES), 1)
    row = lax.broadcasted_iota(jnp.int32, (ROWS, LANES), 0)
    return lane, row


def inner_kernel(
    step,
    links,
    width,
    anchor_down,
    anchor_cross,
    slots,
    state,
    total,
    wide,
    tall,
    after,
    edge,
    rank,
    *rest,
):
    sent, speed = rest[:-1], rest[-1]
    blocks = wide.shape[0]
    node_velocity(total, speed, width)
    place = speed_place(anchor_down, anchor_cross, step)
    lane, row = gather_lanes()
    low, high = edge_limits(width)

    def several(q, listed):
        for base in range(0, GROUP, ROWS):
            slots = [q * GROUP + base + k for k in range(ROWS)]
            start = base if isinstance(q, int) else pl.multiple_of(slots[0], ROWS)
            spot = pl.ds(start, ROWS)
            field = [state[f, spot, :] for f in range(FIELDS)]
            result = gather_eight((wide, tall), speed, slots, place, field, lane, row)
            for f in range(FIELDS):
                after[f, spot, :] = result.get(f, field[f])
            for slot in slots:
                edge[listed] = slot
                col = anchor_cross[step, slot] + GHOST
                listed = listed + ((col < low) | (col > high)).astype(jnp.int32)
        return listed

    steps = blocks // GROUP
    edge[blocks] = several(0, 0) if steps == 1 else lax.fori_loop(0, steps, several, 0)
    cap = slots.shape[2]
    plane = sent[0].shape[0]
    for b in range(blocks):
        rank[b] = links * plane
    for link in range(links):
        side = link_side(link)
        for m in range(cap):
            slot = slots[step, side, m]
            rank[slot] = link * plane + m
            for f in range(FIELDS):
                start = f * cap + m
                sent[link][start : start + 1, :] = after[f, pl.ds(slot, 1), :]


def edge_kernel(step, links, width, cap, anchor_down, anchor_cross, edge, rank, state, total, *rest):
    bands = rest[: links - 2]
    wide, tall, before = rest[links - 2 : links + 1]
    picked_before, after = rest[links + 1 : 2 * links + 1], rest[2 * links + 1]
    sent = rest[2 * links + 2 : 3 * links + 2]
    speed, sums, rows, mail = rest[3 * links + 2 :]
    plane = picked_before[0].shape[0]
    blocks = wide.shape[0]
    after[:, :blocks, :] = before[:, :blocks, :]
    for link, given in enumerate(picked_before):
        mail[link * plane : (link + 1) * plane, :] = given[...]
    add_across(total, bands, sums, width)
    node_velocity(sums, speed, width)
    place = speed_place(anchor_down, anchor_cross, step)
    lane, row = gather_lanes()
    count = edge[blocks]
    used = [f for f in range(FIELDS) if f not in (2, 3, 7)]

    def eight(q, carry):
        picked = [edge[jnp.minimum(q * ROWS + k, count - 1)] for k in range(ROWS)]
        for k, slot in enumerate(picked):
            for f in used:
                rows[f, k : k + 1, :] = state[f, pl.ds(slot, 1), :]
        field = {f: rows[f] for f in used}
        result = gather_eight((wide, tall), speed, picked, place, field, lane, row)
        for f, value in result.items():
            rows[f] = value
        for k, slot in enumerate(picked):
            start = rank[slot]
            for f in result:
                value = rows[f, k : k + 1, :]
                after[f, pl.ds(slot, 1), :] = value
                mail[pl.ds(start + f * cap, 1), :] = value
        return carry

    lax.fori_loop(0, (count + ROWS - 1) // ROWS, eight, 0)
    for link, out in enumerate(sent):
        out[...] = mail[link * plane : (link + 1) * plane, :]


def swap_pairs(size, first):
    pairs = []
    for i in range(first, size - 1, 2):
        pairs += [(i, i + 1), (i + 1, i)]
    return pairs


def odd_groups(size_down, size_cross):
    groups = []
    for i in (0, size_down - 1):
        groups += [[i * size_cross + j, i * size_cross + j + 1] for j in range(0, size_cross, 2)]
    for i in range(1, size_down - 1, 2):
        groups += [[i * size_cross + j, (i + 1) * size_cross + j] for j in range(size_cross)]
    return groups


def solution(mesh):
    size_down, size_cross = mesh.shape["down"], mesh.shape["cross"]
    links = 3 if size_cross <= 2 else 4
    smem = pl.BlockSpec(memory_space=pltpu.SMEM)
    vmem = pl.BlockSpec(memory_space=pltpu.VMEM)
    hbm = pl.BlockSpec(memory_space=pltpu.HBM)
    f32 = jnp.float32

    def swap(x, link):
        axis, second = divmod(link, 2)
        name, size = (("down", size_down), ("cross", size_cross))[axis]
        return lax.ppermute(x, name, swap_pairs(size, second))

    def gather_pairs(x):
        return lax.all_gather(
            x, ("down", "cross"), axis_index_groups=odd_groups(size_down, size_cross)
        )

    def call(name, kernel, outs, in_specs, scratch=(), flops=0):
        return pl.pallas_call(
            kernel,
            out_shape=outs,
            in_specs=in_specs,
            out_specs=tuple(pl.BlockSpec(memory_space=x.memory_space) if isinstance(x, pl.MemoryRef) else vmem for x in outs),
            scratch_shapes=scratch,
            compiler_params=pltpu.CompilerParams(vmem_limit_bytes=VMEM_BYTES),
            cost_estimate=pl.CostEstimate(flops=flops, bytes_accessed=1 << 20, transcendentals=0),
            name=name,
        )

    def on_device(particles, anchor_down, anchor_cross, move_count, move_slots):
        blocks = particles.shape[0]
        cap = move_slots.shape[2]
        height = TILE_DOWN + 2 * GHOST
        width = TILE_CROSS + 2 * GHOST
        tiles = -(-width // LANES)
        halves = (width - WIN_CROSS) // HALF + 1

        def array(*shape, dtype=f32):
            return jax.ShapeDtypeStruct(shape, dtype)

        grid_type = array(tiles, CHANNELS * height, LANES)
        band_type = array(2, ((tiles - 1) * CHANNELS + 1) * BAND, LANES)
        state_type = array(FIELDS, blocks + ROWS, LANES)
        plane = -(-FIELDS * cap // 8) * 8
        sent_type = array(plane, LANES)
        weight_types = (
            array(blocks, 2 * WIN_CROSS, 2 * LANES, dtype=jnp.bfloat16),
            array(blocks, 2 * WIN_DOWN, LANES),
        )
        scatter_scratch = [
            pltpu.VMEM((tiles * LANES, LANES), f32),
            pltpu.VMEM((LOADS, blocks, LANES), f32),
        ]
        ints = (
            anchor_down,
            anchor_cross,
            move_slots.reshape(STEPS, 4, cap),
            move_count.reshape(STEPS, 4),
        )
        given = ints + (jnp.transpose(particles, (1, 0, 2)),)
        edge_type = pltpu.SMEM((blocks + 1,), jnp.int32)
        speed_scratch = pltpu.VMEM((halves * 2 * height, LANES), f32)
        state, grid, pay, *rest = call(
            "scatter_first",
            functools.partial(first_kernel, 0),
            (state_type, grid_type, band_type)
            + weight_types
            + tuple(pltpu.SMEM(x.shape, x.dtype) for x in ints),
            [hbm] * 5,
            scatter_scratch
            + [
                pltpu.SemaphoreType.DMA((5,)),
            ],
        )(*(pltpu.with_memory_space_constraint(x, pltpu.HBM) for x in given))
        weights = rest[:2]
        rest = [pltpu.with_memory_space_constraint(x, pltpu.SMEM) for x in rest[2:]]
        anchors, moves = rest[:2], rest[2:]
        for step in range(STEPS):
            if step:
                state, grid, pay, *weights = call(
                    "scatter_next",
                    functools.partial(next_kernel, step, links),
                    (state_type, grid_type, band_type) + weight_types,
                    [smem] * 4 + [vmem] * (links + 1),
                    scatter_scratch,
                )(*anchors, *moves, state, *arrived)
            band0 = swap(pay[0], 0)
            band1 = gather_pairs(pay[1])
            total, pay = call(
                "add_down",
                functools.partial(cross_kernel, width),
                (grid_type, array(2, BAND, LANES)),
                [vmem] * 3,
            )(grid, band0, band1)
            bands = [swap(pay[k], 2 + k) for k in range(links - 2)]
            ahead, edge, rank, *picked = call(
                "gather_inner",
                functools.partial(inner_kernel, step, links, width),
                (state_type, edge_type, edge_type) + (sent_type,) * links,
                [smem] * 3 + [vmem] * 4,
                [speed_scratch],
                1 << 32,
            )(*anchors, moves[0], state, total, *weights)
            edge, rank = (pltpu.with_memory_space_constraint(x, pltpu.SMEM) for x in (edge, rank))
            state, *sent = call(
                "gather_edge",
                functools.partial(edge_kernel, step, links, width, cap),
                (state_type,) + (sent_type,) * links,
                [smem] * 4 + [vmem] * (3 + 2 * links),
                [
                    speed_scratch,
                    pltpu.VMEM(grid_type.shape, f32),
                    pltpu.VMEM((FIELDS, ROWS, LANES), f32),
                    pltpu.VMEM(((links + 1) * plane, LANES), f32),
                ],
            )(*anchors, edge, rank, state, total, *bands, *weights, ahead, *picked)
            arrived = [
                gather_pairs(x) if link == 1 else swap(x, link) for link, x in enumerate(sent)
            ]
        (state,) = call(
            "settle_last",
            functools.partial(last_kernel, STEPS - 1, links),
            (pltpu.HBM((FIELDS, blocks, LANES), f32),),
            [smem] * 2 + [vmem] * (links + 1),
            [pltpu.VMEM(state_type.shape, f32), pltpu.SemaphoreType.DMA((1,))],
        )(*moves, state, *arrived)
        return jnp.transpose(state, (1, 0, 2))

    return jax.shard_map(
        on_device,
        mesh=mesh,
        in_specs=(
            P(("down", "cross"), None, None),
            P(None, ("down", "cross")),
            P(None, ("down", "cross")),
            P(None, None, "down", "cross"),
            P(None, None, None, "down", "cross"),
        ),
        out_specs=P(("down", "cross"), None, None),
        check_vma=False,
    )
```
